128 devices in a mesh: dp: 2 (over x_hi), fsdp: 16 (over y, z), tensor: 4 (over x_lo, core).
Axes of the slice: x: 4 (x_hi: 2, x_lo: 2; x = x_hi * 2 + x_lo), y: 4, z: 4, core: 2. Of those that a mesh axis runs over, the one named last changes fastest.
Arguments:
- x_in: bfloat16 [32, 512, 4608], P(('dp', 'fsdp'), None, 'tensor'), may hold values from -6 to 6
- lengths: int32 [32], P(('dp', 'fsdp')), may hold values from 128 to 512, as said below
- adapter_ids: int32 [32], P(('dp', 'fsdp')), may hold values from 0 to 15
- attn_grad: bfloat16 [32, 512, 4096], P(('dp', 'fsdp'), None, 'tensor'), may hold values from -6 to 6
- w_query: bfloat16 [4608, 4096], P('fsdp', 'tensor'), may hold values from -0.09375 to 0.09375
- w_key: bfloat16 [4608, 2048], P('fsdp', 'tensor'), may hold values from -0.09375 to 0.09375
- w_value: bfloat16 [4608, 2048], P('fsdp', 'tensor'), may hold values from -0.09375 to 0.09375
- query_down: bfloat16 [16, 16, 4608], replicated, may hold values from -0.09375 to 0.09375
- query_up: bfloat16 [16, 16, 4096], P(None, None, 'tensor'), may hold values from -1.5 to 1.5
- value_down: bfloat16 [16, 16, 4608], replicated, may hold values from -0.09375 to 0.09375
- value_up: bfloat16 [16, 16, 2048], P(None, None, 'tensor'), may hold values from -1.5 to 1.5
Outputs:
- grad_input: bfloat16 [32, 512, 4608], P(('dp', 'fsdp'), None, 'tensor')
- grad_query_down: float32 [16, 16, 4608], P(None, None, 'tensor')
- grad_query_up: float32 [16, 16, 4096], P(None, None, 'tensor')
- grad_value_down: float32 [16, 16, 4608], P(None, None, 'tensor')
- grad_value_up: float32 [16, 16, 2048], P(None, None, 'tensor')
The draws below stay inside these ranges and needn't reach their ends.
Inputs may be any that keep to these rules, and one draw needn't show every extreme that they name: lengths[0] is 512.
All inputs are finite; a program needn't handle non-finite values.
Results may differ from the reference program's by a relative error of at most 0.012.
The reference program's roundings to bfloat16 on the way (of `probs_b`, `cot` and `dscore`) count: a program that leaves them out, or rounds other values in their place, can miss the bound.
Values may be sent and summed in bfloat16 or wider, within the bound.
A program may use at most 128 MiB of HBM per device.

```python
import math
import jax
import jax.numpy as jnp
from jax import lax

D = 4608
HEADS = 32
HD = 128
R = 16
ADAPTERS = 16
LENGTH = 512
SEQS = 32
QW = 4096
KW = 2048


def draw_lengths(key, part):
    key = jax.random.fold_in(key, 11)
    drawn = jax.random.randint(key, (SEQS,), LENGTH // 4, LENGTH + 1, dtype=jnp.int32)
    return drawn.at[0].set(LENGTH)


def set_ends(result, stream_key, low, largest):
    place = [jax.random.randint(jax.random.fold_in(stream_key, axis), (), 0, length) for axis, length in enumerate(result.shape)]
    main_axis = result.shape.index(max(result.shape))
    beside = place[:main_axis] + [(place[main_axis] + 1) % result.shape[main_axis]] + place[main_axis + 1:]
    return result.at[tuple(place)].set(low).at[tuple(beside)].set(largest)


def block_levels(rng, dims, pieces, smallest, top_value):
    def one(position, shards_of):
        steps = jax.random.uniform(jax.random.fold_in(jax.random.fold_in(rng, 6), position), (shards_of,), jnp.float32, smallest / len(pieces), top_value / len(pieces))
        return jnp.repeat(jnp.exp(steps), dims[position] // shards_of).reshape((-1,) + (1,) * (len(dims) - position - 1))

    factor_of = one(*pieces[0])
    for cut in pieces[1:]:
        factor_of = factor_of * one(*cut)
    return factor_of


def centred(rng, extent, scale, most, split=(), held_as=jnp.bfloat16):
    gain = block_levels(rng, extent, split, -0.22, 0.18) if split else 1.0
    array = jax.random.normal(rng, extent, jnp.float32) * scale * gain
    return jnp.minimum(jnp.maximum(array, -most), most).astype(held_as)


def setup_inputs(seed: int = 0) -> dict:
    key_list = jax.random.split(jax.random.key(seed), 12)
    x_in = centred(key_list[0], (SEQS, LENGTH, D), 1.0, 6.0, ((0, 32), (2, 4)))
    lengths = draw_lengths(jax.random.fold_in(key_list[11], 71), 0)
    adapter_ids = set_ends(jax.random.randint(key_list[2], (SEQS,), 0, ADAPTERS), jax.random.fold_in(key_list[2], 1), 0, ADAPTERS - 1).astype(jnp.int32)
    attn_grad = centred(key_list[3], (SEQS, LENGTH, QW), 1.0, 6.0, ((0, 32), (2, 4)))
    w_query = centred(key_list[4], (D, QW), D ** -0.5, 0.09375, ((0, 16), (1, 4)))
    w_key = centred(key_list[5], (D, KW), D ** -0.5, 0.09375, ((0, 16), (1, 4)))
    w_value = centred(key_list[6], (D, KW), D ** -0.5, 0.09375, ((0, 16), (1, 4)))
    query_down = centred(key_list[7], (ADAPTERS, R, D), D ** -0.5, 0.09375)
    query_up = centred(key_list[8], (ADAPTERS, R, QW), R ** -0.5, 1.5, ((2, 4),))
    value_down = centred(key_list[9], (ADAPTERS, R, D), D ** -0.5, 0.09375)
    value_up = centred(key_list[10], (ADAPTERS, R, KW), R ** -0.5, 1.5, ((2, 4),))
    return dict(x_in=x_in, lengths=lengths, adapter_ids=adapter_ids, attn_grad=attn_grad, w_query=w_query, w_key=w_key, w_value=w_value, query_down=query_down, query_up=query_up, value_down=value_down, value_up=value_up)


soft_cap = 50.0
adapter_scale = 2.0

def core_backward(input_rows, cotangent, length, down_q, query_up_weight, down_v, value_up_weight, query_adapter_rows, rows_k, value_adapter_rows):
    count = input_rows.shape[0]
    score_scale = 1.0 / math.sqrt(D // HEADS)
    low_rank_query = jnp.dot(input_rows, down_q.T, preferred_element_type=jnp.float32).astype(jnp.bfloat16)
    low_rank_value = jnp.dot(input_rows, down_v.T, preferred_element_type=jnp.float32).astype(jnp.bfloat16)
    query_rows = (jnp.dot(input_rows, query_adapter_rows, preferred_element_type=jnp.float32) + adapter_scale * jnp.dot(low_rank_query, query_up_weight, preferred_element_type=jnp.float32)).astype(jnp.bfloat16)
    keys = jnp.dot(input_rows, rows_k, preferred_element_type=jnp.float32).astype(jnp.bfloat16)
    value_rows = (jnp.dot(input_rows, value_adapter_rows, preferred_element_type=jnp.float32) + adapter_scale * jnp.dot(low_rank_value, value_up_weight, preferred_element_type=jnp.float32)).astype(jnp.bfloat16)
    kv_count = keys.shape[1] // HD
    group_size = query_rows.shape[1] // keys.shape[1]
    query_heads = query_rows.reshape(count, kv_count, group_size, HD).astype(jnp.float32)
    key_heads = keys.reshape(count, kv_count, HD).astype(jnp.float32)
    value_heads = value_rows.reshape(count, kv_count, HD).astype(jnp.float32)
    raw = jnp.einsum('ikgh,jkh->kgij', query_heads, key_heads) * score_scale
    capped = soft_cap * jnp.tanh(raw / soft_cap)
    positions = jnp.arange(count, dtype=jnp.int32)
    allowed = (positions[None, :] <= positions[:, None]) & (positions[None, :] < length)
    weights = jnp.where(allowed, jnp.exp(capped), 0.0)
    probs = weights / lax.optimization_barrier(jnp.sum(weights, axis=-1, keepdims=True))
    probs_b = probs.astype(jnp.bfloat16)
    row_used = positions < length
    cot = jnp.where(row_used[:, None], cotangent, jnp.zeros_like(cotangent))
    cot_heads = cot.reshape(count, kv_count, group_size, HD).astype(jnp.float32)
    dprob = jnp.einsum('ikgh,jkh->kgij', cot_heads, value_heads)
    row_total = lax.optimization_barrier(jnp.sum(probs * dprob, axis=-1, keepdims=True))
    dscore = (probs * (dprob - row_total) * (1.0 - (capped / soft_cap) ** 2) * score_scale).astype(jnp.bfloat16)
    dscore_f = dscore.astype(jnp.float32)
    query_gradient = jnp.einsum('kgij,jkh->ikgh', dscore_f, key_heads).reshape(count, -1).astype(jnp.bfloat16)
    dkey = jnp.einsum('kgij,ikgh->jkh', dscore_f, query_heads).reshape(count, -1).astype(jnp.bfloat16)
    value_gradient = jnp.einsum('kgij,ikgh->jkh', probs_b.astype(jnp.float32), cot_heads).reshape(count, -1).astype(jnp.bfloat16)
    return (low_rank_query, low_rank_value, query_gradient, dkey, value_gradient)

def one_sequence(input_rows, cotangent, length, chosen, query_down, query_up, value_down, value_up, w_query, w_key, w_value):
    down_q = query_down[chosen]
    query_up_weight = query_up[chosen]
    down_v = value_down[chosen]
    value_up_weight = value_up[chosen]
    low_rank_query, low_rank_value, query_gradient, dkey, value_gradient = core_backward(input_rows, cotangent, length, down_q, query_up_weight, down_v, value_up_weight, w_query, w_key, w_value)
    low_rank_query_gradient = (adapter_scale * jnp.dot(query_gradient, query_up_weight.T, preferred_element_type=jnp.float32)).astype(jnp.bfloat16)
    low_rank_value_gradient = (adapter_scale * jnp.dot(value_gradient, value_up_weight.T, preferred_element_type=jnp.float32)).astype(jnp.bfloat16)
    total = jnp.dot(query_gradient, w_query.T, preferred_element_type=jnp.float32)
    total = total + jnp.dot(dkey, w_key.T, preferred_element_type=jnp.float32)
    total = total + jnp.dot(value_gradient, w_value.T, preferred_element_type=jnp.float32)
    total = total + jnp.dot(low_rank_query_gradient, down_q, preferred_element_type=jnp.float32)
    total = total + jnp.dot(low_rank_value_gradient, down_v, preferred_element_type=jnp.float32)
    term_qa = jnp.dot(low_rank_query_gradient.T, input_rows, preferred_element_type=jnp.float32)
    query_up_contribution = adapter_scale * jnp.dot(low_rank_query.T, query_gradient, preferred_element_type=jnp.float32)
    term_va = jnp.dot(low_rank_value_gradient.T, input_rows, preferred_element_type=jnp.float32)
    value_up_contribution = adapter_scale * jnp.dot(low_rank_value.T, value_gradient, preferred_element_type=jnp.float32)
    return (total.astype(jnp.bfloat16), term_qa, query_up_contribution, term_va, value_up_contribution)

def reference(x_in, lengths, adapter_ids, attn_grad, w_query, w_key, w_value, query_down, query_up, value_down, value_up):

    def step(items):
        input_rows, cotangent, length, chosen = items
        return one_sequence(input_rows, cotangent, length, chosen, query_down, query_up, value_down, value_up, w_query, w_key, w_value)
    grad_input, terms_qa, terms_qb, terms_va, terms_vb = lax.map(step, (x_in, attn_grad, lengths, adapter_ids))
    owners = (adapter_ids[:, None] == jnp.arange(ADAPTERS, dtype=jnp.int32)[None, :]).astype(jnp.float32)
    hp = lax.Precision.HIGHEST
    grad_qa = jnp.einsum('sa,srd->ard', owners, terms_qa, precision=hp)
    grad_qb = jnp.einsum('sa,srd->ard', owners, terms_qb, precision=hp)
    grad_va = jnp.einsum('sa,srd->ard', owners, terms_va, precision=hp)
    grad_vb = jnp.einsum('sa,srd->ard', owners, terms_vb, precision=hp)
    return (grad_input, grad_qa, grad_qb, grad_va, grad_vb)
```

```python
import math

import jax
import jax.numpy as jnp
from jax import lax
from jax.sharding import PartitionSpec as P

D = 4608
HEADS = 32
HD = 128


soft_cap = 50.0
adapter_scale = 2.0


def core_backward(
    input_rows,
    cotangent,
    length,
    down_q,
    query_up_weight,
    down_v,
    value_up_weight,
    frozen_query_weight,
    base_k,
    frozen_value_weight,
):
    count = input_rows.shape[0]
    score_scale = 1.0 / math.sqrt(D // HEADS)
    low_rank_query = lax.dot_general(
        input_rows, down_q, (((1,), (1,)), ((), ())), preferred_element_type=jnp.float32
    ).astype(jnp.bfloat16)
    low_rank_value = lax.dot_general(
        input_rows, down_v, (((1,), (1,)), ((), ())), preferred_element_type=jnp.float32
    ).astype(jnp.bfloat16)
    query_rows = (
        frozen_query_weight
        + adapter_scale
        * jnp.dot(low_rank_query, query_up_weight, preferred_element_type=jnp.float32)
    ).astype(jnp.bfloat16)
    keys = base_k.astype(jnp.bfloat16)
    value_rows = (
        frozen_value_weight
        + adapter_scale
        * jnp.dot(low_rank_value, value_up_weight, preferred_element_type=jnp.float32)
    ).astype(jnp.bfloat16)
    kv_count = keys.shape[1] // HD
    group_size = query_rows.shape[1] // keys.shape[1]
    query_heads = query_rows.reshape(count, kv_count, group_size, HD)
    key_heads = keys.reshape(count, kv_count, HD)
    value_heads = value_rows.reshape(count, kv_count, HD)
    raw = (
        jnp.einsum("ikgh,jkh->kgij", query_heads, key_heads, preferred_element_type=jnp.float32)
        * score_scale
    )
    capped = soft_cap * jnp.tanh(raw / soft_cap)
    positions = lax.iota(jnp.int32, count)
    allowed = (positions[None, :] <= positions[:, None]) & (positions[None, :] < length)
    weights = jnp.where(allowed, jnp.exp(capped), 0.0)
    probs = weights / jnp.sum(weights, axis=-1, keepdims=True)
    probs_b = probs.astype(jnp.bfloat16)
    row_used = positions < length
    cot = jnp.where(row_used[:, None], cotangent, jnp.zeros_like(cotangent))
    cot_heads = cot.reshape(count, kv_count, group_size, HD)
    dprob = jnp.einsum("ikgh,jkh->kgij", cot_heads, value_heads, preferred_element_type=jnp.float32)
    row_total = jnp.sum(probs * dprob, axis=-1, keepdims=True)
    dscore = (probs * (dprob - row_total) * (1.0 - (capped / soft_cap) ** 2) * score_scale).astype(
        jnp.bfloat16
    )
    query_gradient = (
        jnp.einsum("kgij,jkh->ikgh", dscore, key_heads, preferred_element_type=jnp.float32)
        .reshape(count, -1)
        .astype(jnp.bfloat16)
    )
    dkey = (
        jnp.einsum("kgij,ikgh->jkh", dscore, query_heads, preferred_element_type=jnp.float32)
        .reshape(count, -1)
        .astype(jnp.bfloat16)
    )
    value_gradient = (
        jnp.einsum("kgij,ikgh->jkh", probs_b, cot_heads, preferred_element_type=jnp.float32)
        .reshape(count, -1)
        .astype(jnp.bfloat16)
    )
    return (low_rank_query, low_rank_value, query_gradient, dkey, value_gradient)


def pick_adapter(chosen_row, table):
    return jnp.einsum("a,ard->rd", chosen_row, table, preferred_element_type=jnp.float32).astype(
        jnp.bfloat16
    )


def flipped_matrix_product(left, right):
    return lax.dot_general(
        left, right, (((1,), (1,)), ((), ())), preferred_element_type=jnp.float32
    )


def shards(
    x_in,
    lengths,
    adapter_ids,
    attn_grad,
    w_query,
    w_key,
    w_value,
    query_down,
    query_up,
    value_down,
    value_up,
):
    x_local = x_in[0]
    local_width = x_local.shape[1]
    length = lengths[0]
    x_whole = lax.all_gather(x_local, "tensor", axis=1, tiled=True)
    all_ids = lax.all_gather(adapter_ids, ("dp", "fsdp"), axis=0, tiled=True)
    w_rows = lax.all_gather(
        jnp.concatenate([w_query, w_key, w_value], axis=1), "fsdp", axis=0, tiled=True
    )
    q_width, kv_width = w_query.shape[1], w_key.shape[1]
    query_adapter_rows = w_rows[:, :q_width]
    rows_k = w_rows[:, q_width : q_width + kv_width]
    value_adapter_rows = w_rows[:, q_width + kv_width :]
    frozen_query_weight = jnp.dot(x_whole, query_adapter_rows, preferred_element_type=jnp.float32)
    base_k = jnp.dot(x_whole, rows_k, preferred_element_type=jnp.float32)
    frozen_value_weight = jnp.dot(x_whole, value_adapter_rows, preferred_element_type=jnp.float32)
    adapter_count = query_down.shape[0]
    chosen_row = (lax.iota(jnp.int32, adapter_count) == adapter_ids[0]).astype(jnp.bfloat16)
    down_q = pick_adapter(chosen_row, query_down)
    query_up_weight = pick_adapter(chosen_row, query_up)
    down_v = pick_adapter(chosen_row, value_down)
    value_up_weight = pick_adapter(chosen_row, value_up)
    low_rank_query, low_rank_value, query_gradient, dkey, value_gradient = core_backward(
        x_whole,
        attn_grad[0],
        length,
        down_q,
        query_up_weight,
        down_v,
        value_up_weight,
        frozen_query_weight,
        base_k,
        frozen_value_weight,
    )
    query_portion = adapter_scale * flipped_matrix_product(query_gradient, query_up_weight)
    value_portion = adapter_scale * flipped_matrix_product(value_gradient, value_up_weight)
    sum_q, sum_v = lax.psum((query_portion, value_portion), "tensor")
    low_rank_query_gradient = sum_q.astype(jnp.bfloat16)
    low_rank_value_gradient = sum_v.astype(jnp.bfloat16)
    partial_value = flipped_matrix_product(query_gradient, query_adapter_rows)
    partial_value = partial_value + flipped_matrix_product(dkey, rows_k)
    partial_value = partial_value + flipped_matrix_product(value_gradient, value_adapter_rows)
    summed = lax.psum_scatter(partial_value, "tensor", scatter_dimension=1, tiled=True)
    first_column = lax.axis_index("tensor") * local_width
    slice_q = lax.dynamic_slice_in_dim(down_q, first_column, local_width, 1)
    slice_v = lax.dynamic_slice_in_dim(down_v, first_column, local_width, 1)
    summed = summed + jnp.dot(low_rank_query_gradient, slice_q, preferred_element_type=jnp.float32)
    summed = summed + jnp.dot(low_rank_value_gradient, slice_v, preferred_element_type=jnp.float32)
    grad_input = summed.astype(jnp.bfloat16)[None]
    term_qa = jnp.dot(low_rank_query_gradient.T, x_local, preferred_element_type=jnp.float32)
    query_up_contribution = adapter_scale * jnp.dot(
        low_rank_query.T, query_gradient, preferred_element_type=jnp.float32
    )
    term_va = jnp.dot(low_rank_value_gradient.T, x_local, preferred_element_type=jnp.float32)
    value_up_contribution = adapter_scale * jnp.dot(
        low_rank_value.T, value_gradient, preferred_element_type=jnp.float32
    )
    terms = jnp.concatenate(
        [term_qa, query_up_contribution, term_va, value_up_contribution], axis=1
    ).astype(jnp.bfloat16)
    all_terms = lax.all_gather(terms, ("dp", "fsdp"), axis=0)
    owners = (all_ids[:, None] == lax.iota(jnp.int32, adapter_count)[None, :]).astype(jnp.bfloat16)
    tables = jnp.einsum("sa,srd->ard", owners, all_terms, preferred_element_type=jnp.float32)
    qd, qu = term_qa.shape[1], query_up_contribution.shape[1]
    grad_qa = tables[:, :, :qd]
    grad_qb = tables[:, :, qd : qd + qu]
    grad_va = tables[:, :, qd + qu : 2 * qd + qu]
    grad_vb = tables[:, :, 2 * qd + qu :]
    return (grad_input, grad_qa, grad_qb, grad_va, grad_vb)


def solution(mesh):
    placed = (
        P(("dp", "fsdp"), None, "tensor"),
        P(("dp", "fsdp")),
        P(("dp", "fsdp")),
        P(("dp", "fsdp"), None, "tensor"),
        P("fsdp", "tensor"),
        P("fsdp", "tensor"),
        P("fsdp", "tensor"),
        P(),
        P(None, None, "tensor"),
        P(),
        P(None, None, "tensor"),
    )
    return jax.shard_map(
        shards,
        mesh=mesh,
        in_specs=placed,
        out_specs=(
            P(("dp", "fsdp"), None, "tensor"),
            P(None, None, "tensor"),
            P(None, None, "tensor"),
            P(None, None, "tensor"),
            P(None, None, "tensor"),
        ),
        check_vma=False,
    )
```

```python
import math

import jax
import jax.numpy as jnp
from jax import lax
from jax.experimental import pallas as pl
from jax.experimental.pallas import tpu as pltpu
from jax.sharding import PartitionSpec as P

D = 4608
HD = 128
TOKENS = 512
RANK = 16
ADAPTERS = 16
SIDE = 4
ROWS = 288
GROUP = 512
COLS = 1152
TERM = 3840
BLOCK = TERM + 128

soft_cap = 50.0
adapter_scale = 2.0
score_scale = 1.0 / 12.0

MESH = pl.DeviceIdType.MESH
F32 = jnp.float32
BF16 = jnp.bfloat16
VMEM_BYTES = 60 * 1024 * 1024


def dot(a, b, dims):
    return lax.dot_general(a, b, (dims, ((), ())), preferred_element_type=F32)


class Place:
    def __init__(self):
        self.dp = lax.axis_index("dp")
        self.f = lax.axis_index("fsdp")
        self.t = lax.axis_index("tensor")
        self.y, self.z = self.f // SIDE, self.f % SIDE
        self.core = self.t % 2
        self.x = self.dp * 2 + self.t // 2

    def at_x(self, x, core):
        return (x // 2, self.f, (x % 2) * 2 + core)

    def step_x(self, n):
        return (self.x + n) % SIDE

    def ring_x(self, n):
        return self.at_x(self.step_x(n), self.core)

    def sibling(self):
        return self.at_x(self.x, 1 - self.core)

    def ring_y(self, n):
        return (self.dp, ((self.y + n) % SIDE) * SIDE + self.z, self.t)

    def ring_z(self, n):
        return (self.dp, self.y * SIDE + (self.z + n) % SIDE, self.t)


class Net:
    def __init__(self, send_sems, recv_sems):
        self.send_sems, self.recv_sems = send_sems, recv_sems
        self.started = []

    def send(self, index, src, dst, device):
        copy = pltpu.make_async_remote_copy(
            src_ref=src,
            dst_ref=dst,
            send_sem=self.send_sems.at[index],
            recv_sem=self.recv_sems.at[index],
            device_id=device,
            device_id_type=MESH,
        )
        copy.start()
        self.started.append(copy)

    def arrived(self, index, region, device):
        pltpu.make_async_remote_copy(
            src_ref=region,
            dst_ref=region,
            send_sem=self.send_sems.at[index],
            recv_sem=self.recv_sems.at[index],
            device_id=device,
            device_id_type=MESH,
        ).wait_recv()

    def finish(self):
        for copy in self.started:
            copy.wait_send()


def enter(peers):
    barrier = pltpu.get_barrier_semaphore()
    for peer in peers:
        pl.semaphore_signal(barrier, inc=1, device_id=peer, device_id_type=MESH)
    pl.semaphore_wait(barrier, len(peers))


class TorusGather:
    def __init__(self, net, base, place, y_first, view, whole, low, high):
        self.net, self.base = net, base
        self.whole, self.low, self.high = whole, low, high
        p = place
        if y_first:
            self.one, self.two = p.ring_y, p.ring_z
            self.block = lambda n, w: view((p.y + n) % SIDE, p.z, w)
            self.line = lambda n, w: view(None, (p.z + n) % SIDE, w)
        else:
            self.one, self.two = p.ring_z, p.ring_y
            self.block = lambda n, w: view(p.y, (p.z + n) % SIDE, w)
            self.line = lambda n, w: view((p.y + n) % SIDE, None, w)

    def fan(self, base, region, ring):
        own = region(0, self.whole)
        self.net.send(base, own, own, ring(1))
        self.net.send(base + 1, own, own, ring(-1))

    def forward(self, base, region, ring):
        self.net.arrived(base, region(-1, self.whole), ring(-1))
        part = region(-1, self.low)
        self.net.send(base + 2, part, part, ring(1))
        self.net.arrived(base + 1, region(1, self.whole), ring(1))
        part = region(1, self.high)
        self.net.send(base + 3, part, part, ring(-1))

    def close(self, base, region, ring):
        self.net.arrived(base + 2, region(2, self.low), ring(-1))
        self.net.arrived(base + 3, region(2, self.high), ring(1))

    def stage(self, n):
        if n == 1:
            self.fan(self.base, self.block, self.one)
        elif n == 2:
            self.forward(self.base, self.block, self.one)
        elif n == 3:
            self.close(self.base, self.block, self.one)
            self.fan(self.base + 4, self.line, self.two)
        elif n == 4:
            self.forward(self.base + 4, self.line, self.two)
        else:
            self.close(self.base + 4, self.line, self.two)


def gather_kernel(
    x_ref, g_ref, wq_ref, wk_ref, wv_ref, meta_ref, qd_ref, vd_ref, qu_ref, vu_ref,
    w_out, qkv_out, low_out, up_out, down_out, g_out, meta_out,
    xs, ws, qds, vds, down, send_sems, recv_sems, local_sems, first_sems,
):
    p = Place()
    net = Net(send_sems, recv_sems)
    my_cols = pl.ds(pl.multiple_of(p.t * COLS, COLS), COLS)
    half = lambda ref, dp, width: ref.at[:, pl.ds(pl.multiple_of(dp * width, width), width)]

    first = [pltpu.make_async_copy(x_ref, xs.at[p.dp, :, my_cols], first_sems.at[0])]
    for g in range(2):
        c0 = g * GROUP
        for n, (ref, at, width) in enumerate(
            ((wq_ref, c0, 256), (wk_ref, c0 + 256, 128), (wv_ref, c0 + 384, 128))
        ):
            source = ref.at[:, pl.ds(pl.multiple_of(p.dp * 2 * width + g * width, width), width)]
            first.append(
                pltpu.make_async_copy(
                    source,
                    ws.at[p.y, pl.ds(pl.multiple_of(p.z * ROWS, 32), ROWS), at : at + width],
                    first_sems.at[1 + 3 * g + n],
                )
            )
    for copy in first:
        copy.start()
    later = [
        pltpu.make_async_copy(qd_ref, qds, local_sems.at[0]),
        pltpu.make_async_copy(vd_ref, vds, local_sems.at[1]),
        pltpu.make_async_copy(half(g_ref, p.dp, 512), g_out.at[p.dp], local_sems.at[2]),
    ]
    for copy in later:
        copy.start()
    meta_out[p.dp] = meta_ref[...]

    partner = p.ring_x(2)
    enter([
        p.ring_x(1), p.ring_x(-1), partner, p.sibling(),
        p.ring_y(1), p.ring_y(-1), p.ring_z(1), p.ring_z(-1),
    ])

    def x_block(n, core, rows=slice(None)):
        chip = p.step_x(n)
        column = pl.multiple_of(((chip % 2) * 2 + core) * COLS, COLS)
        return xs.at[chip // 2, rows, pl.ds(column, COLS)]

    upper, lower = slice(0, 256), slice(256, 512)
    net.send(0, meta_out.at[p.dp], meta_out.at[p.dp], partner)
    for copy in first:
        copy.wait()

    def view(y, z, window):
        rows = slice(None) if z is None else pl.ds(pl.multiple_of(z * ROWS, 32), ROWS)
        return ws.at[slice(None) if y is None else y, rows, window]

    gathers = []
    for g in range(2):
        for h in range(2):
            c = g * GROUP + h * 256
            gathers.append(
                TorusGather(
                    net, 16 + 8 * (2 * g + h), p, h == 0, view,
                    slice(c, c + 256), slice(c, c + 128), slice(c + 128, c + 256),
                )
            )

    def weights(g, stage):
        for one in gathers[2 * g : 2 * g + 2]:
            one.stage(stage)

    own = x_block(0, p.core)
    weights(0, 1)
    net.send(1, own, own, p.ring_x(1))
    net.send(2, own, own, p.ring_x(-1))
    net.send(3, own, own, p.sibling())
    net.send(4, half(g_ref, 1 - p.dp, 512), g_out.at[p.dp], partner)
    weights(0, 2)
    weights(1, 1)
    weights(0, 3)
    weights(1, 2)

    for copy in later:
        copy.wait()
    net.arrived(0, meta_out.at[1 - p.dp], partner)
    up_out[...] = jnp.zeros_like(up_out)
    for s in range(2):
        chosen = meta_out[s, 0:1, 0:1]

        def add(a, sums):
            weight = (chosen == a).astype(F32)
            return (
                sums[0] + qds[a].astype(F32) * weight,
                sums[1] + vds[a].astype(F32) * weight,
                sums[2] + qu_ref[a].astype(F32) * weight,
                sums[3] + vu_ref[a].astype(F32) * weight,
            )

        zero = lambda width: jnp.zeros((RANK, width), F32)
        q_rows, v_rows, q_up, v_up = lax.fori_loop(
            0, ADAPTERS, add, (zero(D), zero(D), zero(512), zero(256))
        )
        down[s, :RANK, :] = q_rows.astype(BF16)
        down[s, RANK:, :] = v_rows.astype(BF16)
        for g in range(2):
            c0 = g * GROUP
            up_out[s, :RANK, c0 : c0 + 256] = q_up[:, g * 256 : g * 256 + 256].astype(BF16)
            up_out[s, RANK:, c0 + 384 : c0 + 512] = v_up[:, g * 128 : g * 128 + 128].astype(BF16)
    down_out[...] = down[p.dp, :, my_cols]

    net.arrived(1, x_block(-1, p.core), p.ring_x(-1))
    part = x_block(-1, p.core, upper)
    net.send(5, part, part, p.ring_x(1))
    part = x_block(-1, p.core)
    net.send(6, part, part, p.sibling())
    net.arrived(2, x_block(1, p.core), p.ring_x(1))
    part = x_block(1, p.core, lower)
    net.send(7, part, part, p.ring_x(-1))
    part = x_block(1, p.core)
    net.send(8, part, part, p.sibling())
    weights(0, 4)
    weights(1, 3)
    net.arrived(5, x_block(2, p.core, upper), p.ring_x(-1))
    part = x_block(2, p.core, upper)
    net.send(9, part, part, p.sibling())
    net.arrived(7, x_block(2, p.core, lower), p.ring_x(1))
    part = x_block(2, p.core, lower)
    net.send(10, part, part, p.sibling())
    other = 1 - p.core
    net.arrived(3, x_block(0, other), p.sibling())
    net.arrived(6, x_block(-1, other), p.sibling())
    net.arrived(8, x_block(1, other), p.sibling())
    net.arrived(9, x_block(2, other, upper), p.sibling())
    net.arrived(10, x_block(2, other, lower), p.sibling())
    weights(0, 5)
    weights(1, 4)

    @pl.loop(0, 2)
    def _(s):
        low_out[s] = dot(xs[s], down[s], ((1,), (1,))).astype(BF16)

    def project(g):
        @pl.loop(0, 4)
        def _(n):
            s = n // 2
            window = pl.ds(pl.multiple_of(g * GROUP + (n % 2) * 256, 256), 256)
            base = dot(xs[s], ws[:, :, window].reshape(D, 256), ((1,), (0,)))
            extra = dot(low_out[s], up_out[s, :, window], ((1,), (0,)))
            qkv_out[s, :, window] = (base + adapter_scale * extra).astype(BF16)

    project(0)
    weights(1, 5)
    save = pltpu.make_async_copy(ws, w_out, local_sems.at[3])
    save.start()
    project(1)
    net.arrived(4, g_out.at[1 - p.dp], partner)
    net.finish()
    save.wait()


def gather_call(x, g, wq, wk, wv, meta, qd, vd, qu, vu):
    hbm = pl.BlockSpec(memory_space=pl.ANY)
    vmem = pl.BlockSpec(memory_space=pltpu.VMEM)
    return pl.pallas_call(
        gather_kernel,
        name="gather_project",
        out_shape=(
            jax.ShapeDtypeStruct((SIDE, COLS, 2 * GROUP), BF16),
            jax.ShapeDtypeStruct((2, TOKENS, 2 * GROUP), BF16),
            jax.ShapeDtypeStruct((2, TOKENS, 2 * RANK), BF16),
            jax.ShapeDtypeStruct((2, 2 * RANK, 2 * GROUP), BF16),
            jax.ShapeDtypeStruct((2 * RANK, COLS), BF16),
            jax.ShapeDtypeStruct((2, TOKENS, 512), BF16),
            jax.ShapeDtypeStruct((2, 8, 128), jnp.int32),
        ),
        in_specs=[hbm] * 5 + [vmem, hbm, hbm, vmem, vmem],
        out_specs=(hbm, vmem, vmem, vmem, vmem, hbm, vmem),
        scratch_shapes=[
            pltpu.VMEM((2, TOKENS, D), BF16),
            pltpu.VMEM((SIDE, COLS, 2 * GROUP), BF16),
            pltpu.VMEM((ADAPTERS, RANK, D), BF16),
            pltpu.VMEM((ADAPTERS, RANK, D), BF16),
            pltpu.VMEM((2, 2 * RANK, D), BF16),
            pltpu.SemaphoreType.DMA((48,)),
            pltpu.SemaphoreType.DMA((48,)),
            pltpu.SemaphoreType.DMA((4,)),
            pltpu.SemaphoreType.DMA((7,)),
        ],
        compiler_params=pltpu.CompilerParams(
            collective_id=0, has_side_effects=True, vmem_limit_bytes=VMEM_BYTES
        ),
    )(x, g, wq, wk, wv, meta, qd, vd, qu, vu)


def attention_kernel(
    qkv_ref, cot_ref, low_ref, up_ref, meta_ref, d_ref, dlow_ref, term_ref, dk_acc, dv_acc
):
    s, g = pl.program_id(0), pl.program_id(1)
    length = meta_ref[0, 1:2, 0:1]
    k = qkv_ref[0, :, 256:384]
    v = qkv_ref[0, :, 384:512]
    dk_acc[...] = jnp.zeros_like(dk_acc)
    dv_acc[...] = jnp.zeros_like(dv_acc)
    step = 256
    for ib in range(TOKENS // step):
        rows = slice(ib * step, (ib + 1) * step)
        span = (ib + 1) * step
        key_at = lax.broadcasted_iota(jnp.int32, (span, step), 0)
        row_at = lax.broadcasted_iota(jnp.int32, (span, step), 1) + ib * step
        allowed = (key_at <= row_at) & (key_at < length)
        used = lax.broadcasted_iota(jnp.int32, (step, HD), 0) + ib * step < length
        for h in range(2):
            head = slice(h * HD, (h + 1) * HD)
            q = qkv_ref[0, rows, head]
            cot = cot_ref[0, rows, head]
            cot = jnp.where(used, cot, jnp.zeros_like(cot))
            raw = dot(k[:span], q, ((1,), (1,)))
            turned = jnp.tanh(raw * (score_scale / soft_cap))
            weights = jnp.where(allowed, jnp.exp(soft_cap * turned), 0.0)
            probs = weights * (1.0 / jnp.sum(weights, axis=0, keepdims=True))
            probs_b = probs.astype(BF16)
            dprob = dot(v[:span], cot, ((1,), (1,)))
            row_total = jnp.sum(probs * dprob, axis=0, keepdims=True)
            dscore = (
                probs * (dprob - row_total) * ((1.0 - turned * turned) * score_scale)
            ).astype(BF16)
            dq = dot(k[:span], dscore, ((0,), (0,)))
            d_ref[0, rows, head] = dq.T.astype(BF16)
            dk_acc[:span] += dot(dscore, q, ((1,), (0,)))
            dv_acc[:span] += dot(probs_b, cot, ((1,), (0,)))
    d_ref[0, :, 256:384] = dk_acc[...].astype(BF16)
    d_ref[0, :, 384:512] = dv_acc[...].astype(BF16)
    grads = d_ref[0]
    dlow = adapter_scale * dot(up_ref[0], grads, ((1,), (1,)))

    @pl.when(g == 0)
    def _():
        dlow_ref[0] = dlow

    @pl.when(g == 1)
    def _():
        dlow_ref[0] += dlow

    terms = (adapter_scale * dot(low_ref[0], grads, ((0,), (0,)))).astype(BF16)
    q_at = pl.multiple_of(s * 512 + g * 256, 256)
    v_at = pl.multiple_of(1024 + s * 256 + g * 128, 128)
    term_ref[:, pl.ds(q_at, 256)] = terms[:RANK, 0:256]
    term_ref[:, pl.ds(v_at, 128)] = terms[RANK:, 384:512]


def attention_call(qkv, cot, low, up, meta):
    return pl.pallas_call(
        attention_kernel,
        name="attention",
        grid=(2, 2),
        out_shape=(
            jax.ShapeDtypeStruct((2, TOKENS, 2 * GROUP), BF16),
            jax.ShapeDtypeStruct((2, 2 * RANK, TOKENS), F32),
            jax.ShapeDtypeStruct((RANK, 1536), BF16),
        ),
        in_specs=[
            pl.BlockSpec((1, TOKENS, GROUP), lambda s, g: (s, 0, g)),
            pl.BlockSpec((1, TOKENS, 256), lambda s, g: (s, 0, g)),
            pl.BlockSpec((1, TOKENS, 2 * RANK), lambda s, g: (s, 0, 0)),
            pl.BlockSpec((1, 2 * RANK, GROUP), lambda s, g: (s, 0, g)),
            pl.BlockSpec((1, 8, 128), lambda s, g: (s, 0, 0)),
        ],
        out_specs=(
            pl.BlockSpec((1, TOKENS, GROUP), lambda s, g: (s, 0, g)),
            pl.BlockSpec((1, 2 * RANK, TOKENS), lambda s, g: (s, 0, 0)),
            pl.BlockSpec((RANK, 1536), lambda s, g: (0, 0)),
        ),
        scratch_shapes=[pltpu.VMEM((TOKENS, HD), F32), pltpu.VMEM((TOKENS, HD), F32)],
        compiler_params=pltpu.CompilerParams(
            dimension_semantics=("arbitrary", "arbitrary"), vmem_limit_bytes=VMEM_BYTES
        ),
    )(qkv, cot, low, up, meta)


def scatter_kernel(
    d_ref, w_ref, x_ref, dlow_ref, up_term_ref, down_ref, tag_ref,
    grad_out, table_out,
    ws, sib_out, sib_in, ring_out, relay_in, ring_in, chip_low, sib_low, low_in, tables,
    send_sems, recv_sems, local_sems,
):
    p = Place()
    net = Net(send_sems, recv_sems)
    load = pltpu.make_async_copy(w_ref, ws, local_sems.at[0])
    load.start()
    partner = p.ring_x(2)
    sib = p.sibling()
    enter([
        p.ring_x(1), p.ring_x(-1), partner, sib,
        p.ring_y(1), p.ring_y(-1), p.ring_z(1), p.ring_z(-1),
    ])
    net.send(0, dlow_ref, sib_low, sib)

    chunk = 384

    def for_sibling(slot, n):
        chip = p.step_x(n)
        part = (chip % 2) * 2 + 1 - p.core
        for c in range(0, COLS, chunk):
            value = dot(d_ref[chip // 2], ws[part, c : c + chunk], ((1,), (1,)))
            sib_out[slot, :, c : c + chunk] = value.astype(BF16)
        net.send(1 + slot, sib_out.at[slot], sib_in.at[slot], sib)

    def own_core(slot, n):
        chip = p.step_x(n)
        part = (chip % 2) * 2 + p.core
        net.arrived(1 + slot, sib_in.at[slot], sib)
        for c in range(0, COLS, chunk):
            cols = slice(c, c + chunk)
            value = dot(d_ref[chip // 2], ws[part, cols], ((1,), (1,)))
            yield cols, value + sib_in[slot, :, cols].astype(F32)

    upper, lower = slice(0, 256), slice(256, 512)
    load.wait()
    for_sibling(0, 2)
    for_sibling(1, 1)
    net.arrived(0, sib_low, sib)
    chip_low[...] = dlow_ref[...] + sib_low[...]
    for n in (1, 2, 3):
        net.send(4 + n, chip_low.at[p.step_x(n) // 2], low_in.at[n - 1], p.ring_x(n))
    for cols, value in own_core(0, 2):
        ring_out[0, :, cols] = value.astype(BF16)
    net.send(8, ring_out.at[0, upper], relay_in.at[0], p.ring_x(1))
    net.send(9, ring_out.at[0, lower], relay_in.at[1], p.ring_x(-1))
    for_sibling(2, -1)
    for cols, value in own_core(1, 1):
        ring_out[1, :, cols] = value.astype(BF16)
    net.send(10, ring_out.at[1, lower], ring_in.at[0, lower], p.ring_x(1))
    for cols, value in own_core(2, -1):
        ring_out[2, :, cols] = value.astype(BF16)
    net.send(11, ring_out.at[2, upper], ring_in.at[1, upper], p.ring_x(-1))
    for_sibling(3, 0)

    total = chip_low[p.dp]
    for n in (1, 2, 3):
        net.arrived(4 + n, low_in.at[n - 1], p.ring_x(-n))
        total = total + low_in[n - 1]
    low_grad = total.astype(BF16)
    down_terms = dot(low_grad, x_ref[...], ((1,), (0,))).astype(BF16)
    mine = tables.at[p.dp, p.y, p.z]
    mine[:, 0:COLS] = down_terms[:RANK]
    mine[:, COLS : 2 * COLS] = down_terms[RANK:]
    mine[:, 2 * COLS : TERM] = up_term_ref[...]
    mine[:, TERM:] = tag_ref[...]
    net.send(14, mine, mine, partner)

    net.arrived(8, relay_in.at[0], p.ring_x(-1))
    ring_out[1, upper] = (ring_out[1, upper].astype(F32) + relay_in[0].astype(F32)).astype(BF16)
    net.send(12, ring_out.at[1, upper], ring_in.at[0, upper], p.ring_x(1))
    net.arrived(9, relay_in.at[1], p.ring_x(1))
    ring_out[2, lower] = (ring_out[2, lower].astype(F32) + relay_in[1].astype(F32)).astype(BF16)
    net.send(13, ring_out.at[2, lower], ring_in.at[1, lower], p.ring_x(-1))

    def view(y, z, window):
        everything = slice(None)
        return tables.at[
            :, everything if y is None else y, everything if z is None else z, :, window
        ]

    gathers = [
        TorusGather(net, 16, p, True, view, slice(0, 2048), slice(0, 1024), slice(1024, 2048)),
        TorusGather(
            net, 24, p, False, view, slice(2048, BLOCK), slice(2048, 3072), slice(3072, BLOCK)
        ),
    ]
    net.arrived(14, tables.at[1 - p.dp, p.y, p.z], partner)
    for one in gathers:
        one.stage(1)
    low_part = dot(low_grad, down_ref[...], ((0,), (0,)))
    kept = []
    for cols, value in own_core(3, 0):
        kept.append((cols, value + low_part[:, cols]))
    for stage in (2, 3, 4):
        for one in gathers:
            one.stage(stage)
    net.arrived(10, ring_in.at[0, lower], p.ring_x(-1))
    net.arrived(11, ring_in.at[1, upper], p.ring_x(1))
    net.arrived(12, ring_in.at[0, upper], p.ring_x(-1))
    net.arrived(13, ring_in.at[1, lower], p.ring_x(1))
    for cols, value in kept:
        value = value + ring_in[0, :, cols].astype(F32) + ring_in[1, :, cols].astype(F32)
        grad_out[:, cols] = value.astype(BF16)
    for one in gathers:
        one.stage(5)
    save = pltpu.make_async_copy(tables, table_out, local_sems.at[1])
    save.start()
    net.finish()
    save.wait()


def scatter_call(d, w, x, dlow, up_terms, down, tag):
    hbm = pl.BlockSpec(memory_space=pl.ANY)
    vmem = pl.BlockSpec(memory_space=pltpu.VMEM)
    return pl.pallas_call(
        scatter_kernel,
        name="scatter_sum",
        out_shape=(
            jax.ShapeDtypeStruct((TOKENS, COLS), BF16),
            jax.ShapeDtypeStruct((2, SIDE, SIDE, RANK, BLOCK), BF16),
        ),
        in_specs=[vmem, hbm, vmem, vmem, vmem, vmem, vmem],
        out_specs=(vmem, hbm),
        scratch_shapes=[
            pltpu.VMEM((SIDE, COLS, 2 * GROUP), BF16),
            pltpu.VMEM((4, TOKENS, COLS), BF16),
            pltpu.VMEM((4, TOKENS, COLS), BF16),
            pltpu.VMEM((3, TOKENS, COLS), BF16),
            pltpu.VMEM((2, 256, COLS), BF16),
            pltpu.VMEM((2, TOKENS, COLS), BF16),
            pltpu.VMEM((2, 2 * RANK, TOKENS), F32),
            pltpu.VMEM((2, 2 * RANK, TOKENS), F32),
            pltpu.VMEM((3, 2 * RANK, TOKENS), F32),
            pltpu.VMEM((2, SIDE, SIDE, RANK, BLOCK), BF16),
            pltpu.SemaphoreType.DMA((32,)),
            pltpu.SemaphoreType.DMA((32,)),
            pltpu.SemaphoreType.DMA((2,)),
        ],
        compiler_params=pltpu.CompilerParams(
            collective_id=1, has_side_effects=True, vmem_limit_bytes=VMEM_BYTES
        ),
    )(d, w, x, dlow, up_terms, down, tag)


def shards(
    x_in, lengths, adapter_ids, attn_grad, w_query, w_key, w_value,
    query_down, query_up, value_down, value_up,
):
    dp = lax.axis_index("dp")
    meta = jnp.zeros((8, 128), jnp.int32).at[0].set(adapter_ids[0]).at[1].set(lengths[0])
    tag = jnp.full((RANK, 128), adapter_ids[0], jnp.int32).astype(BF16)
    q_up = lax.dynamic_slice_in_dim(query_up, dp * 512, 512, 2)
    v_up = lax.dynamic_slice_in_dim(value_up, dp * 256, 256, 2)
    w_all, qkv, low, up, down, cot, meta_both = gather_call(
        x_in[0], attn_grad[0], w_query, w_key, w_value, meta,
        query_down, value_down, q_up, v_up,
    )
    grads, dlow, up_terms = attention_call(qkv, cot, low, up, meta_both)
    grad_input, blocks = scatter_call(grads, w_all, x_in[0], dlow, up_terms, down, tag)

    ids = blocks[:, :, :, 0, TERM].reshape(2, 16)
    owners = (ids[:, :, None] == lax.iota(jnp.int32, ADAPTERS).astype(BF16)).astype(BF16)
    blocks = blocks.reshape(2, 16, RANK, BLOCK)
    down_terms = blocks[..., : 2 * COLS]
    down_tables = jnp.einsum("dfa,dfrc->arc", owners, down_terms, preferred_element_type=F32)
    q_terms = blocks[..., 2 * COLS : 2 * COLS + 1024].reshape(2, 16, RANK, 2, 512)
    q_tables = jnp.einsum("sfa,dfrsc->ardc", owners, q_terms, preferred_element_type=F32)
    v_terms = blocks[..., 2 * COLS + 1024 : TERM].reshape(2, 16, RANK, 2, 256)
    v_tables = jnp.einsum("sfa,dfrsc->ardc", owners, v_terms, preferred_element_type=F32)
    return (
        grad_input[None],
        down_tables[..., :COLS],
        q_tables.reshape(ADAPTERS, RANK, 1024),
        down_tables[..., COLS:],
        v_tables.reshape(ADAPTERS, RANK, 512),
    )


def solution(mesh):
    placed = (
        P(("dp", "fsdp"), None, "tensor"),
        P(("dp", "fsdp")),
        P(("dp", "fsdp")),
        P(("dp", "fsdp"), None, "tensor"),
        P("fsdp", "tensor"),
        P("fsdp", "tensor"),
        P("fsdp", "tensor"),
        P(),
        P(None, None, "tensor"),
        P(),
        P(None, None, "tensor"),
    )
    return jax.shard_map(
        shards,
        mesh=mesh,
        in_specs=placed,
        out_specs=(
            P(("dp", "fsdp"), None, "tensor"),
            P(None, None, "tensor"),
            P(None, None, "tensor"),
            P(None, None, "tensor"),
            P(None, None, "tensor"),
        ),
        check_vma=False,
    )
```

```python
import math

import jax
import jax.numpy as jnp
from jax import lax
from jax.experimental import pallas as pl
from jax.experimental.pallas import tpu as pltpu
from jax.sharding import PartitionSpec as P

D = 4608
HD = 128
TOKENS = 512
RANK = 16
ADAPTERS = 16
SIDE = 4
ROWS = 288
GROUP = 512
COLS = 1152
HALF = 256
UP = 1536 + 128
DOWN = 2 * COLS

soft_cap = 50.0
adapter_scale = 2.0
score_scale = 1.0 / 12.0

MESH = pl.DeviceIdType.MESH
F32 = jnp.float32
BF16 = jnp.bfloat16
VMEM_BYTES = 60 * 1024 * 1024


def dot(a, b, dims):
    return lax.dot_general(a, b, (dims, ((), ())), preferred_element_type=F32)


class Place:
    def __init__(self):
        self.dp = lax.axis_index("dp")
        self.f = lax.axis_index("fsdp")
        self.t = lax.axis_index("tensor")
        self.y, self.z = self.f // SIDE, self.f % SIDE
        self.core = self.t % 2
        self.x_lo = self.t // 2
        x = self.dp * 2 + self.x_lo
        to_mate = 1 - 2 * self.x_lo
        at = lambda n, core: ((n % SIDE) // 2, self.f, (n % 2) * 2 + core)
        self.mate = at(x + to_mate + SIDE, self.core)
        self.cross = at(x - to_mate + SIDE, self.core)
        self.opposite = at(x + 2, self.core)
        self.sibling = at(x, 1 - self.core)

    def part(self, flip, core):
        return ((self.x_lo + flip) % 2) * 2 + core

    def ring_y(self, n):
        return (self.dp, ((self.y + n) % SIDE) * SIDE + self.z, self.t)

    def ring_z(self, n):
        return (self.dp, self.y * SIDE + (self.z + n) % SIDE, self.t)


class Net:
    def __init__(self, send_sems, recv_sems):
        self.send_sems, self.recv_sems = send_sems, recv_sems
        self.started = []

    def send(self, index, src, dst, device):
        copy = pltpu.make_async_remote_copy(
            src_ref=src,
            dst_ref=dst,
            send_sem=self.send_sems.at[index],
            recv_sem=self.recv_sems.at[index],
            device_id=device,
            device_id_type=MESH,
        )
        copy.start()
        self.started.append(copy)

    def arrived(self, index, region, device):
        pltpu.make_async_remote_copy(
            src_ref=region,
            dst_ref=region,
            send_sem=self.send_sems.at[index],
            recv_sem=self.recv_sems.at[index],
            device_id=device,
            device_id_type=MESH,
        ).wait_recv()

    def finish(self):
        for copy in self.started:
            copy.wait_send()


def enter(peers):
    barrier = pltpu.get_barrier_semaphore()
    for peer in peers:
        pl.semaphore_signal(barrier, inc=1, device_id=peer, device_id_type=MESH)
    pl.semaphore_wait(barrier, len(peers))


class TorusGather:
    def __init__(self, net, base, place, y_first, view, whole, low, high):
        self.net, self.base = net, base
        self.whole, self.low, self.high = whole, low, high
        p = place
        if y_first:
            self.one, self.two = p.ring_y, p.ring_z
            self.block = lambda n, w: view((p.y + n) % SIDE, p.z, w)
            self.line = lambda n, w: view(None, (p.z + n) % SIDE, w)
        else:
            self.one, self.two = p.ring_z, p.ring_y
            self.block = lambda n, w: view(p.y, (p.z + n) % SIDE, w)
            self.line = lambda n, w: view((p.y + n) % SIDE, None, w)

    def fan(self, base, region, ring):
        own = region(0, self.whole)
        self.net.send(base, own, own, ring(1))
        self.net.send(base + 1, own, own, ring(-1))

    def forward(self, base, region, ring):
        self.net.arrived(base, region(-1, self.whole), ring(-1))
        part = region(-1, self.low)
        self.net.send(base + 2, part, part, ring(1))
        self.net.arrived(base + 1, region(1, self.whole), ring(1))
        part = region(1, self.high)
        self.net.send(base + 3, part, part, ring(-1))

    def close(self, base, region, ring):
        self.net.arrived(base + 2, region(2, self.low), ring(-1))
        self.net.arrived(base + 3, region(2, self.high), ring(1))

    def stage(self, n):
        if n == 1:
            self.fan(self.base, self.block, self.one)
        elif n == 2:
            self.forward(self.base, self.block, self.one)
        elif n == 3:
            self.close(self.base, self.block, self.one)
            self.fan(self.base + 4, self.line, self.two)
        elif n == 4:
            self.forward(self.base + 4, self.line, self.two)
        else:
            self.close(self.base + 4, self.line, self.two)


OWN, OTHER = 0, 1
TO_OPPOSITE, TO_CROSS, TO_MATE, TO_OWN = 0, 1, 2, 3
UPPER, LOWER = slice(HALF, TOKENS), slice(0, HALF)


def block_kernel(
    length_ref, id_ref, x_ref, g_ref, wq_ref, wk_ref, wv_ref, qd_ref, vd_ref, qu_ref, vu_ref,
    grad_out, up_out, down_out,
    xs, ws, qds, vds, qus, vus, down, up, low, qkv, grads, cots, meta, dk_acc, dv_acc,
    sib_out, sib_in, ring_out, relay_in, ring_in, kept,
    low_mine, low_sib, low_chip, low_in, up_terms, down_terms,
    send_sems, recv_sems, local_sems,
):
    p = Place()
    net = Net(send_sems, recv_sems)
    copies = iter(range(32))

    def local(src, dst):
        copy = pltpu.make_async_copy(src, dst, local_sems.at[next(copies)])
        copy.start()
        return copy

    def cols_of(ref, start, width):
        return ref.at[..., pl.ds(pl.multiple_of(start, width), width)]

    def x_block(slot, flip, core, rows=slice(None)):
        column = pl.multiple_of(p.part(flip, core) * COLS, COLS)
        return xs.at[slot, rows, pl.ds(column, COLS)]

    my_rows = pl.ds(pl.multiple_of(p.z * ROWS, 32), ROWS)
    first = []
    for g in range(2):
        for ref, at, width in ((wq_ref, 0, 256), (wk_ref, 256, 128), (wv_ref, 384, 128)):
            c = g * GROUP + at
            first.append(
                local(
                    cols_of(ref, p.dp * 2 * width + g * width, width),
                    ws.at[p.y, my_rows, c : c + width],
                )
            )
    first.append(local(x_ref, x_block(OWN, 0, p.core)))
    later = [
        local(qd_ref, qds),
        local(vd_ref, vds),
        local(cols_of(qu_ref, p.dp * 512, 512), qus),
        local(cols_of(vu_ref, p.dp * 256, 256), vus),
        local(cols_of(g_ref, p.dp * 512, 512), cots.at[OWN]),
    ]
    line = lax.broadcasted_iota(jnp.int32, (8, 128), 0)
    meta[OWN] = jnp.where(line == 0, id_ref[0], length_ref[0])

    enter([
        p.mate, p.cross, p.opposite, p.sibling,
        p.ring_y(1), p.ring_y(-1), p.ring_z(1), p.ring_z(-1),
    ])

    net.send(0, meta.at[OWN], meta.at[OTHER], p.opposite)
    for copy in first:
        copy.wait()

    def weight_view(y, z, window):
        rows = slice(None) if z is None else pl.ds(pl.multiple_of(z * ROWS, 32), ROWS)
        return ws.at[slice(None) if y is None else y, rows, window]

    rounds = []
    for g in range(2):
        pair = []
        for h in range(2):
            c = g * GROUP + h * 256
            pair.append(
                TorusGather(
                    net, 32 + 8 * (2 * g + h), p, h == 0, weight_view,
                    slice(c, c + 256), slice(c, c + 128), slice(c + 128, c + 256),
                )
            )
        rounds.append(pair)

    def weights(g, stage):
        for one in rounds[g]:
            one.stage(stage)

    def x_send(index, slot, flip, rows, to_slot, device):
        net.send(
            index, x_block(slot, flip, p.core, rows), x_block(to_slot, flip, p.core, rows), device
        )

    weights(0, 1)
    weights(1, 1)
    every = slice(None)
    x_send(1, OWN, 0, UPPER, OWN, p.mate)
    x_send(2, OWN, 0, LOWER, OTHER, p.cross)
    x_send(3, OWN, 0, LOWER, OWN, p.mate)
    x_send(4, OWN, 0, UPPER, OTHER, p.cross)
    x_send(5, OWN, 0, every, OWN, p.sibling)
    weights(0, 2)
    weights(1, 2)
    weights(0, 3)

    for copy in later:
        copy.wait()
    net.arrived(0, meta.at[OTHER], p.opposite)
    up[...] = jnp.zeros_like(up)

    def choose(slot):
        chosen = meta[slot, 0:1, 0:1]

        def add(a, sums):
            weight = (chosen == a).astype(F32)
            return tuple(
                total + table[a].astype(F32) * weight
                for total, table in zip(sums, (qds, vds, qus, vus))
            )

        zeros = tuple(jnp.zeros((RANK, width), F32) for width in (D, D, 512, 256))
        q_rows, v_rows, q_up, v_up = lax.fori_loop(0, ADAPTERS, add, zeros)
        down[slot, :RANK, :] = q_rows.astype(BF16)
        down[slot, RANK:, :] = v_rows.astype(BF16)
        for g in range(2):
            c0 = g * GROUP
            up[slot, :RANK, c0 : c0 + 256] = q_up[:, g * 256 : g * 256 + 256].astype(BF16)
            up[slot, RANK:, c0 + 384 : c0 + 512] = v_up[:, g * 128 : g * 128 + 128].astype(BF16)

    choose(OWN)

    def x_arrived(index, slot, flip, rows, device, core=None):
        net.arrived(index, x_block(slot, flip, p.core if core is None else core, rows), device)

    x_arrived(1, OWN, 1, UPPER, p.mate)
    x_send(6, OWN, 1, UPPER, OTHER, p.cross)
    x_send(7, OWN, 1, UPPER, OWN, p.sibling)
    x_arrived(2, OTHER, 1, LOWER, p.cross)
    x_send(8, OTHER, 1, LOWER, OTHER, p.mate)
    x_send(9, OTHER, 1, LOWER, OTHER, p.sibling)
    for g in range(2):
        net.send(
            20 + g,
            cols_of(g_ref, (1 - p.dp) * 512 + g * 256, 256),
            cots.at[OTHER, :, g * 256 : g * 256 + 256],
            p.opposite,
        )
    choose(OTHER)
    weights(0, 4)
    weights(1, 3)
    x_arrived(3, OWN, 1, LOWER, p.mate)
    x_send(10, OWN, 1, LOWER, OWN, p.sibling)
    x_arrived(4, OTHER, 1, UPPER, p.cross)
    x_send(11, OTHER, 1, UPPER, OTHER, p.sibling)
    away = 1 - p.core
    x_arrived(5, OWN, 0, every, p.sibling, away)
    x_arrived(7, OWN, 1, UPPER, p.sibling, away)
    x_arrived(10, OWN, 1, LOWER, p.sibling, away)

    def rank_space(slot):
        low[slot] = dot(xs[slot], down[slot], ((1,), (1,))).astype(BF16)

    def project(slot, g):
        @pl.loop(0, 2)
        def _(n):
            window = pl.ds(pl.multiple_of(g * GROUP + n * 256, 256), 256)
            base = dot(xs[slot], ws[:, :, window].reshape(D, 256), ((1,), (0,)))
            extra = dot(low[slot], up[slot, :, window], ((1,), (0,)))
            qkv[slot, :, window] = (base + adapter_scale * extra).astype(BF16)

    def attend(slot, g, rows):
        c0 = g * GROUP
        start, step, span = rows.start, HALF, rows.stop
        length = meta[slot, 1:2, 0:1]
        k = qkv[slot, :span, c0 + 256 : c0 + 384]
        v = qkv[slot, :span, c0 + 384 : c0 + 512]
        key_at = lax.broadcasted_iota(jnp.int32, (span, step), 0)
        row_at = lax.broadcasted_iota(jnp.int32, (span, step), 1) + start
        allowed = (key_at <= row_at) & (key_at < length)
        used = lax.broadcasted_iota(jnp.int32, (step, HD), 0) + start < length
        dk, dv = 0.0, 0.0
        for h in range(2):
            q = qkv[slot, rows, c0 + h * HD : c0 + (h + 1) * HD]
            cot = cots[slot, rows, g * 256 + h * HD : g * 256 + (h + 1) * HD]
            cot = jnp.where(used, cot, jnp.zeros_like(cot))
            raw = dot(k, q, ((1,), (1,)))
            turned = jnp.tanh(raw * (score_scale / soft_cap))
            weight = jnp.where(allowed, jnp.exp(soft_cap * turned), 0.0)
            probs = weight * (1.0 / jnp.sum(weight, axis=0, keepdims=True))
            probs_b = probs.astype(BF16)
            dprob = dot(v, cot, ((1,), (1,)))
            row_total = jnp.sum(probs * dprob, axis=0, keepdims=True)
            dscore = (
                probs * (dprob - row_total) * ((1.0 - turned * turned) * score_scale)
            ).astype(BF16)
            dq = dot(k, dscore, ((0,), (0,)))
            grads[slot, rows, c0 + h * HD : c0 + (h + 1) * HD] = dq.T.astype(BF16)
            dk = dk + dot(dscore, q, ((1,), (0,)))
            dv = dv + dot(probs_b, cot, ((1,), (0,)))
        if rows.stop == TOKENS:
            dk_acc[...] = dk[:HALF]
            dv_acc[...] = dv[:HALF]
            dk, dv = dk[HALF:], dv[HALF:]
        else:
            dk, dv = dk + dk_acc[...], dv + dv_acc[...]
        grads[slot, rows, c0 + 256 : c0 + 384] = dk.astype(BF16)
        grads[slot, rows, c0 + 384 : c0 + 512] = dv.astype(BF16)

    rank_space(OWN)
    weights(0, 5)
    project(OWN, 0)
    attend(OWN, 0, UPPER)
    attend(OWN, 0, LOWER)

    x_arrived(6, OTHER, 0, UPPER, p.cross)
    x_send(12, OTHER, 0, UPPER, OTHER, p.sibling)
    x_arrived(8, OTHER, 0, LOWER, p.mate)
    x_send(13, OTHER, 0, LOWER, OTHER, p.sibling)
    weights(1, 4)
    x_arrived(9, OTHER, 1, LOWER, p.sibling, away)
    x_arrived(11, OTHER, 1, UPPER, p.sibling, away)
    x_arrived(12, OTHER, 0, UPPER, p.sibling, away)
    x_arrived(13, OTHER, 0, LOWER, p.sibling, away)
    rank_space(OTHER)
    project(OTHER, 0)
    net.arrived(20, cots.at[OTHER, :, 0:256], p.opposite)
    attend(OTHER, 0, UPPER)
    attend(OTHER, 0, LOWER)
    weights(1, 5)
    project(OTHER, 1)
    net.arrived(21, cots.at[OTHER, :, 256:512], p.opposite)
    attend(OTHER, 1, UPPER)

    slots = {TO_OPPOSITE: (OTHER, 0), TO_CROSS: (OTHER, 1), TO_MATE: (OWN, 1), TO_OWN: (OWN, 0)}
    chunk = 384

    def products(block, core, rows):
        slot, flip = slots[block]
        part = p.part(flip, core)
        for c in range(0, COLS, chunk):
            cols = slice(c, c + chunk)
            yield cols, dot(grads[slot, rows], ws[part, cols], ((1,), (1,)))

    def sib_index(block, rows):
        return 64 + 2 * block + (rows is UPPER)

    def for_sibling(block, rows):
        for cols, value in products(block, away, rows):
            sib_out[block, rows, cols] = value.astype(BF16)
        net.send(
            sib_index(block, rows), sib_out.at[block, rows], sib_in.at[block, rows], p.sibling
        )

    def both_cores(block, rows):
        net.arrived(sib_index(block, rows), sib_in.at[block, rows], p.sibling)
        for cols, value in products(block, p.core, rows):
            yield cols, value + sib_in[block, rows, cols].astype(F32)

    def to_ring(block, rows):
        for cols, value in both_cores(block, rows):
            ring_out[block, rows, cols] = value.astype(BF16)

    for_sibling(TO_OPPOSITE, UPPER)
    for_sibling(TO_CROSS, UPPER)
    to_ring(TO_OPPOSITE, UPPER)
    net.send(22, ring_out.at[TO_OPPOSITE, UPPER], relay_in.at[0], p.cross)
    to_ring(TO_CROSS, UPPER)
    net.send(24, ring_out.at[TO_CROSS, UPPER], ring_in.at[0, UPPER], p.cross)
    attend(OTHER, 1, LOWER)
    for_sibling(TO_OPPOSITE, LOWER)
    for_sibling(TO_CROSS, LOWER)
    to_ring(TO_OPPOSITE, LOWER)
    net.send(23, ring_out.at[TO_OPPOSITE, LOWER], relay_in.at[1], p.mate)
    project(OWN, 1)
    attend(OWN, 1, UPPER)
    attend(OWN, 1, LOWER)

    for slot in (OWN, OTHER):
        low_mine[slot] = adapter_scale * dot(up[slot], grads[slot], ((1,), (1,)))
    net.send(14, low_mine, low_sib, p.sibling)
    my_up = up_terms.at[p.dp, p.y, p.z]
    for slot in (OWN, OTHER):
        seq = p.dp if slot == OWN else 1 - p.dp
        terms = (adapter_scale * dot(low[slot], grads[slot], ((0,), (0,)))).astype(BF16)
        for g in range(2):
            c0 = g * GROUP
            at = pl.multiple_of(seq * 512 + g * 256, 256)
            my_up[:, pl.ds(at, 256)] = terms[:RANK, c0 : c0 + 256]
            at = pl.multiple_of(1024 + seq * 256 + g * 128, 128)
            my_up[:, pl.ds(at, 128)] = terms[RANK:, c0 + 384 : c0 + 512]
    my_up[:, 1536:UP] = jnp.broadcast_to(meta[OWN, 0:1, :], (RANK, 128)).astype(F32).astype(BF16)
    net.send(15, my_up, my_up, p.opposite)
    for_sibling(TO_MATE, LOWER)
    for_sibling(TO_MATE, UPPER)
    net.arrived(14, low_sib, p.sibling)
    low_chip[...] = low_mine[...] + low_sib[...]
    net.send(16, low_chip.at[OWN], low_in.at[0], p.mate)
    net.send(17, low_chip.at[OTHER], low_in.at[1], p.cross)
    net.send(18, low_chip.at[OTHER], low_in.at[2], p.opposite)
    to_ring(TO_MATE, LOWER)
    net.send(26, ring_out.at[TO_MATE, LOWER], ring_in.at[1, LOWER], p.mate)

    def terms_gather(base, ref, cuts):
        everything = slice(None)

        def view(y, z, window):
            return ref.at[
                :, everything if y is None else y, everything if z is None else z, :, window
            ]

        return [
            TorusGather(
                net, base + 8 * n, p, n == 0, view,
                slice(cuts[2 * n], cuts[2 * n + 2]),
                slice(cuts[2 * n], cuts[2 * n + 1]),
                slice(cuts[2 * n + 1], cuts[2 * n + 2]),
            )
            for n in range(2)
        ]

    up_gather = terms_gather(72, up_terms, (0, 384, 768, 1152, UP))
    down_gather = terms_gather(88, down_terms, (0, 640, 1152, 1792, DOWN))

    def stage(gather, n):
        for one in gather:
            one.stage(n)

    net.arrived(15, up_terms.at[1 - p.dp, p.y, p.z], p.opposite)
    stage(up_gather, 1)
    total = low_chip[OWN]
    for n, device in enumerate((p.mate, p.cross, p.opposite)):
        net.arrived(16 + n, low_in.at[n], device)
        total = total + low_in[n]
    low_grad = total.astype(BF16)
    my_cols = pl.ds(pl.multiple_of(p.t * COLS, COLS), COLS)
    my_x = x_block(OWN, 0, p.core)
    my_down = down_terms.at[p.dp, p.y, p.z]
    value = dot(low_grad, my_x[...], ((1,), (0,))).astype(BF16)
    my_down[:, 0:COLS] = value[:RANK]
    my_down[:, COLS:DOWN] = value[RANK:]
    net.send(19, my_down, my_down, p.opposite)

    for_sibling(TO_OWN, LOWER)
    for_sibling(TO_OWN, UPPER)
    to_ring(TO_MATE, UPPER)
    net.arrived(22, relay_in.at[0], p.cross)
    ring_out[TO_MATE, UPPER] = (
        ring_out[TO_MATE, UPPER].astype(F32) + relay_in[0].astype(F32)
    ).astype(BF16)
    net.send(27, ring_out.at[TO_MATE, UPPER], ring_in.at[1, UPPER], p.mate)
    stage(up_gather, 2)
    to_ring(TO_CROSS, LOWER)
    net.arrived(23, relay_in.at[1], p.mate)
    ring_out[TO_CROSS, LOWER] = (
        ring_out[TO_CROSS, LOWER].astype(F32) + relay_in[1].astype(F32)
    ).astype(BF16)
    net.send(25, ring_out.at[TO_CROSS, LOWER], ring_in.at[0, LOWER], p.cross)
    stage(up_gather, 3)
    net.arrived(19, down_terms.at[1 - p.dp, p.y, p.z], p.opposite)
    stage(down_gather, 1)
    for rows in (LOWER, UPPER):
        for cols, value in both_cores(TO_OWN, rows):
            kept[rows, cols] = value
    kept[...] += dot(low_grad, down[OWN, :, my_cols], ((0,), (0,)))
    stage(up_gather, 4)
    stage(down_gather, 2)
    stage(down_gather, 3)
    stage(up_gather, 5)
    save_up = local(up_terms, up_out)
    stage(down_gather, 4)
    for index, n, rows, device in (
        (24, 0, UPPER, p.cross), (26, 1, LOWER, p.mate),
        (27, 1, UPPER, p.mate), (25, 0, LOWER, p.cross),
    ):
        net.arrived(index, ring_in.at[n, rows], device)
    grad_out[...] = (
        kept[...] + ring_in[0].astype(F32) + ring_in[1].astype(F32)
    ).astype(BF16)
    stage(down_gather, 5)
    save_down = local(down_terms, down_out)
    net.finish()
    save_up.wait()
    save_down.wait()


def block_call(lengths, ids, *arrays):
    hbm = pl.BlockSpec(memory_space=pl.ANY)
    vmem = pl.BlockSpec(memory_space=pltpu.VMEM)
    smem = pl.BlockSpec(memory_space=pltpu.SMEM)
    bf16 = lambda *shape: pltpu.VMEM(shape, BF16)
    f32 = lambda *shape: pltpu.VMEM(shape, F32)
    return pl.pallas_call(
        block_kernel,
        name="attention_block",
        out_shape=(
            jax.ShapeDtypeStruct((TOKENS, COLS), BF16),
            jax.ShapeDtypeStruct((2, SIDE, SIDE, RANK, UP), BF16),
            jax.ShapeDtypeStruct((2, SIDE, SIDE, RANK, DOWN), BF16),
        ),
        in_specs=[smem, smem] + [hbm] * 9,
        out_specs=(vmem, hbm, hbm),
        scratch_shapes=[
            bf16(2, TOKENS, D),
            bf16(SIDE, COLS, 2 * GROUP),
            bf16(ADAPTERS, RANK, D),
            bf16(ADAPTERS, RANK, D),
            bf16(ADAPTERS, RANK, 512),
            bf16(ADAPTERS, RANK, 256),
            bf16(2, 2 * RANK, D),
            bf16(2, 2 * RANK, 2 * GROUP),
            bf16(2, TOKENS, 2 * RANK),
            bf16(2, TOKENS, 2 * GROUP),
            bf16(2, TOKENS, 2 * GROUP),
            bf16(2, TOKENS, 512),
            pltpu.VMEM((2, 8, 128), jnp.int32),
            f32(HALF, HD),
            f32(HALF, HD),
            bf16(4, TOKENS, COLS),
            bf16(4, TOKENS, COLS),
            bf16(3, TOKENS, COLS),
            bf16(2, HALF, COLS),
            bf16(2, TOKENS, COLS),
            f32(TOKENS, COLS),
            f32(2, 2 * RANK, TOKENS),
            f32(2, 2 * RANK, TOKENS),
            f32(2, 2 * RANK, TOKENS),
            f32(3, 2 * RANK, TOKENS),
            bf16(2, SIDE, SIDE, RANK, UP),
            bf16(2, SIDE, SIDE, RANK, DOWN),
            pltpu.SemaphoreType.DMA((104,)),
            pltpu.SemaphoreType.DMA((104,)),
            pltpu.SemaphoreType.DMA((14,)),
        ],
        compiler_params=pltpu.CompilerParams(
            collective_id=0, has_side_effects=True, vmem_limit_bytes=VMEM_BYTES
        ),
    )(lengths, ids, *arrays)


def table_kernel(grad_ref, up_ref, down_ref, grad_out, qa_out, qb_out, va_out, vb_out, sem):
    copy = pltpu.make_async_copy(grad_ref, grad_out, sem)
    copy.start()
    rows = 16 * RANK
    at = lax.broadcasted_iota(jnp.int32, (rows, rows), 0)
    to = lax.broadcasted_iota(jnp.int32, (rows, rows), 1)
    owners = []
    for s in range(2):
        chosen = up_ref[s, :, 1536:1537].astype(F32)
        own = ((to // RANK).astype(F32) == chosen) & (at % RANK == to % RANK)
        owners.append(own.astype(F32).T.astype(BF16))

    def total(first, second):
        return dot(owners[0], first, ((1,), (0,))) + dot(owners[1], second, ((1,), (0,)))

    for c in range(0, COLS, 384):
        cols = slice(c, c + 384)
        qa_out[:, cols] = total(down_ref[0, :, cols], down_ref[1, :, cols])
        cols = slice(COLS + c, COLS + c + 384)
        va_out[:, c : c + 384] = total(down_ref[0, :, cols], down_ref[1, :, cols])
    for d in range(2):
        for out, start, width in ((qb_out, 0, 512), (vb_out, 1024, 256)):
            out[:, d * width : (d + 1) * width] = total(
                up_ref[d, :, start : start + width],
                up_ref[d, :, start + width : start + 2 * width],
            )
    copy.wait()


def table_call(grad, up_terms, down_terms):
    hbm = pl.BlockSpec(memory_space=pl.ANY)
    vmem = pl.BlockSpec(memory_space=pltpu.VMEM)
    rows = 16 * RANK
    table = lambda width: jax.ShapeDtypeStruct((rows, width), F32)
    return pl.pallas_call(
        table_kernel,
        name="tables",
        out_shape=(
            jax.ShapeDtypeStruct((TOKENS, COLS), BF16),
            table(COLS), table(1024), table(COLS), table(512),
        ),
        in_specs=[hbm, vmem, vmem],
        out_specs=(hbm, vmem, vmem, vmem, vmem),
        scratch_shapes=[pltpu.SemaphoreType.DMA],
        compiler_params=pltpu.CompilerParams(vmem_limit_bytes=VMEM_BYTES),
    )(grad, up_terms.reshape(2, rows, UP), down_terms.reshape(2, rows, DOWN))


def shards(
    x_in, lengths, adapter_ids, attn_grad, w_query, w_key, w_value,
    query_down, query_up, value_down, value_up,
):
    grad, up_terms, down_terms = block_call(
        lengths, adapter_ids, x_in[0], attn_grad[0], w_query, w_key, w_value,
        query_down, value_down, query_up, value_up,
    )
    grad, qa, qb, va, vb = table_call(grad, up_terms, down_terms)
    tables = (table.reshape(ADAPTERS, RANK, -1) for table in (qa, qb, va, vb))
    return (grad[None], *tables)


def solution(mesh):
    placed = (
        P(("dp", "fsdp"), None, "tensor"),
        P(("dp", "fsdp")),
        P(("dp", "fsdp")),
        P(("dp", "fsdp"), None, "tensor"),
        P("fsdp", "tensor"),
        P("fsdp", "tensor"),
        P("fsdp", "tensor"),
        P(),
        P(None, None, "tensor"),
        P(),
        P(None, None, "tensor"),
    )
    return jax.shard_map(
        shards,
        mesh=mesh,
        in_specs=placed,
        out_specs=(
            P(("dp", "fsdp"), None, "tensor"),
            P(None, None, "tensor"),
            P(None, None, "tensor"),
            P(None, None, "tensor"),
            P(None, None, "tensor"),
        ),
        check_vma=False,
    )
```

```python
import math

import jax
import jax.numpy as jnp
from jax import lax
from jax.experimental import pallas as pl
from jax.experimental.pallas import tpu as pltpu
from jax.sharding import PartitionSpec as P

D = 4608
HD = 128
TOKENS = 512
RANK = 16
ADAPTERS = 16
SIDE = 4
ROWS = 288
GROUP = 512
COLS = 1152
HALF = 256
UP = 1536 + 128
DOWN = 2 * COLS

soft_cap = 50.0
adapter_scale = 2.0
score_scale = 1.0 / 12.0

MESH = pl.DeviceIdType.MESH
F32 = jnp.float32
BF16 = jnp.bfloat16
VMEM_BYTES = 60 * 1024 * 1024


def dot(a, b, dims):
    return lax.dot_general(a, b, (dims, ((), ())), preferred_element_type=F32)


class Place:
    def __init__(self):
        self.dp = lax.axis_index("dp")
        self.f = lax.axis_index("fsdp")
        self.t = lax.axis_index("tensor")
        self.y, self.z = self.f // SIDE, self.f % SIDE
        self.core = self.t % 2
        self.x_lo = self.t // 2
        x = self.dp * 2 + self.x_lo
        to_mate = 1 - 2 * self.x_lo
        at = lambda n, core: ((n % SIDE) // 2, self.f, (n % 2) * 2 + core)
        self.mate = at(x + to_mate + SIDE, self.core)
        self.cross = at(x - to_mate + SIDE, self.core)
        self.opposite = at(x + 2, self.core)
        self.sibling = at(x, 1 - self.core)

    def part(self, flip, core):
        return ((self.x_lo + flip) % 2) * 2 + core

    def ring_y(self, n):
        return (self.dp, ((self.y + n) % SIDE) * SIDE + self.z, self.t)

    def ring_z(self, n):
        return (self.dp, self.y * SIDE + (self.z + n) % SIDE, self.t)


class Net:
    def __init__(self, send_sems, recv_sems):
        self.send_sems, self.recv_sems = send_sems, recv_sems
        self.started = []

    def send(self, index, src, dst, device):
        copy = pltpu.make_async_remote_copy(
            src_ref=src,
            dst_ref=dst,
            send_sem=self.send_sems.at[index],
            recv_sem=self.recv_sems.at[index],
            device_id=device,
            device_id_type=MESH,
        )
        copy.start()
        self.started.append(copy)

    def arrived(self, index, region, device):
        pltpu.make_async_remote_copy(
            src_ref=region,
            dst_ref=region,
            send_sem=self.send_sems.at[index],
            recv_sem=self.recv_sems.at[index],
            device_id=device,
            device_id_type=MESH,
        ).wait_recv()

    def finish(self):
        for copy in self.started:
            copy.wait_send()


def enter(peers):
    barrier = pltpu.get_barrier_semaphore()
    for peer in peers:
        pl.semaphore_signal(barrier, inc=1, device_id=peer, device_id_type=MESH)
    pl.semaphore_wait(barrier, len(peers))


class TorusGather:
    def __init__(self, net, base, place, y_first, view, whole, low, high):
        self.net, self.base = net, base
        self.whole, self.low, self.high = whole, low, high
        p = place
        if y_first:
            self.one, self.two = p.ring_y, p.ring_z
            self.block = lambda n, w: view((p.y + n) % SIDE, p.z, w)
            self.line = lambda n, w: view(None, (p.z + n) % SIDE, w)
        else:
            self.one, self.two = p.ring_z, p.ring_y
            self.block = lambda n, w: view(p.y, (p.z + n) % SIDE, w)
            self.line = lambda n, w: view((p.y + n) % SIDE, None, w)

    def fan(self, base, region, ring):
        own = region(0, self.whole)
        self.net.send(base, own, own, ring(1))
        self.net.send(base + 1, own, own, ring(-1))

    def forward(self, base, region, ring):
        self.net.arrived(base, region(-1, self.whole), ring(-1))
        part = region(-1, self.low)
        self.net.send(base + 2, part, part, ring(1))
        self.net.arrived(base + 1, region(1, self.whole), ring(1))
        part = region(1, self.high)
        self.net.send(base + 3, part, part, ring(-1))

    def close(self, base, region, ring):
        self.net.arrived(base + 2, region(2, self.low), ring(-1))
        self.net.arrived(base + 3, region(2, self.high), ring(1))

    def stage(self, n):
        if n == 1:
            self.fan(self.base, self.block, self.one)
        elif n == 2:
            self.forward(self.base, self.block, self.one)
        elif n == 3:
            self.close(self.base, self.block, self.one)
            self.fan(self.base + 4, self.line, self.two)
        elif n == 4:
            self.forward(self.base + 4, self.line, self.two)
        else:
            self.close(self.base + 4, self.line, self.two)


OWN, OTHER = 0, 1
TO_OPPOSITE, TO_CROSS, TO_MATE, TO_OWN = 0, 1, 2, 3
UPPER, LOWER = slice(HALF, TOKENS), slice(0, HALF)


def block_kernel(
    length_ref, id_ref, x_ref, g_ref, wq_ref, wk_ref, wv_ref, qd_ref, vd_ref, qu_ref, vu_ref,
    grad_out, up_out, down_out,
    xs, ws, qds, vds, qus, vus, down, up, low, qkv, grads, cots, meta, dk_acc, dv_acc,
    sib_out, sib_in, ring_out, relay_in, ring_in, kept,
    low_mine, low_sib, low_chip, low_in, up_terms, down_terms,
    send_sems, recv_sems, local_sems,
):
    p = Place()
    net = Net(send_sems, recv_sems)
    copies = iter(range(32))

    def local(src, dst):
        copy = pltpu.make_async_copy(src, dst, local_sems.at[next(copies)])
        copy.start()
        return copy

    def cols_of(ref, start, width):
        return ref.at[..., pl.ds(pl.multiple_of(start, width), width)]

    def x_block(slot, flip, core, rows=slice(None)):
        column = pl.multiple_of(p.part(flip, core) * COLS, COLS)
        return xs.at[slot, rows, pl.ds(column, COLS)]

    my_rows = pl.ds(pl.multiple_of(p.z * ROWS, 32), ROWS)
    first = []
    for g in range(2):
        for ref, at, width in ((wq_ref, 0, 256), (wk_ref, 256, 128), (wv_ref, 384, 128)):
            c = g * GROUP + at
            first.append(
                local(
                    cols_of(ref, p.dp * 2 * width + g * width, width),
                    ws.at[p.y, my_rows, c : c + width],
                )
            )
    first.append(local(x_ref, x_block(OWN, 0, p.core)))
    later = [
        local(qd_ref, qds),
        local(vd_ref, vds),
        local(cols_of(qu_ref, p.dp * 512, 512), qus),
        local(cols_of(vu_ref, p.dp * 256, 256), vus),
        local(cols_of(g_ref, p.dp * 512, 512), cots.at[OWN]),
    ]
    line = lax.broadcasted_iota(jnp.int32, (8, 128), 0)
    meta[OWN] = jnp.where(line == 0, id_ref[0], length_ref[0])

    enter([
        p.mate, p.cross, p.opposite, p.sibling,
        p.ring_y(1), p.ring_y(-1), p.ring_z(1), p.ring_z(-1),
    ])

    net.send(0, meta.at[OWN], meta.at[OTHER], p.opposite)
    for copy in first:
        copy.wait()

    def weight_view(y, z, window):
        rows = slice(None) if z is None else pl.ds(pl.multiple_of(z * ROWS, 32), ROWS)
        return ws.at[slice(None) if y is None else y, rows, window]

    rounds = []
    for g in range(2):
        pair = []
        for h in range(2):
            c = g * GROUP + h * 256
            pair.append(
                TorusGather(
                    net, 32 + 8 * (2 * g + h), p, h == 0, weight_view,
                    slice(c, c + 256), slice(c, c + 128), slice(c + 128, c + 256),
                )
            )
        rounds.append(pair)

    def weights(g, stage):
        for one in rounds[g]:
            one.stage(stage)

    def x_send(index, slot, flip, rows, to_slot, device):
        net.send(
            index, x_block(slot, flip, p.core, rows), x_block(to_slot, flip, p.core, rows), device
        )

    weights(0, 1)
    weights(1, 1)
    every = slice(None)
    x_send(1, OWN, 0, UPPER, OWN, p.mate)
    x_send(2, OWN, 0, LOWER, OTHER, p.cross)
    x_send(3, OWN, 0, LOWER, OWN, p.mate)
    x_send(4, OWN, 0, UPPER, OTHER, p.cross)
    x_send(5, OWN, 0, every, OWN, p.sibling)
    weights(0, 2)
    weights(1, 2)
    weights(0, 3)

    for copy in later:
        copy.wait()
    net.arrived(0, meta.at[OTHER], p.opposite)
    up[...] = jnp.zeros_like(up)

    def choose(slot):
        chosen = meta[slot, 0:1, 0:1]

        def add(a, sums):
            weight = (chosen == a).astype(F32)
            return tuple(
                total + table[a].astype(F32) * weight
                for total, table in zip(sums, (qds, vds, qus, vus))
            )

        zeros = tuple(jnp.zeros((RANK, width), F32) for width in (D, D, 512, 256))
        q_rows, v_rows, q_up, v_up = lax.fori_loop(0, ADAPTERS, add, zeros)
        down[slot, :RANK, :] = q_rows.astype(BF16)
        down[slot, RANK:, :] = v_rows.astype(BF16)
        for g in range(2):
            c0 = g * GROUP
            up[slot, :RANK, c0 : c0 + 256] = q_up[:, g * 256 : g * 256 + 256].astype(BF16)
            up[slot, RANK:, c0 + 384 : c0 + 512] = v_up[:, g * 128 : g * 128 + 128].astype(BF16)

    choose(OWN)

    def x_arrived(index, slot, flip, rows, device, core=None):
        net.arrived(index, x_block(slot, flip, p.core if core is None else core, rows), device)

    x_arrived(1, OWN, 1, UPPER, p.mate)
    x_send(6, OWN, 1, UPPER, OTHER, p.cross)
    x_send(7, OWN, 1, UPPER, OWN, p.sibling)
    x_arrived(2, OTHER, 1, LOWER, p.cross)
    x_send(8, OTHER, 1, LOWER, OTHER, p.mate)
    x_send(9, OTHER, 1, LOWER, OTHER, p.sibling)
    for g in range(2):
        net.send(
            20 + g,
            cols_of(g_ref, (1 - p.dp) * 512 + g * 256, 256),
            cots.at[OTHER, :, g * 256 : g * 256 + 256],
            p.opposite,
        )
    choose(OTHER)
    weights(0, 4)
    weights(1, 3)
    x_arrived(3, OWN, 1, LOWER, p.mate)
    x_send(10, OWN, 1, LOWER, OWN, p.sibling)
    x_arrived(4, OTHER, 1, UPPER, p.cross)
    x_send(11, OTHER, 1, UPPER, OTHER, p.sibling)
    away = 1 - p.core
    x_arrived(5, OWN, 0, every, p.sibling, away)
    x_arrived(7, OWN, 1, UPPER, p.sibling, away)
    x_arrived(10, OWN, 1, LOWER, p.sibling, away)

    def rank_space(slot):
        low[slot] = dot(xs[slot], down[slot], ((1,), (1,))).astype(BF16)

    def project(slot, g):
        @pl.loop(0, 2)
        def _(n):
            window = pl.ds(pl.multiple_of(g * GROUP + n * 256, 256), 256)
            base = dot(xs[slot], ws[:, :, window].reshape(D, 256), ((1,), (0,)))
            extra = dot(low[slot], up[slot, :, window], ((1,), (0,)))
            qkv[slot, :, window] = (base + adapter_scale * extra).astype(BF16)

    def attend(slot, g, rows):
        c0 = g * GROUP
        start, step, span = rows.start, HALF, rows.stop
        length = meta[slot, 1:2, 0:1]
        k = qkv[slot, :span, c0 + 256 : c0 + 384]
        v = qkv[slot, :span, c0 + 384 : c0 + 512]
        key_at = lax.broadcasted_iota(jnp.int32, (span, step), 0)
        row_at = lax.broadcasted_iota(jnp.int32, (span, step), 1) + start
        allowed = (key_at <= row_at) & (key_at < length)
        used = lax.broadcasted_iota(jnp.int32, (step, HD), 0) + start < length
        dk, dv = 0.0, 0.0
        for h in range(2):
            q = qkv[slot, rows, c0 + h * HD : c0 + (h + 1) * HD]
            cot = cots[slot, rows, g * 256 + h * HD : g * 256 + (h + 1) * HD]
            cot = jnp.where(used, cot, jnp.zeros_like(cot))
            raw = dot(k, q, ((1,), (1,)))
            turned = jnp.tanh(raw * (score_scale / soft_cap))
            weight = jnp.where(allowed, jnp.exp(soft_cap * turned), 0.0)
            probs = weight * (1.0 / jnp.sum(weight, axis=0, keepdims=True))
            probs_b = probs.astype(BF16)
            dprob = dot(v, cot, ((1,), (1,)))
            row_total = jnp.sum(probs * dprob, axis=0, keepdims=True)
            dscore = (
                probs * (dprob - row_total) * ((1.0 - turned * turned) * score_scale)
            ).astype(BF16)
            dq = dot(k, dscore, ((0,), (0,)))
            grads[slot, rows, c0 + h * HD : c0 + (h + 1) * HD] = dq.T.astype(BF16)
            dk = dk + dot(dscore, q, ((1,), (0,)))
            dv = dv + dot(probs_b, cot, ((1,), (0,)))
        if rows.stop == TOKENS:
            dk_acc[...] = dk[:HALF]
            dv_acc[...] = dv[:HALF]
            dk, dv = dk[HALF:], dv[HALF:]
        else:
            dk, dv = dk + dk_acc[...], dv + dv_acc[...]
        grads[slot, rows, c0 + 256 : c0 + 384] = dk.astype(BF16)
        grads[slot, rows, c0 + 384 : c0 + 512] = dv.astype(BF16)

    rank_space(OWN)
    weights(0, 5)
    project(OWN, 0)
    attend(OWN, 0, UPPER)
    attend(OWN, 0, LOWER)

    x_arrived(6, OTHER, 0, UPPER, p.cross)
    x_send(12, OTHER, 0, UPPER, OTHER, p.sibling)
    x_arrived(8, OTHER, 0, LOWER, p.mate)
    x_send(13, OTHER, 0, LOWER, OTHER, p.sibling)
    weights(1, 4)
    x_arrived(9, OTHER, 1, LOWER, p.sibling, away)
    x_arrived(11, OTHER, 1, UPPER, p.sibling, away)
    x_arrived(12, OTHER, 0, UPPER, p.sibling, away)
    x_arrived(13, OTHER, 0, LOWER, p.sibling, away)
    rank_space(OTHER)
    project(OTHER, 0)
    net.arrived(20, cots.at[OTHER, :, 0:256], p.opposite)
    attend(OTHER, 0, UPPER)
    attend(OTHER, 0, LOWER)
    weights(1, 5)
    project(OTHER, 1)
    net.arrived(21, cots.at[OTHER, :, 256:512], p.opposite)
    attend(OTHER, 1, UPPER)

    slots = {TO_OPPOSITE: (OTHER, 0), TO_CROSS: (OTHER, 1), TO_MATE: (OWN, 1), TO_OWN: (OWN, 0)}
    chunk = 384

    def products(block, core, rows):
        slot, flip = slots[block]
        part = p.part(flip, core)
        for c in range(0, COLS, chunk):
            cols = slice(c, c + chunk)
            yield cols, dot(grads[slot, rows], ws[part, cols], ((1,), (1,)))

    def sib_index(block, rows):
        return 64 + 2 * block + (rows is UPPER)

    def for_sibling(block, rows):
        for cols, value in products(block, away, rows):
            sib_out[block, rows, cols] = value.astype(BF16)
        net.send(
            sib_index(block, rows), sib_out.at[block, rows], sib_in.at[block, rows], p.sibling
        )

    def both_cores(block, rows):
        net.arrived(sib_index(block, rows), sib_in.at[block, rows], p.sibling)
        for cols, value in products(block, p.core, rows):
            yield cols, value + sib_in[block, rows, cols].astype(F32)

    def to_ring(block, rows):
        for cols, value in both_cores(block, rows):
            ring_out[block, rows, cols] = value.astype(BF16)

    for_sibling(TO_OPPOSITE, UPPER)
    for_sibling(TO_CROSS, UPPER)
    to_ring(TO_OPPOSITE, UPPER)
    net.send(22, ring_out.at[TO_OPPOSITE, UPPER], relay_in.at[0], p.cross)
    attend(OTHER, 1, LOWER)
    for_sibling(TO_OPPOSITE, LOWER)
    for_sibling(TO_CROSS, LOWER)
    to_ring(TO_OPPOSITE, LOWER)
    net.send(23, ring_out.at[TO_OPPOSITE, LOWER], relay_in.at[1], p.mate)
    project(OWN, 1)
    attend(OWN, 1, UPPER)
    attend(OWN, 1, LOWER)

    for slot in (OWN, OTHER):
        low_mine[slot] = adapter_scale * dot(up[slot], grads[slot], ((1,), (1,)))
    net.send(14, low_mine, low_sib, p.sibling)
    my_up = up_terms.at[p.dp, p.y, p.z]
    for slot in (OWN, OTHER):
        seq = p.dp if slot == OWN else 1 - p.dp
        terms = (adapter_scale * dot(low[slot], grads[slot], ((0,), (0,)))).astype(BF16)
        for g in range(2):
            c0 = g * GROUP
            at = pl.multiple_of(seq * 512 + g * 256, 256)
            my_up[:, pl.ds(at, 256)] = terms[:RANK, c0 : c0 + 256]
            at = pl.multiple_of(1024 + seq * 256 + g * 128, 128)
            my_up[:, pl.ds(at, 128)] = terms[RANK:, c0 + 384 : c0 + 512]
    my_up[:, 1536:UP] = jnp.broadcast_to(meta[OWN, 0:1, :], (RANK, 128)).astype(F32).astype(BF16)
    net.send(15, my_up, my_up, p.opposite)
    to_ring(TO_CROSS, UPPER)
    net.arrived(14, low_sib, p.sibling)
    low_chip[...] = (low_mine[...] + low_sib[...]).astype(BF16)
    net.send(16, low_chip, low_in.at[0], p.mate)
    net.send(17, low_chip, low_in.at[1], p.cross)
    net.send(18, low_chip, low_in.at[2], p.opposite)
    net.send(24, ring_out.at[TO_CROSS, UPPER], ring_in.at[0, UPPER], p.cross)
    for_sibling(TO_MATE, LOWER)
    for_sibling(TO_MATE, UPPER)
    to_ring(TO_MATE, LOWER)
    net.send(26, ring_out.at[TO_MATE, LOWER], ring_in.at[1, LOWER], p.mate)

    def terms_gather(base, ref, cuts):
        everything = slice(None)

        def view(y, z, window):
            return ref.at[
                :, everything if y is None else y, everything if z is None else z, :, window
            ]

        return [
            TorusGather(
                net, base + 8 * n, p, n == 0, view,
                slice(cuts[2 * n], cuts[2 * n + 2]),
                slice(cuts[2 * n], cuts[2 * n + 1]),
                slice(cuts[2 * n + 1], cuts[2 * n + 2]),
            )
            for n in range(2)
        ]

    up_gather = terms_gather(72, up_terms, (0, 384, 768, 1152, UP))
    down_gather = terms_gather(88, down_terms, (0, 640, 1152, 1792, DOWN))

    def stage(gather, n):
        for one in gather:
            one.stage(n)

    net.arrived(15, up_terms.at[1 - p.dp, p.y, p.z], p.opposite)
    stage(up_gather, 1)
    for_sibling(TO_OWN, LOWER)
    for_sibling(TO_OWN, UPPER)
    to_ring(TO_MATE, UPPER)
    net.arrived(22, relay_in.at[0], p.cross)
    ring_out[TO_MATE, UPPER] = (
        ring_out[TO_MATE, UPPER].astype(F32) + relay_in[0].astype(F32)
    ).astype(BF16)
    net.send(27, ring_out.at[TO_MATE, UPPER], ring_in.at[1, UPPER], p.mate)
    stage(up_gather, 2)

    for n, device in enumerate((p.mate, p.cross, p.opposite)):
        net.arrived(16 + n, low_in.at[n], device)
    my_cols = pl.ds(pl.multiple_of(p.t * COLS, COLS), COLS)
    low_grads = []
    for slot in (OWN, OTHER):
        pair = low_chip[slot].astype(F32) + low_in[0, slot].astype(F32)
        far = low_in[1, 1 - slot].astype(F32) + low_in[2, 1 - slot].astype(F32)
        low_grads.append((pair + far).astype(BF16))
        value = dot(low_grads[slot], xs[slot, :, my_cols], ((1,), (0,))).astype(BF16)
        my_down = down_terms.at[p.dp if slot == OWN else 1 - p.dp, p.y, p.z]
        my_down[:, 0:COLS] = value[:RANK]
        my_down[:, COLS:DOWN] = value[RANK:]
    stage(down_gather, 1)
    to_ring(TO_CROSS, LOWER)
    net.arrived(23, relay_in.at[1], p.mate)
    ring_out[TO_CROSS, LOWER] = (
        ring_out[TO_CROSS, LOWER].astype(F32) + relay_in[1].astype(F32)
    ).astype(BF16)
    net.send(25, ring_out.at[TO_CROSS, LOWER], ring_in.at[0, LOWER], p.cross)
    stage(up_gather, 3)
    stage(down_gather, 2)
    for rows in (LOWER, UPPER):
        for cols, value in both_cores(TO_OWN, rows):
            kept[rows, cols] = value
    kept[...] += dot(low_grads[OWN], down[OWN, :, my_cols], ((0,), (0,)))
    stage(down_gather, 3)
    stage(up_gather, 4)
    stage(up_gather, 5)
    save_up = local(up_terms, up_out)
    stage(down_gather, 4)
    stage(down_gather, 5)
    save_down = local(down_terms, down_out)
    for index, n, rows, device in (
        (24, 0, UPPER, p.cross), (26, 1, LOWER, p.mate),
        (27, 1, UPPER, p.mate), (25, 0, LOWER, p.cross),
    ):
        net.arrived(index, ring_in.at[n, rows], device)
    grad_out[...] = (
        kept[...] + ring_in[0].astype(F32) + ring_in[1].astype(F32)
    ).astype(BF16)
    net.finish()
    save_up.wait()
    save_down.wait()


def block_call(lengths, ids, *arrays):
    hbm = pl.BlockSpec(memory_space=pl.ANY)
    vmem = pl.BlockSpec(memory_space=pltpu.VMEM)
    smem = pl.BlockSpec(memory_space=pltpu.SMEM)
    bf16 = lambda *shape: pltpu.VMEM(shape, BF16)
    f32 = lambda *shape: pltpu.VMEM(shape, F32)
    return pl.pallas_call(
        block_kernel,
        name="attention_block",
        out_shape=(
            jax.ShapeDtypeStruct((TOKENS, COLS), BF16),
            jax.ShapeDtypeStruct((2, SIDE, SIDE, RANK, UP), BF16),
            jax.ShapeDtypeStruct((2, SIDE, SIDE, RANK, DOWN), BF16),
        ),
        in_specs=[smem, smem] + [hbm] * 9,
        out_specs=(vmem, hbm, hbm),
        scratch_shapes=[
            bf16(2, TOKENS, D),
            bf16(SIDE, COLS, 2 * GROUP),
            bf16(ADAPTERS, RANK, D),
            bf16(ADAPTERS, RANK, D),
            bf16(ADAPTERS, RANK, 512),
            bf16(ADAPTERS, RANK, 256),
            bf16(2, 2 * RANK, D),
            bf16(2, 2 * RANK, 2 * GROUP),
            bf16(2, TOKENS, 2 * RANK),
            bf16(2, TOKENS, 2 * GROUP),
            bf16(2, TOKENS, 2 * GROUP),
            bf16(2, TOKENS, 512),
            pltpu.VMEM((2, 8, 128), jnp.int32),
            f32(HALF, HD),
            f32(HALF, HD),
            bf16(4, TOKENS, COLS),
            bf16(4, TOKENS, COLS),
            bf16(3, TOKENS, COLS),
            bf16(2, HALF, COLS),
            bf16(2, TOKENS, COLS),
            f32(TOKENS, COLS),
            f32(2, 2 * RANK, TOKENS),
            f32(2, 2 * RANK, TOKENS),
            bf16(2, 2 * RANK, TOKENS),
            bf16(3, 2, 2 * RANK, TOKENS),
            bf16(2, SIDE, SIDE, RANK, UP),
            bf16(2, SIDE, SIDE, RANK, DOWN),
            pltpu.SemaphoreType.DMA((104,)),
            pltpu.SemaphoreType.DMA((104,)),
            pltpu.SemaphoreType.DMA((14,)),
        ],
        compiler_params=pltpu.CompilerParams(
            collective_id=0, has_side_effects=True, vmem_limit_bytes=VMEM_BYTES
        ),
    )(lengths, ids, *arrays)


def table_kernel(grad_ref, up_ref, down_ref, grad_out, qa_out, qb_out, va_out, vb_out):
    grad_out[...] = grad_ref[...]
    rows = 16 * RANK
    at = lax.broadcasted_iota(jnp.int32, (rows, rows), 0)
    to = lax.broadcasted_iota(jnp.int32, (rows, rows), 1)
    owners = []
    for s in range(2):
        chosen = up_ref[s, :, 1536:1537].astype(F32)
        own = ((to // RANK).astype(F32) == chosen) & (at % RANK == to % RANK)
        owners.append(own.astype(F32).T.astype(BF16))

    def total(first, second):
        return dot(owners[0], first, ((1,), (0,))) + dot(owners[1], second, ((1,), (0,)))

    for c in range(0, COLS, 384):
        cols = slice(c, c + 384)
        qa_out[:, cols] = total(down_ref[0, :, cols], down_ref[1, :, cols])
        cols = slice(COLS + c, COLS + c + 384)
        va_out[:, c : c + 384] = total(down_ref[0, :, cols], down_ref[1, :, cols])
    for d in range(2):
        for out, start, width in ((qb_out, 0, 512), (vb_out, 1024, 256)):
            out[:, d * width : (d + 1) * width] = total(
                up_ref[d, :, start : start + width],
                up_ref[d, :, start + width : start + 2 * width],
            )


def table_call(grad, up_terms, down_terms):
    vmem = pl.BlockSpec(memory_space=pltpu.VMEM)
    rows = 16 * RANK
    table = lambda width: jax.ShapeDtypeStruct((rows, width), F32)
    return pl.pallas_call(
        table_kernel,
        name="tables",
        out_shape=(
            jax.ShapeDtypeStruct((TOKENS, COLS), BF16),
            table(COLS), table(1024), table(COLS), table(512),
        ),
        in_specs=[vmem, vmem, vmem],
        out_specs=(vmem, vmem, vmem, vmem, vmem),
        compiler_params=pltpu.CompilerParams(vmem_limit_bytes=VMEM_BYTES),
    )(grad, up_terms.reshape(2, rows, UP), down_terms.reshape(2, rows, DOWN))


def shards(
    x_in, lengths, adapter_ids, attn_grad, w_query, w_key, w_value,
    query_down, query_up, value_down, value_up,
):
    grad, up_terms, down_terms = block_call(
        lengths, adapter_ids, x_in[0], attn_grad[0], w_query, w_key, w_value,
        query_down, value_down, query_up, value_up,
    )
    grad, qa, qb, va, vb = table_call(grad, up_terms, down_terms)
    tables = (table.reshape(ADAPTERS, RANK, -1) for table in (qa, qb, va, vb))
    return (grad[None], *tables)


def solution(mesh):
    placed = (
        P(("dp", "fsdp"), None, "tensor"),
        P(("dp", "fsdp")),
        P(("dp", "fsdp")),
        P(("dp", "fsdp"), None, "tensor"),
        P("fsdp", "tensor"),
        P("fsdp", "tensor"),
        P("fsdp", "tensor"),
        P(),
        P(None, None, "tensor"),
        P(),
        P(None, None, "tensor"),
    )
    return jax.shard_map(
        shards,
        mesh=mesh,
        in_specs=placed,
        out_specs=(
            P(("dp", "fsdp"), None, "tensor"),
            P(None, None, "tensor"),
            P(None, None, "tensor"),
            P(None, None, "tensor"),
            P(None, None, "tensor"),
        ),
        check_vma=False,
    )
```

```python
import math

import jax
import jax.numpy as jnp
from jax import lax
from jax.experimental import pallas as pl
from jax.experimental.pallas import tpu as pltpu
from jax.sharding import PartitionSpec as P

D = 4608
HD = 128
TOKENS = 512
RANK = 16
ADAPTERS = 16
SIDE = 4
ROWS = 288
GROUP = 512
COLS = 1152
HALF = 256
UP = 1536 + 128
DOWN = 2 * COLS

soft_cap = 50.0
adapter_scale = 2.0
score_scale = 1.0 / 12.0

MESH = pl.DeviceIdType.MESH
F32 = jnp.float32
BF16 = jnp.bfloat16
VMEM_BYTES = 60 * 1024 * 1024


def dot(a, b, dims):
    return lax.dot_general(a, b, (dims, ((), ())), preferred_element_type=F32)


class Place:
    def __init__(self):
        self.dp = lax.axis_index("dp")
        self.f = lax.axis_index("fsdp")
        self.t = lax.axis_index("tensor")
        self.y, self.z = self.f // SIDE, self.f % SIDE
        self.core = self.t % 2
        self.x_lo = self.t // 2
        x = self.dp * 2 + self.x_lo
        to_mate = 1 - 2 * self.x_lo
        at = lambda n, core: ((n % SIDE) // 2, self.f, (n % 2) * 2 + core)
        self.mate = at(x + to_mate + SIDE, self.core)
        self.cross = at(x - to_mate + SIDE, self.core)
        self.opposite = at(x + 2, self.core)
        self.sibling = at(x, 1 - self.core)

    def part(self, flip, core):
        return ((self.x_lo + flip) % 2) * 2 + core

    def ring_y(self, n):
        return (self.dp, ((self.y + n) % SIDE) * SIDE + self.z, self.t)

    def ring_z(self, n):
        return (self.dp, self.y * SIDE + (self.z + n) % SIDE, self.t)


class Net:
    def __init__(self, send_sems, recv_sems):
        self.send_sems, self.recv_sems = send_sems, recv_sems
        self.started = []

    def send(self, index, src, dst, device):
        copy = pltpu.make_async_remote_copy(
            src_ref=src,
            dst_ref=dst,
            send_sem=self.send_sems.at[index],
            recv_sem=self.recv_sems.at[index],
            device_id=device,
            device_id_type=MESH,
        )
        copy.start()
        self.started.append(copy)

    def arrived(self, index, region, device):
        pltpu.make_async_remote_copy(
            src_ref=region,
            dst_ref=region,
            send_sem=self.send_sems.at[index],
            recv_sem=self.recv_sems.at[index],
            device_id=device,
            device_id_type=MESH,
        ).wait_recv()

    def finish(self):
        for copy in self.started:
            copy.wait_send()


def enter(peers):
    barrier = pltpu.get_barrier_semaphore()
    for peer in peers:
        pl.semaphore_signal(barrier, inc=1, device_id=peer, device_id_type=MESH)
    pl.semaphore_wait(barrier, len(peers))


class TorusGather:
    def __init__(self, net, base, place, y_first, view, low, high):
        self.net, self.base = net, base
        self.low, self.high = low, high
        p = place
        if y_first:
            self.one, self.two = p.ring_y, p.ring_z
            self.block = lambda n, w: view((p.y + n) % SIDE, p.z, w)
            self.line = lambda n, w: view(None, (p.z + n) % SIDE, w)
        else:
            self.one, self.two = p.ring_z, p.ring_y
            self.block = lambda n, w: view(p.y, (p.z + n) % SIDE, w)
            self.line = lambda n, w: view((p.y + n) % SIDE, None, w)

    def fan(self, base, region, ring):
        low, high = region(0, self.low), region(0, self.high)
        self.net.send(base, low, low, ring(1))
        self.net.send(base + 1, high, high, ring(-1))
        self.net.send(base + 2, high, high, ring(1))
        self.net.send(base + 3, low, low, ring(-1))

    def forward(self, base, region, ring):
        part = region(-1, self.low)
        self.net.arrived(base, part, ring(-1))
        self.net.send(base + 4, part, part, ring(1))
        part = region(1, self.high)
        self.net.arrived(base + 1, part, ring(1))
        self.net.send(base + 5, part, part, ring(-1))

    def close(self, base, region, ring):
        self.net.arrived(base + 2, region(-1, self.high), ring(-1))
        self.net.arrived(base + 3, region(1, self.low), ring(1))
        self.net.arrived(base + 4, region(2, self.low), ring(-1))
        self.net.arrived(base + 5, region(2, self.high), ring(1))

    def stage(self, n):
        if n == 1:
            self.fan(self.base, self.block, self.one)
        elif n == 2:
            self.forward(self.base, self.block, self.one)
        elif n == 3:
            self.close(self.base, self.block, self.one)
            self.fan(self.base + 6, self.line, self.two)
        elif n == 4:
            self.forward(self.base + 6, self.line, self.two)
        else:
            self.close(self.base + 6, self.line, self.two)


OWN, OTHER = 0, 1
TO_OPPOSITE, TO_CROSS, TO_MATE, TO_OWN = 0, 1, 2, 3
UPPER, LOWER = slice(HALF, TOKENS), slice(0, HALF)


def block_kernel(
    length_ref, id_ref, x_ref, g_ref, wq_ref, wk_ref, wv_ref, qd_ref, vd_ref, qu_ref, vu_ref,
    grad_out, up_out, down_out,
    xs, ws, qds, vds, qus, vus, down, up, low, qkv, grads, cots, meta, dk_acc, dv_acc,
    sib_out, sib_in, ring_out, relay_in, ring_in, kept,
    low_mine, low_sib, low_chip, low_in, low_grad, up_terms, down_terms, low_acc, proj_acc,
    send_sems, recv_sems, local_sems,
):
    p = Place()
    net = Net(send_sems, recv_sems)
    copies = iter(range(32))

    def local(src, dst):
        copy = pltpu.make_async_copy(src, dst, local_sems.at[next(copies)])
        copy.start()
        return copy

    def cols_of(ref, start, width):
        return ref.at[..., pl.ds(pl.multiple_of(start, width), width)]

    def x_block(slot, flip, core, rows=slice(None)):
        column = pl.multiple_of(p.part(flip, core) * COLS, COLS)
        return xs.at[slot, rows, pl.ds(column, COLS)]

    my_rows = pl.ds(pl.multiple_of(p.z * ROWS, 32), ROWS)
    first = [local(x_ref, x_block(OWN, 0, p.core))]
    for g in range(2):
        for ref, at, width in ((wq_ref, 0, 256), (wk_ref, 256, 128), (wv_ref, 384, 128)):
            c = g * GROUP + at
            first.append(
                local(
                    cols_of(ref, p.dp * 2 * width + g * width, width),
                    ws.at[p.y, my_rows, c : c + width],
                )
            )
    later = [
        local(qd_ref, qds),
        local(vd_ref, vds),
        local(cols_of(qu_ref, p.dp * 512, 512), qus),
        local(cols_of(vu_ref, p.dp * 256, 256), vus),
        local(cols_of(g_ref, p.dp * 512, 512), cots.at[OWN]),
    ]
    line = lax.broadcasted_iota(jnp.int32, (8, 128), 0)
    meta[OWN] = jnp.where(line == 0, id_ref[0], length_ref[0])

    enter([
        p.mate, p.cross, p.opposite, p.sibling,
        p.ring_y(1), p.ring_y(-1), p.ring_z(1), p.ring_z(-1),
    ])

    net.send(0, meta.at[OWN], meta.at[OTHER], p.opposite)

    def weight_view(y, z, window):
        rows = slice(None) if z is None else pl.ds(pl.multiple_of(z * ROWS, 32), ROWS)
        return ws.at[slice(None) if y is None else y, rows, window]

    rounds = []
    for g in range(2):
        pair = []
        for h in range(2):
            c = g * GROUP + h * 256
            pair.append(
                TorusGather(
                    net, 40 + 12 * (2 * g + h), p, h == 0, weight_view,
                    slice(c, c + 128), slice(c + 128, c + 256),
                )
            )
        rounds.append(pair)

    def weights(g, stage):
        for one in rounds[g]:
            one.stage(stage)

    def x_send(index, slot, flip, rows, to_slot, device):
        net.send(
            index, x_block(slot, flip, p.core, rows), x_block(to_slot, flip, p.core, rows), device
        )

    for copy in first:
        copy.wait()
    weights(0, 1)
    weights(1, 1)
    every = slice(None)
    for index, rows, to_slot, device in (
        (1, UPPER, OWN, p.mate), (2, LOWER, OTHER, p.cross),
        (3, LOWER, OWN, p.mate), (4, UPPER, OTHER, p.cross), (5, every, OWN, p.sibling),
    ):
        net.send(index, x_block(OWN, 0, p.core, rows), x_block(to_slot, 0, p.core, rows), device)

    def send_cotangent(index, rows):
        net.send(
            index,
            g_ref.at[rows, pl.ds(pl.multiple_of((1 - p.dp) * 512, 512), 512)],
            cots.at[OTHER, rows],
            p.opposite,
        )

    weights(0, 2)
    weights(1, 2)
    weights(0, 3)

    for copy in later:
        copy.wait()
    net.arrived(0, meta.at[OTHER], p.opposite)
    up[...] = jnp.zeros_like(up)

    def choose(slot):
        chosen = meta[slot, 0:1, 0:1]

        def add(a, sums):
            weight = (chosen == a).astype(F32)
            return tuple(
                total + table[a].astype(F32) * weight
                for total, table in zip(sums, (qds, vds, qus, vus))
            )

        zeros = tuple(jnp.zeros((RANK, width), F32) for width in (D, D, 512, 256))
        q_rows, v_rows, q_up, v_up = lax.fori_loop(0, ADAPTERS, add, zeros)
        down[slot, :RANK, :] = q_rows.astype(BF16)
        down[slot, RANK:, :] = v_rows.astype(BF16)
        for g in range(2):
            c0 = g * GROUP
            up[slot, :RANK, c0 : c0 + 256] = q_up[:, g * 256 : g * 256 + 256].astype(BF16)
            up[slot, RANK:, c0 + 384 : c0 + 512] = v_up[:, g * 128 : g * 128 + 128].astype(BF16)

    choose(OWN)

    def x_arrived(index, slot, flip, rows, device, core=None):
        net.arrived(index, x_block(slot, flip, p.core if core is None else core, rows), device)

    x_arrived(1, OWN, 1, UPPER, p.mate)
    x_send(6, OWN, 1, UPPER, OTHER, p.cross)
    x_send(7, OWN, 1, UPPER, OWN, p.sibling)
    x_arrived(2, OTHER, 1, LOWER, p.cross)
    x_send(8, OTHER, 1, LOWER, OTHER, p.mate)
    x_send(9, OTHER, 1, LOWER, OTHER, p.sibling)
    send_cotangent(20, UPPER)
    send_cotangent(21, LOWER)
    choose(OTHER)
    weights(0, 4)
    weights(1, 3)
    x_arrived(3, OWN, 1, LOWER, p.mate)
    x_send(10, OWN, 1, LOWER, OWN, p.sibling)
    x_arrived(4, OTHER, 1, UPPER, p.cross)
    x_send(11, OTHER, 1, UPPER, OTHER, p.sibling)
    away = 1 - p.core
    x_arrived(5, OWN, 0, every, p.sibling, away)
    x_arrived(7, OWN, 1, UPPER, p.sibling, away)
    x_arrived(10, OWN, 1, LOWER, p.sibling, away)

    def rank_space(slot):
        low[slot] = dot(xs[slot], down[slot], ((1,), (1,))).astype(BF16)

    def project(slot, g):
        @pl.loop(0, 2)
        def _(n):
            window = pl.ds(pl.multiple_of(g * GROUP + n * 256, 256), 256)
            base = dot(xs[slot], ws[:, :, window].reshape(D, 256), ((1,), (0,)))
            extra = dot(low[slot], up[slot, :, window], ((1,), (0,)))
            qkv[slot, :, window] = (base + adapter_scale * extra).astype(BF16)

    def attend(slot, g, rows):
        c0 = g * GROUP
        start, step, span = rows.start, HALF, rows.stop
        length = meta[slot, 1:2, 0:1]
        k = qkv[slot, :span, c0 + 256 : c0 + 384]
        v = qkv[slot, :span, c0 + 384 : c0 + 512]
        key_at = lax.broadcasted_iota(jnp.int32, (span, step), 0)
        row_at = lax.broadcasted_iota(jnp.int32, (span, step), 1) + start
        allowed = (key_at <= row_at) & (key_at < length)
        used = lax.broadcasted_iota(jnp.int32, (step, HD), 0) + start < length
        dk, dv = 0.0, 0.0
        for h in range(2):
            q = qkv[slot, rows, c0 + h * HD : c0 + (h + 1) * HD]
            cot = cots[slot, rows, g * 256 + h * HD : g * 256 + (h + 1) * HD]
            cot = jnp.where(used, cot, jnp.zeros_like(cot))
            raw = dot(k, q, ((1,), (1,)))
            turned = jnp.tanh(raw * (score_scale / soft_cap))
            weight = jnp.where(allowed, jnp.exp(soft_cap * turned), 0.0)
            probs = weight * (1.0 / jnp.sum(weight, axis=0, keepdims=True))
            probs_b = probs.astype(BF16)
            dprob = dot(v, cot, ((1,), (1,)))
            row_total = jnp.sum(probs * dprob, axis=0, keepdims=True)
            dscore = (
                probs * (dprob - row_total) * ((1.0 - turned * turned) * score_scale)
            ).astype(BF16)
            dq = dot(k, dscore, ((0,), (0,)))
            grads[slot, rows, c0 + h * HD : c0 + (h + 1) * HD] = dq.T.astype(BF16)
            dk = dk + dot(dscore, q, ((1,), (0,)))
            dv = dv + dot(probs_b, cot, ((1,), (0,)))
        if rows.stop == TOKENS:
            dk_acc[g] = dk[:HALF]
            dv_acc[g] = dv[:HALF]
            dk, dv = dk[HALF:], dv[HALF:]
        else:
            dk, dv = dk + dk_acc[g], dv + dv_acc[g]
        grads[slot, rows, c0 + 256 : c0 + 384] = dk.astype(BF16)
        grads[slot, rows, c0 + 384 : c0 + 512] = dv.astype(BF16)

    rank_space(OWN)
    weights(0, 5)
    project(OWN, 0)
    attend(OWN, 0, UPPER)
    attend(OWN, 0, LOWER)

    x_arrived(9, OTHER, 1, LOWER, p.sibling, away)
    x_arrived(11, OTHER, 1, UPPER, p.sibling, away)
    wide = 2 * COLS

    def half_of(flip):
        lo = (p.x_lo + flip) % 2
        return pl.ds(pl.multiple_of(lo * wide, wide), wide), pl.ds(lo * 2, 2)

    columns, parts = half_of(1)
    low_acc[...] = dot(xs[OTHER, :, columns], down[OTHER, :, columns], ((1,), (1,)))

    @pl.loop(0, 2)
    def _(n):
        window = pl.ds(pl.multiple_of(n * 256, 256), 256)
        proj_acc[:, window] = dot(
            xs[OTHER, :, columns], ws[parts, :, window].reshape(wide, 256), ((1,), (0,))
        )

    x_arrived(6, OTHER, 0, UPPER, p.cross)
    x_send(12, OTHER, 0, UPPER, OTHER, p.sibling)
    x_arrived(8, OTHER, 0, LOWER, p.mate)
    x_send(13, OTHER, 0, LOWER, OTHER, p.sibling)
    weights(1, 4)
    x_arrived(12, OTHER, 0, UPPER, p.sibling, away)
    x_arrived(13, OTHER, 0, LOWER, p.sibling, away)
    columns, parts = half_of(0)
    rest = dot(xs[OTHER, :, columns], down[OTHER, :, columns], ((1,), (1,)))
    low[OTHER] = (low_acc[...] + rest).astype(BF16)

    @pl.loop(0, 2)
    def _(n):
        window = pl.ds(pl.multiple_of(n * 256, 256), 256)
        base = dot(xs[OTHER, :, columns], ws[parts, :, window].reshape(wide, 256), ((1,), (0,)))
        extra = dot(low[OTHER], up[OTHER, :, window], ((1,), (0,)))
        qkv[OTHER, :, window] = (
            base + proj_acc[:, window] + adapter_scale * extra
        ).astype(BF16)

    net.arrived(20, cots.at[OTHER, UPPER], p.opposite)
    attend(OTHER, 0, UPPER)
    weights(1, 5)
    project(OTHER, 1)
    attend(OTHER, 1, UPPER)

    slots = {TO_OPPOSITE: (OTHER, 0), TO_CROSS: (OTHER, 1), TO_MATE: (OWN, 1), TO_OWN: (OWN, 0)}

    def piece(rows, side):
        cut = 640 if rows is UPPER else 512
        return slice(0, cut) if side == 0 else slice(cut, COLS)

    def product(block, core, rows, cols):
        slot, flip = slots[block]
        return dot(grads[slot, rows], ws[p.part(flip, core), cols], ((1,), (1,)))

    def sib_index(block, rows, side):
        return 136 + 4 * block + 2 * (rows is UPPER) + side

    def for_sibling(block, rows):
        for side in range(2):
            cols = piece(rows, side)
            sib_out[block, rows, cols] = product(block, away, rows, cols).astype(BF16)
            net.send(
                sib_index(block, rows, side),
                sib_out.at[block, rows, cols], sib_in.at[block, rows, cols], p.sibling,
            )

    def both_cores(block, rows, side):
        cols = piece(rows, side)
        value = product(block, p.core, rows, cols)
        net.arrived(sib_index(block, rows, side), sib_in.at[block, rows, cols], p.sibling)
        return value + sib_in[block, rows, cols].astype(F32)

    def ring_index(block, rows, side):
        return 20 + 4 * block + 2 * (rows is UPPER) + side if block else (
            32 + 2 * (rows is UPPER) + side
        )

    def to_ring(block, rows, side, relay=None):
        cols = piece(rows, side)
        value = both_cores(block, rows, side)
        if relay is not None:
            net.arrived(
                ring_index(TO_OPPOSITE, rows, side), relay_in.at[rows, cols],
                (p.cross, p.mate)[side],
            )
            value = value + relay_in[rows, cols].astype(F32)
        ring_out[block, rows, cols] = value.astype(BF16)

    def ship(block, rows, side):
        cols = piece(rows, side)
        if block == TO_OPPOSITE:
            target, device = relay_in.at[rows, cols], (p.cross, p.mate)[side]
        elif block == TO_CROSS:
            target, device = ring_in.at[0, rows, cols], p.cross
        else:
            target, device = ring_in.at[1, rows, cols], p.mate
        net.send(ring_index(block, rows, side), ring_out.at[block, rows, cols], target, device)

    for_sibling(TO_OPPOSITE, UPPER)
    net.arrived(21, cots.at[OTHER, LOWER], p.opposite)
    attend(OTHER, 0, LOWER)
    for side in range(2):
        to_ring(TO_OPPOSITE, UPPER, side)
        ship(TO_OPPOSITE, UPPER, side)
    attend(OTHER, 1, LOWER)
    for_sibling(TO_OPPOSITE, LOWER)
    for_sibling(TO_CROSS, UPPER)
    for side in range(2):
        to_ring(TO_OPPOSITE, LOWER, side)
        ship(TO_OPPOSITE, LOWER, side)
    project(OWN, 1)
    attend(OWN, 1, UPPER)
    attend(OWN, 1, LOWER)

    for slot in (OWN, OTHER):
        low_mine[slot] = adapter_scale * dot(up[slot], grads[slot], ((1,), (1,)))
    net.send(14, low_mine, low_sib, p.sibling)
    my_up = up_terms.at[p.dp, p.y, p.z]
    for slot in (OWN, OTHER):
        seq = p.dp if slot == OWN else 1 - p.dp
        terms = (adapter_scale * dot(low[slot], grads[slot], ((0,), (0,)))).astype(BF16)
        for g in range(2):
            c0 = g * GROUP
            at = pl.multiple_of(seq * 512 + g * 256, 256)
            my_up[:, pl.ds(at, 256)] = terms[:RANK, c0 : c0 + 256]
            at = pl.multiple_of(1024 + seq * 256 + g * 128, 128)
            my_up[:, pl.ds(at, 128)] = terms[RANK:, c0 + 384 : c0 + 512]
    my_up[:, 1536:UP] = jnp.broadcast_to(meta[OWN, 0:1, :], (RANK, 128)).astype(F32).astype(BF16)
    net.send(15, my_up, my_up, p.opposite)
    to_ring(TO_CROSS, UPPER, 0)
    for_sibling(TO_MATE, UPPER)
    net.arrived(14, low_sib, p.sibling)
    low_chip[...] = (low_mine[...] + low_sib[...]).astype(BF16)
    my_rank = pl.ds(pl.multiple_of(p.core * RANK, RANK), RANK)
    for n, device in enumerate((p.mate, p.cross, p.opposite)):
        net.send(16 + n, low_chip.at[:, my_rank], low_in.at[n], device)
    ship(TO_CROSS, UPPER, 0)
    to_ring(TO_MATE, UPPER, 1)
    ship(TO_MATE, UPPER, 1)
    for_sibling(TO_CROSS, LOWER)
    for_sibling(TO_MATE, LOWER)
    to_ring(TO_CROSS, LOWER, 0)
    ship(TO_CROSS, LOWER, 0)
    to_ring(TO_MATE, LOWER, 1)
    ship(TO_MATE, LOWER, 1)

    def terms_gather(base, ref, cuts):
        everything = slice(None)

        def view(y, z, window):
            return ref.at[
                :, everything if y is None else y, everything if z is None else z, :, window
            ]

        return [
            TorusGather(
                net, base + 12 * n, p, n == 0, view,
                slice(cuts[2 * n], cuts[2 * n + 1]),
                slice(cuts[2 * n + 1], cuts[2 * n + 2]),
            )
            for n in range(2)
        ]

    up_gather = terms_gather(88, up_terms, (0, 384, 768, 1152, UP))
    down_gather = terms_gather(112, down_terms, (0, 640, 1152, 1792, DOWN))

    def stage(gather, n):
        for one in gather:
            one.stage(n)

    net.arrived(15, up_terms.at[1 - p.dp, p.y, p.z], p.opposite)
    stage(up_gather, 1)

    for n, device in enumerate((p.mate, p.cross, p.opposite)):
        net.arrived(16 + n, low_in.at[n], device)
    for slot in (OWN, OTHER):
        pair = low_chip[slot, my_rank].astype(F32) + low_in[0, slot].astype(F32)
        far = low_in[1, 1 - slot].astype(F32) + low_in[2, 1 - slot].astype(F32)
        low_grad[slot, my_rank] = (pair + far).astype(BF16)
    swapped = low_grad.at[:, my_rank]
    net.send(19, swapped, swapped, p.sibling)
    stage(up_gather, 2)
    to_ring(TO_MATE, UPPER, 0, True)
    ship(TO_MATE, UPPER, 0)
    other_rank = pl.ds(pl.multiple_of(away * RANK, RANK), RANK)
    net.arrived(19, low_grad.at[:, other_rank], p.sibling)
    my_cols = pl.ds(pl.multiple_of(p.t * COLS, COLS), COLS)
    for slot in (OWN, OTHER):
        value = dot(low_grad[slot], xs[slot, :, my_cols], ((1,), (0,))).astype(BF16)
        my_down = down_terms.at[p.dp if slot == OWN else 1 - p.dp, p.y, p.z]
        my_down[:, 0:COLS] = value[:RANK]
        my_down[:, COLS:DOWN] = value[RANK:]
    stage(down_gather, 1)
    stage(up_gather, 3)
    to_ring(TO_CROSS, UPPER, 1, True)
    ship(TO_CROSS, UPPER, 1)
    stage(down_gather, 2)
    to_ring(TO_MATE, LOWER, 0, True)
    ship(TO_MATE, LOWER, 0)
    to_ring(TO_CROSS, LOWER, 1, True)
    ship(TO_CROSS, LOWER, 1)
    stage(down_gather, 3)
    for_sibling(TO_OWN, UPPER)
    for_sibling(TO_OWN, LOWER)

    def keep(rows):
        for side in range(2):
            cols = piece(rows, side)
            columns = pl.ds(pl.multiple_of(p.t * COLS + cols.start, 128), cols.stop - cols.start)
            extra = dot(low_grad[OWN, :, rows], down[OWN, :, columns], ((0,), (0,)))
            kept[rows, cols] = both_cores(TO_OWN, rows, side) + extra

    keep(UPPER)
    stage(up_gather, 4)
    keep(LOWER)
    stage(up_gather, 5)
    save_up = local(up_terms, up_out)
    stage(down_gather, 4)

    def finish_rows(rows):
        for side in range(2):
            cols = piece(rows, side)
            net.arrived(ring_index(TO_CROSS, rows, side), ring_in.at[0, rows, cols], p.cross)
            net.arrived(ring_index(TO_MATE, rows, side), ring_in.at[1, rows, cols], p.mate)
        grad_out[rows] = (
            kept[rows] + ring_in[0, rows].astype(F32) + ring_in[1, rows].astype(F32)
        ).astype(BF16)

    finish_rows(UPPER)
    stage(down_gather, 5)
    save_down = local(down_terms, down_out)
    finish_rows(LOWER)
    net.finish()
    save_up.wait()
    save_down.wait()


def block_call(lengths, ids, *arrays):
    hbm = pl.BlockSpec(memory_space=pl.ANY)
    vmem = pl.BlockSpec(memory_space=pltpu.VMEM)
    smem = pl.BlockSpec(memory_space=pltpu.SMEM)
    bf16 = lambda *shape: pltpu.VMEM(shape, BF16)
    f32 = lambda *shape: pltpu.VMEM(shape, F32)
    return pl.pallas_call(
        block_kernel,
        name="attention_block",
        out_shape=(
            jax.ShapeDtypeStruct((TOKENS, COLS), BF16),
            jax.ShapeDtypeStruct((2, SIDE, SIDE, RANK, UP), BF16),
            jax.ShapeDtypeStruct((2, SIDE, SIDE, RANK, DOWN), BF16),
        ),
        in_specs=[smem, smem] + [hbm] * 9,
        out_specs=(vmem, hbm, hbm),
        scratch_shapes=[
            bf16(2, TOKENS, D),
            bf16(SIDE, COLS, 2 * GROUP),
            bf16(ADAPTERS, RANK, D),
            bf16(ADAPTERS, RANK, D),
            bf16(ADAPTERS, RANK, 512),
            bf16(ADAPTERS, RANK, 256),
            bf16(2, 2 * RANK, D),
            bf16(2, 2 * RANK, 2 * GROUP),
            bf16(2, TOKENS, 2 * RANK),
            bf16(2, TOKENS, 2 * GROUP),
            bf16(2, TOKENS, 2 * GROUP),
            bf16(2, TOKENS, 512),
            pltpu.VMEM((2, 8, 128), jnp.int32),
            f32(2, HALF, HD),
            f32(2, HALF, HD),
            bf16(4, TOKENS, COLS),
            bf16(4, TOKENS, COLS),
            bf16(3, TOKENS, COLS),
            bf16(TOKENS, COLS),
            bf16(2, TOKENS, COLS),
            f32(TOKENS, COLS),
            f32(2, 2 * RANK, TOKENS),
            f32(2, 2 * RANK, TOKENS),
            bf16(2, 2 * RANK, TOKENS),
            bf16(3, 2, RANK, TOKENS),
            bf16(2, 2 * RANK, TOKENS),
            bf16(2, SIDE, SIDE, RANK, UP),
            bf16(2, SIDE, SIDE, RANK, DOWN),
            f32(TOKENS, 2 * RANK),
            f32(TOKENS, GROUP),
            pltpu.SemaphoreType.DMA((152,)),
            pltpu.SemaphoreType.DMA((152,)),
            pltpu.SemaphoreType.DMA((14,)),
        ],
        compiler_params=pltpu.CompilerParams(
            collective_id=0, has_side_effects=True, vmem_limit_bytes=VMEM_BYTES
        ),
    )(lengths, ids, *arrays)


def table_kernel(
    grad_ref, up_ref, down_ref, grad_out, qa_out, qb_out, va_out, vb_out,
    grad, up, down, qa, qb, va, vb, in_sems, out_sems,
):
    width = 384
    loads = [pltpu.make_async_copy(up_ref.at[s], up.at[s], in_sems.at[s]) for s in range(2)]
    for n in range(2 * COLS // width):
        cols = slice(n * width, (n + 1) * width)
        loads.append(
            pltpu.make_async_copy(down_ref.at[:, :, cols], down.at[:, :, cols], in_sems.at[2 + n])
        )
    loads.append(pltpu.make_async_copy(grad_ref, grad, in_sems.at[2 + 2 * COLS // width]))
    for load in loads:
        load.start()
    stores = []

    def store(src, dst):
        copy = pltpu.make_async_copy(src, dst, out_sems.at[len(stores)])
        copy.start()
        stores.append(copy)

    rows = 16 * RANK
    at = lax.broadcasted_iota(jnp.int32, (rows, rows), 0)
    to = lax.broadcasted_iota(jnp.int32, (rows, rows), 1)
    same = at % RANK == to % RANK
    table = (to // RANK).astype(F32)
    owners = []
    for s in range(2):
        loads[s].wait()
        chosen = up[s, :, 1536:1537].astype(F32)
        own = (table == chosen) & same
        owners.append(own.astype(F32).T.astype(BF16))

    def total(first, second):
        return dot(owners[0], first, ((1,), (0,))) + dot(owners[1], second, ((1,), (0,)))

    for d in range(2):
        for out, to_ref, start, size in ((qb, qb_out, 0, 512), (vb, vb_out, 1024, 256)):
            cols = slice(d * size, (d + 1) * size)
            out[:, cols] = total(
                up[d, :, start : start + size], up[d, :, start + size : start + 2 * size]
            )
            store(out.at[:, cols], to_ref.at[:, cols])
    for n in range(2 * COLS // width):
        loads[2 + n].wait()
        out, to_ref, c = (qa, qa_out, 0) if n < COLS // width else (va, va_out, COLS)
        cols = slice(n * width, (n + 1) * width)
        here = slice(n * width - c, (n + 1) * width - c)
        out[:, here] = total(down[0, :, cols], down[1, :, cols])
        store(out.at[:, here], to_ref.at[:, here])
    loads[-1].wait()
    store(grad, grad_out)
    for copy in stores:
        copy.wait()


def table_call(grad, up_terms, down_terms):
    hbm = pl.BlockSpec(memory_space=pl.ANY)
    rows = 16 * RANK
    widths = (COLS, 1024, COLS, 512)
    return pl.pallas_call(
        table_kernel,
        name="tables",
        out_shape=(jax.ShapeDtypeStruct((TOKENS, COLS), BF16),)
        + tuple(jax.ShapeDtypeStruct((rows, width), F32) for width in widths),
        in_specs=[hbm] * 3,
        out_specs=(hbm,) * 5,
        scratch_shapes=[
            pltpu.VMEM((TOKENS, COLS), BF16),
            pltpu.VMEM((2, rows, UP), BF16),
            pltpu.VMEM((2, rows, DOWN), BF16),
        ]
        + [pltpu.VMEM((rows, width), F32) for width in widths]
        + [pltpu.SemaphoreType.DMA((9,)), pltpu.SemaphoreType.DMA((11,))],
        compiler_params=pltpu.CompilerParams(vmem_limit_bytes=VMEM_BYTES),
    )(grad, up_terms.reshape(2, rows, UP), down_terms.reshape(2, rows, DOWN))


def shards(
    x_in, lengths, adapter_ids, attn_grad, w_query, w_key, w_value,
    query_down, query_up, value_down, value_up,
):
    grad, up_terms, down_terms = block_call(
        lengths, adapter_ids, x_in[0], attn_grad[0], w_query, w_key, w_value,
        query_down, value_down, query_up, value_up,
    )
    grad, qa, qb, va, vb = table_call(grad, up_terms, down_terms)
    tables = (table.reshape(ADAPTERS, RANK, -1) for table in (qa, qb, va, vb))
    return (grad[None], *tables)


def solution(mesh):
    placed = (
        P(("dp", "fsdp"), None, "tensor"),
        P(("dp", "fsdp")),
        P(("dp", "fsdp")),
        P(("dp", "fsdp"), None, "tensor"),
        P("fsdp", "tensor"),
        P("fsdp", "tensor"),
        P("fsdp", "tensor"),
        P(),
        P(None, None, "tensor"),
        P(),
        P(None, None, "tensor"),
    )
    return jax.shard_map(
        shards,
        mesh=mesh,
        in_specs=placed,
        out_specs=(
            P(("dp", "fsdp"), None, "tensor"),
            P(None, None, "tensor"),
            P(None, None, "tensor"),
            P(None, None, "tensor"),
            P(None, None, "tensor"),
        ),
        check_vma=False,
    )
```

```python
import math

import jax
import jax.numpy as jnp
from jax import lax
from jax.experimental import pallas as pl
from jax.experimental.pallas import tpu as pltpu
from jax.sharding import PartitionSpec as P

D = 4608
HD = 128
TOKENS = 512
RANK = 16
ADAPTERS = 16
SIDE = 4
ROWS = 288
GROUP = 512
COLS = 1152
HALF = 256
HEAD = 768
UP = 2 * HEAD
DOWN = 2 * COLS
TAGGED = DOWN + 128

soft_cap = 50.0
adapter_scale = 2.0
score_scale = 1.0 / 12.0

MESH = pl.DeviceIdType.MESH
F32 = jnp.float32
BF16 = jnp.bfloat16
VMEM_BYTES = 60 * 1024 * 1024


def dot(a, b, dims):
    return lax.dot_general(a, b, (dims, ((), ())), preferred_element_type=F32)


class Place:
    def __init__(self):
        self.dp = lax.axis_index("dp")
        self.f = lax.axis_index("fsdp")
        self.t = lax.axis_index("tensor")
        self.y, self.z = self.f // SIDE, self.f % SIDE
        self.core = self.t % 2
        self.x_lo = self.t // 2
        x = self.dp * 2 + self.x_lo
        to_mate = 1 - 2 * self.x_lo
        at = lambda n, core: ((n % SIDE) // 2, self.f, (n % 2) * 2 + core)
        self.mate = at(x + to_mate + SIDE, self.core)
        self.cross = at(x - to_mate + SIDE, self.core)
        self.opposite = at(x + 2, self.core)
        self.sibling = at(x, 1 - self.core)

    def part(self, flip, core):
        return ((self.x_lo + flip) % 2) * 2 + core

    def ring_y(self, n):
        return (self.dp, ((self.y + n) % SIDE) * SIDE + self.z, self.t)

    def ring_z(self, n):
        return (self.dp, self.y * SIDE + (self.z + n) % SIDE, self.t)


class Net:
    def __init__(self, send_sems, recv_sems):
        self.send_sems, self.recv_sems = send_sems, recv_sems
        self.started = []

    def send(self, index, src, dst, device):
        copy = pltpu.make_async_remote_copy(
            src_ref=src,
            dst_ref=dst,
            send_sem=self.send_sems.at[index],
            recv_sem=self.recv_sems.at[index],
            device_id=device,
            device_id_type=MESH,
        )
        copy.start()
        self.started.append(copy)

    def arrived(self, index, region, device):
        pltpu.make_async_remote_copy(
            src_ref=region,
            dst_ref=region,
            send_sem=self.send_sems.at[index],
            recv_sem=self.recv_sems.at[index],
            device_id=device,
            device_id_type=MESH,
        ).wait_recv()

    def finish(self):
        for copy in self.started:
            copy.wait_send()


def enter(peers):
    barrier = pltpu.get_barrier_semaphore()
    for peer in peers:
        pl.semaphore_signal(barrier, inc=1, device_id=peer, device_id_type=MESH)
    pl.semaphore_wait(barrier, len(peers))


class TorusGather:
    def __init__(self, net, base, place, y_first, view, low, high):
        self.net, self.base = net, base
        self.low, self.high = low, high
        p = place
        if y_first:
            self.one, self.two = p.ring_y, p.ring_z
            self.block = lambda n, w: view((p.y + n) % SIDE, p.z, w)
            self.line = lambda n, w: view(None, (p.z + n) % SIDE, w)
        else:
            self.one, self.two = p.ring_z, p.ring_y
            self.block = lambda n, w: view(p.y, (p.z + n) % SIDE, w)
            self.line = lambda n, w: view((p.y + n) % SIDE, None, w)

    def fan(self, base, region, ring):
        low, high = region(0, self.low), region(0, self.high)
        self.net.send(base, low, low, ring(1))
        self.net.send(base + 1, high, high, ring(-1))
        self.net.send(base + 2, high, high, ring(1))
        self.net.send(base + 3, low, low, ring(-1))

    def forward(self, base, region, ring):
        part = region(-1, self.low)
        self.net.arrived(base, part, ring(-1))
        self.net.send(base + 4, part, part, ring(1))
        part = region(1, self.high)
        self.net.arrived(base + 1, part, ring(1))
        self.net.send(base + 5, part, part, ring(-1))

    def close(self, base, region, ring):
        self.net.arrived(base + 2, region(-1, self.high), ring(-1))
        self.net.arrived(base + 3, region(1, self.low), ring(1))
        self.net.arrived(base + 4, region(2, self.low), ring(-1))
        self.net.arrived(base + 5, region(2, self.high), ring(1))

    def stage(self, n):
        if n == 1:
            self.fan(self.base, self.block, self.one)
        elif n == 2:
            self.forward(self.base, self.block, self.one)
        elif n == 3:
            self.close(self.base, self.block, self.one)
            self.fan(self.base + 6, self.line, self.two)
        elif n == 4:
            self.forward(self.base + 6, self.line, self.two)
        else:
            self.close(self.base + 6, self.line, self.two)


OWN, OTHER = 0, 1
TO_OPPOSITE, TO_CROSS, TO_MATE, TO_OWN = 0, 1, 2, 3
UPPER, LOWER = slice(HALF, TOKENS), slice(0, HALF)


def block_kernel(
    length_ref, id_ref, x_ref, g_ref, wq_ref, wk_ref, wv_ref, qd_ref, vd_ref, qu_ref, vu_ref,
    grad_out, owner_out, up_out, down_out,
    xs, ws, qds, vds, qus, vus, down, up, low, qkv, grads, cots, meta, dk_acc, dv_acc,
    sib_out, sib_in, ring_out, relay_in, ring_in, kept,
    low_mine, low_sib, low_chip, low_in, low_grad, up_terms, down_terms, low_acc, proj_acc,
    send_sems, recv_sems, local_sems,
):
    p = Place()
    net = Net(send_sems, recv_sems)
    copies = iter(range(32))

    def local(src, dst):
        copy = pltpu.make_async_copy(src, dst, local_sems.at[next(copies)])
        copy.start()
        return copy

    def cols_of(ref, start, width):
        return ref.at[..., pl.ds(pl.multiple_of(start, width), width)]

    def x_block(slot, flip, core, rows=slice(None)):
        column = pl.multiple_of(p.part(flip, core) * COLS, COLS)
        return xs.at[slot, rows, pl.ds(column, COLS)]

    my_rows = pl.ds(pl.multiple_of(p.z * ROWS, 32), ROWS)
    first = [local(x_ref, x_block(OWN, 0, p.core))]
    for g in range(2):
        for ref, at, width in ((wq_ref, 0, 256), (wk_ref, 256, 128), (wv_ref, 384, 128)):
            c = g * GROUP + at
            first.append(
                local(
                    cols_of(ref, p.dp * 2 * width + g * width, width),
                    ws.at[p.y, my_rows, c : c + width],
                )
            )
    later = [
        local(qd_ref, qds),
        local(vd_ref, vds),
        local(cols_of(qu_ref, p.dp * 512, 512), qus),
        local(cols_of(vu_ref, p.dp * 256, 256), vus),
        local(cols_of(g_ref, p.dp * 512, 512), cots.at[OWN]),
    ]
    line = lax.broadcasted_iota(jnp.int32, (8, 128), 0)
    meta[OWN] = jnp.where(line == 0, id_ref[0], length_ref[0])

    enter([
        p.mate, p.cross, p.opposite, p.sibling,
        p.ring_y(1), p.ring_y(-1), p.ring_z(1), p.ring_z(-1),
    ])

    net.send(0, meta.at[OWN], meta.at[OTHER], p.opposite)

    def weight_view(y, z, window):
        rows = slice(None) if z is None else pl.ds(pl.multiple_of(z * ROWS, 32), ROWS)
        return ws.at[slice(None) if y is None else y, rows, window]

    rounds = []
    for g in range(2):
        pair = []
        for h in range(2):
            c = g * GROUP + h * 256
            pair.append(
                TorusGather(
                    net, 40 + 12 * (2 * g + h), p, h == 0, weight_view,
                    slice(c, c + 128), slice(c + 128, c + 256),
                )
            )
        rounds.append(pair)

    def weights(g, stage):
        for one in rounds[g]:
            one.stage(stage)

    def x_send(index, slot, flip, rows, to_slot, device):
        net.send(
            index, x_block(slot, flip, p.core, rows), x_block(to_slot, flip, p.core, rows), device
        )

    for copy in first:
        copy.wait()
    weights(0, 1)
    weights(1, 1)
    every = slice(None)
    for index, rows, to_slot, device in (
        (1, UPPER, OWN, p.mate), (2, LOWER, OTHER, p.cross),
        (3, LOWER, OWN, p.mate), (4, UPPER, OTHER, p.cross), (5, every, OWN, p.sibling),
    ):
        net.send(index, x_block(OWN, 0, p.core, rows), x_block(to_slot, 0, p.core, rows), device)

    def send_cotangent(index, rows):
        net.send(
            index,
            g_ref.at[rows, pl.ds(pl.multiple_of((1 - p.dp) * 512, 512), 512)],
            cots.at[OTHER, rows],
            p.opposite,
        )

    weights(0, 2)
    weights(1, 2)
    weights(0, 3)

    for copy in later:
        copy.wait()
    net.arrived(0, meta.at[OTHER], p.opposite)
    up[...] = jnp.zeros_like(up)

    def choose(slot):
        chosen = meta[slot, 0:1, 0:1]

        def add(a, sums):
            weight = (chosen == a).astype(F32)
            return tuple(
                total + table[a].astype(F32) * weight
                for total, table in zip(sums, (qds, vds, qus, vus))
            )

        zeros = tuple(jnp.zeros((RANK, width), F32) for width in (D, D, 512, 256))
        q_rows, v_rows, q_up, v_up = lax.fori_loop(0, ADAPTERS, add, zeros)
        down[slot, :RANK, :] = q_rows.astype(BF16)
        down[slot, RANK:, :] = v_rows.astype(BF16)
        for g in range(2):
            c0 = g * GROUP
            up[slot, :RANK, c0 : c0 + 256] = q_up[:, g * 256 : g * 256 + 256].astype(BF16)
            up[slot, RANK:, c0 + 384 : c0 + 512] = v_up[:, g * 128 : g * 128 + 128].astype(BF16)

    choose(OWN)

    def x_arrived(index, slot, flip, rows, device, core=None):
        net.arrived(index, x_block(slot, flip, p.core if core is None else core, rows), device)

    x_arrived(1, OWN, 1, UPPER, p.mate)
    x_send(6, OWN, 1, UPPER, OTHER, p.cross)
    x_send(7, OWN, 1, UPPER, OWN, p.sibling)
    x_arrived(2, OTHER, 1, LOWER, p.cross)
    x_send(8, OTHER, 1, LOWER, OTHER, p.mate)
    x_send(9, OTHER, 1, LOWER, OTHER, p.sibling)
    send_cotangent(20, UPPER)
    send_cotangent(21, LOWER)
    choose(OTHER)
    weights(0, 4)
    weights(1, 3)
    x_arrived(3, OWN, 1, LOWER, p.mate)
    x_send(10, OWN, 1, LOWER, OWN, p.sibling)
    x_arrived(4, OTHER, 1, UPPER, p.cross)
    x_send(11, OTHER, 1, UPPER, OTHER, p.sibling)
    away = 1 - p.core
    x_arrived(5, OWN, 0, every, p.sibling, away)
    x_arrived(7, OWN, 1, UPPER, p.sibling, away)
    x_arrived(10, OWN, 1, LOWER, p.sibling, away)

    def rank_space(slot):
        low[slot] = dot(xs[slot], down[slot], ((1,), (1,))).astype(BF16)

    def project(slot, g):
        @pl.loop(0, 2)
        def _(n):
            window = pl.ds(pl.multiple_of(g * GROUP + n * 256, 256), 256)
            base = dot(xs[slot], ws[:, :, window].reshape(D, 256), ((1,), (0,)))
            extra = dot(low[slot], up[slot, :, window], ((1,), (0,)))
            qkv[slot, :, window] = (base + adapter_scale * extra).astype(BF16)

    def attend(slot, g, rows):
        c0 = g * GROUP
        start, step, span = rows.start, HALF, rows.stop
        length = meta[slot, 1:2, 0:1]
        k = qkv[slot, :span, c0 + 256 : c0 + 384]
        v = qkv[slot, :span, c0 + 384 : c0 + 512]
        key_at = lax.broadcasted_iota(jnp.int32, (span, step), 0)
        row_at = lax.broadcasted_iota(jnp.int32, (span, step), 1) + start
        allowed = (key_at <= row_at) & (key_at < length)
        used = lax.broadcasted_iota(jnp.int32, (step, HD), 0) + start < length
        dk, dv = 0.0, 0.0
        for h in range(2):
            q = qkv[slot, rows, c0 + h * HD : c0 + (h + 1) * HD]
            cot = cots[slot, rows, g * 256 + h * HD : g * 256 + (h + 1) * HD]
            cot = jnp.where(used, cot, jnp.zeros_like(cot))
            raw = dot(k, q, ((1,), (1,)))
            turned = jnp.tanh(raw * (score_scale / soft_cap))
            weight = jnp.where(allowed, jnp.exp(soft_cap * turned), 0.0)
            probs = weight * (1.0 / jnp.sum(weight, axis=0, keepdims=True))
            probs_b = probs.astype(BF16)
            dprob = dot(v, cot, ((1,), (1,)))
            row_total = jnp.sum(probs * dprob, axis=0, keepdims=True)
            dscore = (
                probs * (dprob - row_total) * ((1.0 - turned * turned) * score_scale)
            ).astype(BF16)
            dq = dot(k, dscore, ((0,), (0,)))
            grads[slot, rows, c0 + h * HD : c0 + (h + 1) * HD] = dq.T.astype(BF16)
            dk = dk + dot(dscore, q, ((1,), (0,)))
            dv = dv + dot(probs_b, cot, ((1,), (0,)))
        if rows.stop == TOKENS:
            dk_acc[g] = dk[:HALF]
            dv_acc[g] = dv[:HALF]
            dk, dv = dk[HALF:], dv[HALF:]
        else:
            dk, dv = dk + dk_acc[g], dv + dv_acc[g]
        grads[slot, rows, c0 + 256 : c0 + 384] = dk.astype(BF16)
        grads[slot, rows, c0 + 384 : c0 + 512] = dv.astype(BF16)

    rank_space(OWN)
    weights(0, 5)
    project(OWN, 0)
    attend(OWN, 0, UPPER)
    attend(OWN, 0, LOWER)

    x_arrived(9, OTHER, 1, LOWER, p.sibling, away)
    x_arrived(11, OTHER, 1, UPPER, p.sibling, away)
    wide = 2 * COLS

    def half_of(flip):
        lo = (p.x_lo + flip) % 2
        return pl.ds(pl.multiple_of(lo * wide, wide), wide), pl.ds(lo * 2, 2)

    columns, parts = half_of(1)
    low_acc[...] = dot(xs[OTHER, :, columns], down[OTHER, :, columns], ((1,), (1,)))

    @pl.loop(0, 2)
    def _(n):
        window = pl.ds(pl.multiple_of(n * 256, 256), 256)
        proj_acc[:, window] = dot(
            xs[OTHER, :, columns], ws[parts, :, window].reshape(wide, 256), ((1,), (0,))
        )

    x_arrived(6, OTHER, 0, UPPER, p.cross)
    x_send(12, OTHER, 0, UPPER, OTHER, p.sibling)
    x_arrived(8, OTHER, 0, LOWER, p.mate)
    x_send(13, OTHER, 0, LOWER, OTHER, p.sibling)
    weights(1, 4)
    x_arrived(12, OTHER, 0, UPPER, p.sibling, away)
    x_arrived(13, OTHER, 0, LOWER, p.sibling, away)
    columns, parts = half_of(0)
    rest = dot(xs[OTHER, :, columns], down[OTHER, :, columns], ((1,), (1,)))
    low[OTHER] = (low_acc[...] + rest).astype(BF16)

    @pl.loop(0, 2)
    def _(n):
        window = pl.ds(pl.multiple_of(n * 256, 256), 256)
        base = dot(xs[OTHER, :, columns], ws[parts, :, window].reshape(wide, 256), ((1,), (0,)))
        extra = dot(low[OTHER], up[OTHER, :, window], ((1,), (0,)))
        qkv[OTHER, :, window] = (
            base + proj_acc[:, window] + adapter_scale * extra
        ).astype(BF16)

    net.arrived(20, cots.at[OTHER, UPPER], p.opposite)
    attend(OTHER, 0, UPPER)
    weights(1, 5)
    project(OTHER, 1)
    attend(OTHER, 1, UPPER)

    slots = {TO_OPPOSITE: (OTHER, 0), TO_CROSS: (OTHER, 1), TO_MATE: (OWN, 1), TO_OWN: (OWN, 0)}

    def piece(rows, side):
        cut = 640 if rows is UPPER else 512
        return slice(0, cut) if side == 0 else slice(cut, COLS)

    def product(block, core, rows, cols):
        slot, flip = slots[block]
        return dot(grads[slot, rows], ws[p.part(flip, core), cols], ((1,), (1,)))

    def sib_index(block, rows, side):
        return 136 + 4 * block + 2 * (rows is UPPER) + side

    def for_sibling(block, rows):
        for side in range(2):
            cols = piece(rows, side)
            sib_out[block, rows, cols] = product(block, away, rows, cols).astype(BF16)
            net.send(
                sib_index(block, rows, side),
                sib_out.at[block, rows, cols], sib_in.at[block, rows, cols], p.sibling,
            )

    def both_cores(block, rows, side):
        cols = piece(rows, side)
        value = product(block, p.core, rows, cols)
        net.arrived(sib_index(block, rows, side), sib_in.at[block, rows, cols], p.sibling)
        return value + sib_in[block, rows, cols].astype(F32)

    def relayed(rows, side):
        if rows is UPPER:
            return ((32 + side, UPPER),)
        return ((34 + side, slice(128, 256)), (176 + side, slice(0, 128)))

    def to_ring(block, rows, side, relay=False):
        cols = piece(rows, side)
        value = both_cores(block, rows, side)
        if relay:
            for index, part in relayed(rows, side):
                net.arrived(index, relay_in.at[part, cols], (p.cross, p.mate)[side])
            value = value + relay_in[rows, cols].astype(F32)
        ring_out[block, rows, cols] = value.astype(BF16)

    def ship_relayed(rows, side, n):
        cols = piece(rows, side)
        index, part = relayed(rows, side)[n]
        net.send(
            index, ring_out.at[TO_OPPOSITE, part, cols], relay_in.at[part, cols],
            (p.cross, p.mate)[side],
        )

    def ring_index(block, rows, side):
        return 20 + 4 * block + 2 * (rows is UPPER) + side

    def ship(block, rows, side):
        cols = piece(rows, side)
        n, device = (0, p.cross) if block == TO_CROSS else (1, p.mate)
        net.send(
            ring_index(block, rows, side),
            ring_out.at[block, rows, cols], ring_in.at[n, rows, cols], device,
        )

    def up_terms_of(g):
        mine = up_terms.at[p.dp, p.y, p.z]
        window = slice(g * GROUP, (g + 1) * GROUP)
        for slot in (OWN, OTHER):
            seq = p.dp if slot == OWN else 1 - p.dp
            value = adapter_scale * dot(low[slot], grads[slot, :, window], ((0,), (0,)))
            value = value.astype(BF16)
            at = pl.multiple_of(g * HEAD + seq * 256, 256)
            mine[:, pl.ds(at, 256)] = value[:RANK, :256]
            at = pl.multiple_of(g * HEAD + 512 + seq * 128, 128)
            mine[:, pl.ds(at, 128)] = value[RANK:, 384:]

    def terms_gather(base, ref, cuts):
        everything = slice(None)

        def view(y, z, window):
            return ref.at[
                :, everything if y is None else y, everything if z is None else z, :, window
            ]

        return [
            TorusGather(
                net, base + 12 * n, p, n == 0, view,
                slice(cuts[2 * n], cuts[2 * n + 1]),
                slice(cuts[2 * n + 1], cuts[2 * n + 2]),
            )
            for n in range(2)
        ]

    up_gather = terms_gather(88, up_terms, (0, 384, 768, 1152, UP))
    down_gather = terms_gather(112, down_terms, (0, 640, 1280, 1920, TAGGED))

    def stage(gather, n):
        for one in gather:
            one.stage(n)

    for_sibling(TO_OPPOSITE, UPPER)
    for side in range(2):
        to_ring(TO_OPPOSITE, UPPER, side)
        ship_relayed(UPPER, side, 0)
    net.arrived(21, cots.at[OTHER, LOWER], p.opposite)
    attend(OTHER, 0, LOWER)
    attend(OTHER, 1, LOWER)
    up_terms_of(0)
    for_sibling(TO_OPPOSITE, LOWER)
    project(OWN, 1)
    for side in range(2):
        to_ring(TO_OPPOSITE, LOWER, side)
        ship_relayed(LOWER, side, 0)
    attend(OWN, 1, UPPER)
    attend(OWN, 1, LOWER)

    for slot in (OWN, OTHER):
        low_mine[slot] = adapter_scale * dot(up[slot], grads[slot], ((1,), (1,)))
    net.send(14, low_mine, low_sib, p.sibling)
    up_terms_of(1)
    net.arrived(14, low_sib, p.sibling)
    low_chip[...] = (low_mine[...] + low_sib[...]).astype(BF16)
    for n, device in enumerate((p.mate, p.cross, p.opposite)):
        net.send(16 + n, low_chip, low_in.at[n], device)
    my_up = up_terms.at[p.dp, p.y, p.z]
    net.send(15, my_up, my_up, p.opposite)
    for side in range(2):
        ship_relayed(LOWER, side, 1)
    for_sibling(TO_CROSS, UPPER)
    for_sibling(TO_MATE, UPPER)
    to_ring(TO_CROSS, UPPER, 0)
    ship(TO_CROSS, UPPER, 0)
    to_ring(TO_MATE, UPPER, 1)
    ship(TO_MATE, UPPER, 1)

    for n, device in enumerate((p.mate, p.cross, p.opposite)):
        net.arrived(16 + n, low_in.at[n], device)
    my_cols = pl.ds(pl.multiple_of(p.t * COLS, COLS), COLS)
    for slot in (OWN, OTHER):
        pair = low_chip[slot].astype(F32) + low_in[0, slot].astype(F32)
        far = low_in[1, 1 - slot].astype(F32) + low_in[2, 1 - slot].astype(F32)
        low_grad[slot] = (pair + far).astype(BF16)
        value = dot(low_grad[slot], xs[slot, :, my_cols], ((1,), (0,))).astype(BF16)
        my_down = down_terms.at[p.dp if slot == OWN else 1 - p.dp, p.y, p.z]
        my_down[:, 0:COLS] = value[:RANK]
        my_down[:, COLS:DOWN] = value[RANK:]
        tag = jnp.broadcast_to(meta[slot, 0:1, :], (RANK, 128))
        my_down[:, DOWN:TAGGED] = tag.astype(F32).astype(BF16)
    stage(down_gather, 1)
    net.arrived(15, up_terms.at[1 - p.dp, p.y, p.z], p.opposite)
    stage(up_gather, 1)
    for_sibling(TO_CROSS, LOWER)
    for_sibling(TO_MATE, LOWER)
    stage(down_gather, 2)
    to_ring(TO_CROSS, LOWER, 0)
    ship(TO_CROSS, LOWER, 0)
    to_ring(TO_MATE, LOWER, 1)
    ship(TO_MATE, LOWER, 1)
    stage(up_gather, 2)
    to_ring(TO_MATE, UPPER, 0, True)
    ship(TO_MATE, UPPER, 0)
    to_ring(TO_CROSS, UPPER, 1, True)
    ship(TO_CROSS, UPPER, 1)
    stage(down_gather, 3)
    to_ring(TO_MATE, LOWER, 0, True)
    ship(TO_MATE, LOWER, 0)
    to_ring(TO_CROSS, LOWER, 1, True)
    ship(TO_CROSS, LOWER, 1)
    for_sibling(TO_OWN, UPPER)
    for_sibling(TO_OWN, LOWER)
    stage(up_gather, 3)

    def keep(rows):
        for side in range(2):
            cols = piece(rows, side)
            columns = pl.ds(pl.multiple_of(p.t * COLS + cols.start, 128), cols.stop - cols.start)
            extra = dot(low_grad[OWN, :, rows], down[OWN, :, columns], ((0,), (0,)))
            kept[rows, cols] = both_cores(TO_OWN, rows, side) + extra

    keep(UPPER)
    stage(down_gather, 4)
    keep(LOWER)
    stage(up_gather, 4)
    stage(down_gather, 5)
    save = local(down_terms, down_out)

    rows = 16 * RANK
    at = lax.broadcasted_iota(jnp.int32, (rows, rows), 0)
    to = lax.broadcasted_iota(jnp.int32, (rows, rows), 1)
    for s in range(2):
        chosen = down_terms[s, :, :, :, DOWN:TAGGED].reshape(rows, 128)[:, 0:1].astype(F32)
        own = ((to // RANK).astype(F32) == chosen) & (at % RANK == to % RANK)
        owner_out[s] = own.astype(F32).T.astype(BF16)


    def finish_rows(rows):
        for side in range(2):
            cols = piece(rows, side)
            net.arrived(ring_index(TO_CROSS, rows, side), ring_in.at[0, rows, cols], p.cross)
            net.arrived(ring_index(TO_MATE, rows, side), ring_in.at[1, rows, cols], p.mate)
        grad_out[rows] = (
            kept[rows] + ring_in[0, rows].astype(F32) + ring_in[1, rows].astype(F32)
        ).astype(BF16)

    finish_rows(UPPER)
    stage(up_gather, 5)
    save_up = local(up_terms, up_out)
    finish_rows(LOWER)
    net.finish()
    save_up.wait()
    save.wait()


def block_call(lengths, ids, *arrays):
    hbm = pl.BlockSpec(memory_space=pl.ANY)
    vmem = pl.BlockSpec(memory_space=pltpu.VMEM)
    smem = pl.BlockSpec(memory_space=pltpu.SMEM)
    bf16 = lambda *shape: pltpu.VMEM(shape, BF16)
    f32 = lambda *shape: pltpu.VMEM(shape, F32)
    return pl.pallas_call(
        block_kernel,
        name="attention_block",
        out_shape=(
            jax.ShapeDtypeStruct((TOKENS, COLS), BF16),
            jax.ShapeDtypeStruct((2, 16 * RANK, 16 * RANK), BF16),
            jax.ShapeDtypeStruct((2, SIDE, SIDE, RANK, UP), BF16),
            jax.ShapeDtypeStruct((2, SIDE, SIDE, RANK, TAGGED), BF16),
        ),
        in_specs=[smem, smem] + [hbm] * 9,
        out_specs=(vmem, vmem, hbm, hbm),
        scratch_shapes=[
            bf16(2, TOKENS, D),
            bf16(SIDE, COLS, 2 * GROUP),
            bf16(ADAPTERS, RANK, D),
            bf16(ADAPTERS, RANK, D),
            bf16(ADAPTERS, RANK, 512),
            bf16(ADAPTERS, RANK, 256),
            bf16(2, 2 * RANK, D),
            bf16(2, 2 * RANK, 2 * GROUP),
            bf16(2, TOKENS, 2 * RANK),
            bf16(2, TOKENS, 2 * GROUP),
            bf16(2, TOKENS, 2 * GROUP),
            bf16(2, TOKENS, 512),
            pltpu.VMEM((2, 8, 128), jnp.int32),
            f32(2, HALF, HD),
            f32(2, HALF, HD),
            bf16(4, TOKENS, COLS),
            bf16(4, TOKENS, COLS),
            bf16(3, TOKENS, COLS),
            bf16(TOKENS, COLS),
            bf16(2, TOKENS, COLS),
            f32(TOKENS, COLS),
            f32(2, 2 * RANK, TOKENS),
            f32(2, 2 * RANK, TOKENS),
            bf16(2, 2 * RANK, TOKENS),
            bf16(3, 2, 2 * RANK, TOKENS),
            bf16(2, 2 * RANK, TOKENS),
            bf16(2, SIDE, SIDE, RANK, UP),
            bf16(2, SIDE, SIDE, RANK, TAGGED),
            f32(TOKENS, 2 * RANK),
            f32(TOKENS, GROUP),
            pltpu.SemaphoreType.DMA((178,)),
            pltpu.SemaphoreType.DMA((178,)),
            pltpu.SemaphoreType.DMA((16,)),
        ],
        compiler_params=pltpu.CompilerParams(
            collective_id=0, has_side_effects=True, vmem_limit_bytes=VMEM_BYTES
        ),
    )(lengths, ids, *arrays)


def table_kernel(
    grad_ref, owner_ref, up_ref, down_ref,
    grad_out, qa_out, qb_out, va_out, vb_out,
    grad, owners, up, down, qa, qb, va, vb, in_sems, out_sems,
):
    width = 384
    pairs = [(owner_ref, owners), (up_ref, up)]
    for n in range(2 * COLS // width):
        cols = slice(n * width, (n + 1) * width)
        pairs.append((down_ref.at[:, :, cols], down.at[:, :, cols]))
    pairs.append((grad_ref, grad))
    loads = [
        pltpu.make_async_copy(src, dst, in_sems.at[n]) for n, (src, dst) in enumerate(pairs)
    ]
    for load in loads:
        load.start()
    stores = []

    def store(src, dst):
        copy = pltpu.make_async_copy(src, dst, out_sems.at[len(stores)])
        copy.start()
        stores.append(copy)

    def total(first, second):
        return dot(owners[0], first, ((1,), (0,))) + dot(owners[1], second, ((1,), (0,)))

    for load in loads[:2]:
        load.wait()
    for out, to_ref, start, size in ((qb, qb_out, 0, 256), (vb, vb_out, 512, 128)):
        for d in range(2):
            for g in range(2):
                at, first = (2 * d + g) * size, g * HEAD + start
                out[:, at : at + size] = total(
                    up[d, :, first : first + size], up[d, :, first + size : first + 2 * size]
                )
        store(out, to_ref)
    for n in range(2 * COLS // width):
        loads[2 + n].wait()
        out, to_ref, c = (qa, qa_out, 0) if n < COLS // width else (va, va_out, COLS)
        cols = slice(n * width, (n + 1) * width)
        here = slice(n * width - c, (n + 1) * width - c)
        out[:, here] = total(down[0, :, cols], down[1, :, cols])
        store(out.at[:, here], to_ref.at[:, here])
    loads[-1].wait()
    store(grad, grad_out)
    for copy in stores:
        copy.wait()


def table_call(grad, owners, *terms):
    hbm = pl.BlockSpec(memory_space=pl.ANY)
    rows = 16 * RANK
    widths = (COLS, 1024, COLS, 512)
    return pl.pallas_call(
        table_kernel,
        name="tables",
        out_shape=(jax.ShapeDtypeStruct((TOKENS, COLS), BF16),)
        + tuple(jax.ShapeDtypeStruct((rows, width), F32) for width in widths),
        in_specs=[hbm] * 4,
        out_specs=(hbm,) * 5,
        scratch_shapes=[
            pltpu.VMEM((TOKENS, COLS), BF16),
            pltpu.VMEM((2, rows, rows), BF16),
            pltpu.VMEM((2, rows, UP), BF16),
            pltpu.VMEM((2, rows, DOWN), BF16),
        ]
        + [pltpu.VMEM((rows, width), F32) for width in widths]
        + [pltpu.SemaphoreType.DMA((10,)), pltpu.SemaphoreType.DMA((9,))],
        compiler_params=pltpu.CompilerParams(vmem_limit_bytes=VMEM_BYTES),
    )(grad, owners, *(block.reshape(2, rows, -1) for block in terms))


def shards(
    x_in, lengths, adapter_ids, attn_grad, w_query, w_key, w_value,
    query_down, query_up, value_down, value_up,
):
    grad, owners, *terms = block_call(
        lengths, adapter_ids, x_in[0], attn_grad[0], w_query, w_key, w_value,
        query_down, value_down, query_up, value_up,
    )
    grad, qa, qb, va, vb = table_call(grad, owners, *terms)
    tables = (table.reshape(ADAPTERS, RANK, -1) for table in (qa, qb, va, vb))
    return (grad[None], *tables)


def solution(mesh):
    placed = (
        P(("dp", "fsdp"), None, "tensor"),
        P(("dp", "fsdp")),
        P(("dp", "fsdp")),
        P(("dp", "fsdp"), None, "tensor"),
        P("fsdp", "tensor"),
        P("fsdp", "tensor"),
        P("fsdp", "tensor"),
        P(),
        P(None, None, "tensor"),
        P(),
        P(None, None, "tensor"),
    )
    return jax.shard_map(
        shards,
        mesh=mesh,
        in_specs=placed,
        out_specs=(
            P(("dp", "fsdp"), None, "tensor"),
            P(None, None, "tensor"),
            P(None, None, "tensor"),
            P(None, None, "tensor"),
            P(None, None, "tensor"),
        ),
        check_vma=False,
    )
```

```python
import math

import jax
import jax.numpy as jnp
from jax import lax
from jax.experimental import pallas as pl
from jax.experimental.pallas import tpu as pltpu
from jax.sharding import PartitionSpec as P

D = 4608
HD = 128
TOKENS = 512
RANK = 16
ADAPTERS = 16
SIDE = 4
ROWS = 288
GROUP = 512
COLS = 1152
HALF = 256
HEAD = 768
UP = 2 * HEAD
DOWN = 2 * COLS
TAGGED = DOWN + 128

soft_cap = 50.0
adapter_scale = 2.0
score_scale = 1.0 / 12.0

MESH = pl.DeviceIdType.MESH
F32 = jnp.float32
BF16 = jnp.bfloat16
VMEM_BYTES = 60 * 1024 * 1024


def dot(a, b, dims):
    return lax.dot_general(a, b, (dims, ((), ())), preferred_element_type=F32)


class Place:
    def __init__(self):
        self.dp = lax.axis_index("dp")
        self.f = lax.axis_index("fsdp")
        self.t = lax.axis_index("tensor")
        self.y, self.z = self.f // SIDE, self.f % SIDE
        self.core = self.t % 2
        self.x_lo = self.t // 2
        x = self.dp * 2 + self.x_lo
        to_mate = 1 - 2 * self.x_lo
        at = lambda n, core: ((n % SIDE) // 2, self.f, (n % 2) * 2 + core)
        self.mate = at(x + to_mate + SIDE, self.core)
        self.cross = at(x - to_mate + SIDE, self.core)
        self.opposite = at(x + 2, self.core)
        self.sibling = at(x, 1 - self.core)

    def part(self, flip, core):
        return ((self.x_lo + flip) % 2) * 2 + core

    def ring_y(self, n):
        return (self.dp, ((self.y + n) % SIDE) * SIDE + self.z, self.t)

    def ring_z(self, n):
        return (self.dp, self.y * SIDE + (self.z + n) % SIDE, self.t)


class Net:
    def __init__(self, send_sems, recv_sems):
        self.send_sems, self.recv_sems = send_sems, recv_sems
        self.started = []

    def send(self, index, src, dst, device):
        copy = pltpu.make_async_remote_copy(
            src_ref=src,
            dst_ref=dst,
            send_sem=self.send_sems.at[index],
            recv_sem=self.recv_sems.at[index],
            device_id=device,
            device_id_type=MESH,
        )
        copy.start()
        self.started.append(copy)

    def arrived(self, index, region, device):
        pltpu.make_async_remote_copy(
            src_ref=region,
            dst_ref=region,
            send_sem=self.send_sems.at[index],
            recv_sem=self.recv_sems.at[index],
            device_id=device,
            device_id_type=MESH,
        ).wait_recv()

    def finish(self):
        for copy in self.started:
            copy.wait_send()


def enter(peers):
    barrier = pltpu.get_barrier_semaphore()
    for peer in peers:
        pl.semaphore_signal(barrier, inc=1, device_id=peer, device_id_type=MESH)
    pl.semaphore_wait(barrier, len(peers))


class TorusGather:
    def __init__(self, net, base, place, y_first, view, low, high):
        self.net, self.base = net, base
        self.low, self.high = low, high
        p = place
        if y_first:
            self.one, self.two = p.ring_y, p.ring_z
            self.block = lambda n, w: view((p.y + n) % SIDE, p.z, w)
            self.line = lambda n, w: view(None, (p.z + n) % SIDE, w)
        else:
            self.one, self.two = p.ring_z, p.ring_y
            self.block = lambda n, w: view(p.y, (p.z + n) % SIDE, w)
            self.line = lambda n, w: view((p.y + n) % SIDE, None, w)

    def fan(self, base, region, ring):
        low, high = region(0, self.low), region(0, self.high)
        self.net.send(base, low, low, ring(1))
        self.net.send(base + 1, high, high, ring(-1))
        self.net.send(base + 2, high, high, ring(1))
        self.net.send(base + 3, low, low, ring(-1))

    def forward(self, base, region, ring):
        part = region(-1, self.low)
        self.net.arrived(base, part, ring(-1))
        self.net.send(base + 4, part, part, ring(1))
        part = region(1, self.high)
        self.net.arrived(base + 1, part, ring(1))
        self.net.send(base + 5, part, part, ring(-1))

    def close(self, base, region, ring):
        self.net.arrived(base + 2, region(-1, self.high), ring(-1))
        self.net.arrived(base + 3, region(1, self.low), ring(1))
        self.net.arrived(base + 4, region(2, self.low), ring(-1))
        self.net.arrived(base + 5, region(2, self.high), ring(1))

    def stage(self, n):
        if n == 1:
            self.fan(self.base, self.block, self.one)
        elif n == 2:
            self.forward(self.base, self.block, self.one)
        elif n == 3:
            self.close(self.base, self.block, self.one)
            self.fan(self.base + 6, self.line, self.two)
        elif n == 4:
            self.forward(self.base + 6, self.line, self.two)
        else:
            self.close(self.base + 6, self.line, self.two)


OWN, OTHER = 0, 1
TO_OPPOSITE, TO_CROSS, TO_MATE, TO_OWN = 0, 1, 2, 3
UPPER, LOWER = slice(HALF, TOKENS), slice(0, HALF)


def block_kernel(
    length_ref, id_ref, x_ref, g_ref, wq_ref, wk_ref, wv_ref, qd_ref, vd_ref, qu_ref, vu_ref,
    grad_out, owner_out, up_out, down_out,
    xs, ws, qds, vds, qus, vus, down, up, low, qkv, grads, cots, meta, dk_acc, dv_acc,
    sib_out, sib_in, ring_out, relay_in, ring_in, kept,
    low_mine, low_sib, low_chip, low_in, low_grad, up_terms, down_terms, low_acc, proj_acc,
    send_sems, recv_sems, local_sems,
):
    p = Place()
    net = Net(send_sems, recv_sems)
    copies = iter(range(32))

    def local(src, dst):
        copy = pltpu.make_async_copy(src, dst, local_sems.at[next(copies)])
        copy.start()
        return copy

    def cols_of(ref, start, width):
        return ref.at[..., pl.ds(pl.multiple_of(start, width), width)]

    def x_block(slot, flip, core, rows=slice(None)):
        column = pl.multiple_of(p.part(flip, core) * COLS, COLS)
        return xs.at[slot, rows, pl.ds(column, COLS)]

    my_rows = pl.ds(pl.multiple_of(p.z * ROWS, 32), ROWS)
    first = [local(x_ref, x_block(OWN, 0, p.core))]
    for g in range(2):
        for ref, at, width in ((wq_ref, 0, 256), (wk_ref, 256, 128), (wv_ref, 384, 128)):
            c = g * GROUP + at
            first.append(
                local(
                    cols_of(ref, p.dp * 2 * width + g * width, width),
                    ws.at[p.y, my_rows, c : c + width],
                )
            )
    later = [
        local(qd_ref, qds),
        local(vd_ref, vds),
        local(cols_of(qu_ref, p.dp * 512, 512), qus),
        local(cols_of(vu_ref, p.dp * 256, 256), vus),
        local(cols_of(g_ref, p.dp * 512, 512), cots.at[OWN]),
    ]
    line = lax.broadcasted_iota(jnp.int32, (8, 128), 0)
    meta[OWN] = jnp.where(line == 0, id_ref[0], length_ref[0])

    enter([
        p.mate, p.cross, p.opposite, p.sibling,
        p.ring_y(1), p.ring_y(-1), p.ring_z(1), p.ring_z(-1),
    ])

    net.send(0, meta.at[OWN], meta.at[OTHER], p.opposite)

    def weight_view(y, z, window):
        rows = slice(None) if z is None else pl.ds(pl.multiple_of(z * ROWS, 32), ROWS)
        return ws.at[slice(None) if y is None else y, rows, window]

    rounds = []
    for g in range(2):
        pair = []
        for h in range(2):
            c = g * GROUP + h * 256
            pair.append(
                TorusGather(
                    net, 40 + 12 * (2 * g + h), p, h == 0, weight_view,
                    slice(c, c + 128), slice(c + 128, c + 256),
                )
            )
        rounds.append(pair)

    def weights(g, stage):
        for one in rounds[g]:
            one.stage(stage)

    def x_send(index, slot, flip, rows, to_slot, device):
        net.send(
            index, x_block(slot, flip, p.core, rows), x_block(to_slot, flip, p.core, rows), device
        )

    for copy in first:
        copy.wait()
    weights(0, 1)
    weights(1, 1)
    every = slice(None)
    for index, rows, to_slot, device in (
        (1, UPPER, OWN, p.mate), (2, LOWER, OTHER, p.cross),
        (3, LOWER, OWN, p.mate), (4, UPPER, OTHER, p.cross), (5, every, OWN, p.sibling),
    ):
        net.send(index, x_block(OWN, 0, p.core, rows), x_block(to_slot, 0, p.core, rows), device)

    def send_cotangent(index, rows):
        net.send(
            index,
            g_ref.at[rows, pl.ds(pl.multiple_of((1 - p.dp) * 512, 512), 512)],
            cots.at[OTHER, rows],
            p.opposite,
        )

    weights(0, 2)
    weights(1, 2)
    weights(0, 3)

    for copy in later:
        copy.wait()
    net.arrived(0, meta.at[OTHER], p.opposite)
    up[...] = jnp.zeros_like(up)

    def choose(slot):
        chosen = meta[slot, 0:1, 0:1]

        def add(a, sums):
            weight = (chosen == a).astype(F32)
            return tuple(
                total + table[a].astype(F32) * weight
                for total, table in zip(sums, (qds, vds, qus, vus))
            )

        zeros = tuple(jnp.zeros((RANK, width), F32) for width in (D, D, 512, 256))
        q_rows, v_rows, q_up, v_up = lax.fori_loop(0, ADAPTERS, add, zeros)
        down[slot, :RANK, :] = q_rows.astype(BF16)
        down[slot, RANK:, :] = v_rows.astype(BF16)
        for g in range(2):
            c0 = g * GROUP
            up[slot, :RANK, c0 : c0 + 256] = q_up[:, g * 256 : g * 256 + 256].astype(BF16)
            up[slot, RANK:, c0 + 384 : c0 + 512] = v_up[:, g * 128 : g * 128 + 128].astype(BF16)

    choose(OWN)

    def x_arrived(index, slot, flip, rows, device, core=None):
        net.arrived(index, x_block(slot, flip, p.core if core is None else core, rows), device)

    x_arrived(1, OWN, 1, UPPER, p.mate)
    x_send(6, OWN, 1, UPPER, OTHER, p.cross)
    x_send(7, OWN, 1, UPPER, OWN, p.sibling)
    x_arrived(2, OTHER, 1, LOWER, p.cross)
    x_send(8, OTHER, 1, LOWER, OTHER, p.mate)
    x_send(9, OTHER, 1, LOWER, OTHER, p.sibling)
    send_cotangent(20, UPPER)
    send_cotangent(21, LOWER)
    choose(OTHER)
    weights(0, 4)
    weights(1, 3)
    x_arrived(3, OWN, 1, LOWER, p.mate)
    x_send(10, OWN, 1, LOWER, OWN, p.sibling)
    x_arrived(4, OTHER, 1, UPPER, p.cross)
    x_send(11, OTHER, 1, UPPER, OTHER, p.sibling)
    away = 1 - p.core
    x_arrived(5, OWN, 0, every, p.sibling, away)
    x_arrived(7, OWN, 1, UPPER, p.sibling, away)
    x_arrived(10, OWN, 1, LOWER, p.sibling, away)

    def rank_space(slot):
        low[slot] = dot(xs[slot], down[slot], ((1,), (1,))).astype(BF16)

    def project(slot, g):
        @pl.loop(0, 2)
        def _(n):
            window = pl.ds(pl.multiple_of(g * GROUP + n * 256, 256), 256)
            base = dot(xs[slot], ws[:, :, window].reshape(D, 256), ((1,), (0,)))
            extra = dot(low[slot], up[slot, :, window], ((1,), (0,)))
            qkv[slot, :, window] = (base + adapter_scale * extra).astype(BF16)

    def attend(slot, g, rows):
        c0 = g * GROUP
        start, step, span = rows.start, HALF, rows.stop
        length = meta[slot, 1:2, 0:1]
        k = qkv[slot, :span, c0 + 256 : c0 + 384]
        v = qkv[slot, :span, c0 + 384 : c0 + 512]
        key_at = lax.broadcasted_iota(jnp.int32, (span, step), 0)
        row_at = lax.broadcasted_iota(jnp.int32, (span, step), 1) + start
        allowed = (key_at <= row_at) & (key_at < length)
        used = lax.broadcasted_iota(jnp.int32, (step, HD), 0) + start < length
        dk, dv = 0.0, 0.0
        for h in range(2):
            q = qkv[slot, rows, c0 + h * HD : c0 + (h + 1) * HD]
            cot = cots[slot, rows, g * 256 + h * HD : g * 256 + (h + 1) * HD]
            cot = jnp.where(used, cot, jnp.zeros_like(cot))
            raw = dot(k, q, ((1,), (1,)))
            turned = jnp.tanh(raw * (score_scale / soft_cap))
            weight = jnp.where(allowed, jnp.exp(soft_cap * turned), 0.0)
            probs = weight * (1.0 / jnp.sum(weight, axis=0, keepdims=True))
            probs_b = probs.astype(BF16)
            dprob = dot(v, cot, ((1,), (1,)))
            row_total = jnp.sum(probs * dprob, axis=0, keepdims=True)
            dscore = (
                probs * (dprob - row_total) * ((1.0 - turned * turned) * score_scale)
            ).astype(BF16)
            dq = dot(k, dscore, ((0,), (0,)))
            grads[slot, rows, c0 + h * HD : c0 + (h + 1) * HD] = dq.T.astype(BF16)
            dk = dk + dot(dscore, q, ((1,), (0,)))
            dv = dv + dot(probs_b, cot, ((1,), (0,)))
        if rows.stop == TOKENS:
            dk_acc[g] = dk[:HALF]
            dv_acc[g] = dv[:HALF]
            dk, dv = dk[HALF:], dv[HALF:]
        else:
            dk, dv = dk + dk_acc[g], dv + dv_acc[g]
        grads[slot, rows, c0 + 256 : c0 + 384] = dk.astype(BF16)
        grads[slot, rows, c0 + 384 : c0 + 512] = dv.astype(BF16)

    rank_space(OWN)
    weights(0, 5)
    project(OWN, 0)
    attend(OWN, 0, UPPER)
    attend(OWN, 0, LOWER)

    x_arrived(9, OTHER, 1, LOWER, p.sibling, away)
    x_arrived(11, OTHER, 1, UPPER, p.sibling, away)
    wide = 2 * COLS

    def half_of(flip):
        lo = (p.x_lo + flip) % 2
        return pl.ds(pl.multiple_of(lo * wide, wide), wide), pl.ds(lo * 2, 2)

    columns, parts = half_of(1)
    low_acc[...] = dot(xs[OTHER, :, columns], down[OTHER, :, columns], ((1,), (1,)))

    @pl.loop(0, 2)
    def _(n):
        window = pl.ds(pl.multiple_of(n * 256, 256), 256)
        proj_acc[:, window] = dot(
            xs[OTHER, :, columns], ws[parts, :, window].reshape(wide, 256), ((1,), (0,))
        )

    x_arrived(6, OTHER, 0, UPPER, p.cross)
    x_send(12, OTHER, 0, UPPER, OTHER, p.sibling)
    x_arrived(8, OTHER, 0, LOWER, p.mate)
    x_send(13, OTHER, 0, LOWER, OTHER, p.sibling)
    weights(1, 4)
    x_arrived(12, OTHER, 0, UPPER, p.sibling, away)
    x_arrived(13, OTHER, 0, LOWER, p.sibling, away)
    columns, parts = half_of(0)
    rest = dot(xs[OTHER, :, columns], down[OTHER, :, columns], ((1,), (1,)))
    low[OTHER] = (low_acc[...] + rest).astype(BF16)

    @pl.loop(0, 2)
    def _(n):
        window = pl.ds(pl.multiple_of(n * 256, 256), 256)
        base = dot(xs[OTHER, :, columns], ws[parts, :, window].reshape(wide, 256), ((1,), (0,)))
        extra = dot(low[OTHER], up[OTHER, :, window], ((1,), (0,)))
        qkv[OTHER, :, window] = (
            base + proj_acc[:, window] + adapter_scale * extra
        ).astype(BF16)

    net.arrived(20, cots.at[OTHER, UPPER], p.opposite)
    attend(OTHER, 0, UPPER)
    weights(1, 5)
    project(OTHER, 1)
    attend(OTHER, 1, UPPER)

    slots = {TO_OPPOSITE: (OTHER, 0), TO_CROSS: (OTHER, 1), TO_MATE: (OWN, 1), TO_OWN: (OWN, 0)}

    def piece(rows, side):
        cut = 640 if rows is UPPER else 512
        return slice(0, cut) if side == 0 else slice(cut, COLS)

    def product(block, core, rows, cols):
        slot, flip = slots[block]
        return dot(grads[slot, rows], ws[p.part(flip, core), cols], ((1,), (1,)))

    def sib_index(block, rows, side):
        return 136 + 4 * block + 2 * (rows is UPPER) + side

    def for_sibling(block, rows):
        for side in range(2):
            cols = piece(rows, side)
            sib_out[block, rows, cols] = product(block, away, rows, cols).astype(BF16)
            net.send(
                sib_index(block, rows, side),
                sib_out.at[block, rows, cols], sib_in.at[block, rows, cols], p.sibling,
            )

    def both_cores(block, rows, side):
        cols = piece(rows, side)
        value = product(block, p.core, rows, cols)
        net.arrived(sib_index(block, rows, side), sib_in.at[block, rows, cols], p.sibling)
        return value + sib_in[block, rows, cols].astype(F32)

    def relayed(rows, side):
        if rows is UPPER:
            return ((32 + side, UPPER),)
        return ((34 + side, slice(128, 256)), (176 + side, slice(0, 128)))

    def to_ring(block, rows, side, relay=False):
        cols = piece(rows, side)
        value = both_cores(block, rows, side)
        if relay:
            for index, part in relayed(rows, side):
                net.arrived(index, relay_in.at[part, cols], (p.cross, p.mate)[side])
            value = value + relay_in[rows, cols].astype(F32)
        ring_out[block, rows, cols] = value.astype(BF16)

    def ship_relayed(rows, side, n):
        cols = piece(rows, side)
        index, part = relayed(rows, side)[n]
        net.send(
            index, ring_out.at[TO_OPPOSITE, part, cols], relay_in.at[part, cols],
            (p.cross, p.mate)[side],
        )

    def ring_index(block, rows, side):
        return 20 + 4 * block + 2 * (rows is UPPER) + side

    def ship(block, rows, side):
        cols = piece(rows, side)
        n, device = (0, p.cross) if block == TO_CROSS else (1, p.mate)
        net.send(
            ring_index(block, rows, side),
            ring_out.at[block, rows, cols], ring_in.at[n, rows, cols], device,
        )

    def up_terms_of(g):
        mine = up_terms.at[p.dp, p.y, p.z]
        window = slice(g * GROUP, (g + 1) * GROUP)
        for slot in (OWN, OTHER):
            seq = p.dp if slot == OWN else 1 - p.dp
            value = adapter_scale * dot(low[slot], grads[slot, :, window], ((0,), (0,)))
            value = value.astype(BF16)
            at = pl.multiple_of(g * HEAD + seq * 256, 256)
            mine[:, pl.ds(at, 256)] = value[:RANK, :256]
            at = pl.multiple_of(g * HEAD + 512 + seq * 128, 128)
            mine[:, pl.ds(at, 128)] = value[RANK:, 384:]

    def terms_gather(base, ref, cuts):
        everything = slice(None)

        def view(y, z, window):
            return ref.at[
                :, everything if y is None else y, everything if z is None else z, :, window
            ]

        return [
            TorusGather(
                net, base + 12 * n, p, n == 0, view,
                slice(cuts[2 * n], cuts[2 * n + 1]),
                slice(cuts[2 * n + 1], cuts[2 * n + 2]),
            )
            for n in range(2)
        ]

    up_gather = terms_gather(88, up_terms, (0, 384, 768, 1152, UP))
    down_gather = terms_gather(112, down_terms, (0, 640, 1280, 1920, TAGGED))

    def stage(gather, n):
        for one in gather:
            one.stage(n)

    for_sibling(TO_OPPOSITE, UPPER)
    for side in range(2):
        to_ring(TO_OPPOSITE, UPPER, side)
        ship_relayed(UPPER, side, 0)
    net.arrived(21, cots.at[OTHER, LOWER], p.opposite)
    attend(OTHER, 0, LOWER)
    attend(OTHER, 1, LOWER)
    for_sibling(TO_OPPOSITE, LOWER)
    project(OWN, 1)
    for side in range(2):
        to_ring(TO_OPPOSITE, LOWER, side)
        ship_relayed(LOWER, side, 0)
    attend(OWN, 1, UPPER)
    attend(OWN, 1, LOWER)

    for slot in (OWN, OTHER):
        low_mine[slot] = adapter_scale * dot(up[slot], grads[slot], ((1,), (1,)))
    net.send(14, low_mine, low_sib, p.sibling)
    up_terms_of(0)
    up_terms_of(1)
    net.arrived(14, low_sib, p.sibling)
    low_chip[...] = (low_mine[...] + low_sib[...]).astype(BF16)
    for n, device in enumerate((p.mate, p.cross, p.opposite)):
        net.send(16 + n, low_chip, low_in.at[n], device)
    my_up = up_terms.at[p.dp, p.y, p.z]
    net.send(15, my_up, my_up, p.opposite)
    for side in range(2):
        ship_relayed(LOWER, side, 1)
    for_sibling(TO_CROSS, UPPER)
    for_sibling(TO_MATE, UPPER)
    to_ring(TO_CROSS, UPPER, 0)
    ship(TO_CROSS, UPPER, 0)
    to_ring(TO_MATE, UPPER, 1)
    ship(TO_MATE, UPPER, 1)

    for n, device in enumerate((p.mate, p.cross, p.opposite)):
        net.arrived(16 + n, low_in.at[n], device)
    my_cols = pl.ds(pl.multiple_of(p.t * COLS, COLS), COLS)
    for slot in (OWN, OTHER):
        pair = low_chip[slot].astype(F32) + low_in[0, slot].astype(F32)
        far = low_in[1, 1 - slot].astype(F32) + low_in[2, 1 - slot].astype(F32)
        low_grad[slot] = (pair + far).astype(BF16)
        value = dot(low_grad[slot], xs[slot, :, my_cols], ((1,), (0,))).astype(BF16)
        my_down = down_terms.at[p.dp if slot == OWN else 1 - p.dp, p.y, p.z]
        my_down[:, 0:COLS] = value[:RANK]
        my_down[:, COLS:DOWN] = value[RANK:]
        tag = jnp.broadcast_to(meta[slot, 0:1, :], (RANK, 128))
        my_down[:, DOWN:TAGGED] = tag.astype(F32).astype(BF16)
    stage(down_gather, 1)
    net.arrived(15, up_terms.at[1 - p.dp, p.y, p.z], p.opposite)
    stage(up_gather, 1)
    for_sibling(TO_CROSS, LOWER)
    for_sibling(TO_MATE, LOWER)
    stage(down_gather, 2)
    to_ring(TO_CROSS, LOWER, 0)
    ship(TO_CROSS, LOWER, 0)
    to_ring(TO_MATE, LOWER, 1)
    ship(TO_MATE, LOWER, 1)
    stage(up_gather, 2)
    to_ring(TO_MATE, UPPER, 0, True)
    ship(TO_MATE, UPPER, 0)
    to_ring(TO_CROSS, UPPER, 1, True)
    ship(TO_CROSS, UPPER, 1)
    stage(down_gather, 3)
    to_ring(TO_MATE, LOWER, 0, True)
    ship(TO_MATE, LOWER, 0)
    to_ring(TO_CROSS, LOWER, 1, True)
    ship(TO_CROSS, LOWER, 1)
    for_sibling(TO_OWN, UPPER)
    for_sibling(TO_OWN, LOWER)
    stage(up_gather, 3)

    def keep(rows):
        for side in range(2):
            cols = piece(rows, side)
            columns = pl.ds(pl.multiple_of(p.t * COLS + cols.start, 128), cols.stop - cols.start)
            extra = dot(low_grad[OWN, :, rows], down[OWN, :, columns], ((0,), (0,)))
            kept[rows, cols] = both_cores(TO_OWN, rows, side) + extra

    keep(UPPER)
    stage(down_gather, 4)
    keep(LOWER)
    stage(up_gather, 4)
    stage(down_gather, 5)
    save = local(down_terms, down_out)

    rows = 16 * RANK
    at = lax.broadcasted_iota(jnp.int32, (rows, rows), 0)
    to = lax.broadcasted_iota(jnp.int32, (rows, rows), 1)
    for s in range(2):
        chosen = down_terms[s, :, :, :, DOWN:TAGGED].reshape(rows, 128)[:, 0:1].astype(F32)
        own = ((to // RANK).astype(F32) == chosen) & (at % RANK == to % RANK)
        owner_out[s] = own.astype(F32).T.astype(BF16)


    def finish_rows(rows):
        for side in range(2):
            cols = piece(rows, side)
            net.arrived(ring_index(TO_CROSS, rows, side), ring_in.at[0, rows, cols], p.cross)
            net.arrived(ring_index(TO_MATE, rows, side), ring_in.at[1, rows, cols], p.mate)
        grad_out[rows] = (
            kept[rows] + ring_in[0, rows].astype(F32) + ring_in[1, rows].astype(F32)
        ).astype(BF16)

    finish_rows(UPPER)
    stage(up_gather, 5)
    save_up = local(up_terms, up_out)
    finish_rows(LOWER)
    net.finish()
    save_up.wait()
    save.wait()


def block_call(lengths, ids, *arrays):
    hbm = pl.BlockSpec(memory_space=pl.ANY)
    vmem = pl.BlockSpec(memory_space=pltpu.VMEM)
    smem = pl.BlockSpec(memory_space=pltpu.SMEM)
    bf16 = lambda *shape: pltpu.VMEM(shape, BF16)
    f32 = lambda *shape: pltpu.VMEM(shape, F32)
    return pl.pallas_call(
        block_kernel,
        name="attention_block",
        out_shape=(
            jax.ShapeDtypeStruct((TOKENS, COLS), BF16),
            jax.ShapeDtypeStruct((2, 16 * RANK, 16 * RANK), BF16),
            jax.ShapeDtypeStruct((2, SIDE, SIDE, RANK, UP), BF16),
            jax.ShapeDtypeStruct((2, SIDE, SIDE, RANK, TAGGED), BF16),
        ),
        in_specs=[smem, smem] + [hbm] * 9,
        out_specs=(vmem, vmem, hbm, hbm),
        scratch_shapes=[
            bf16(2, TOKENS, D),
            bf16(SIDE, COLS, 2 * GROUP),
            bf16(ADAPTERS, RANK, D),
            bf16(ADAPTERS, RANK, D),
            bf16(ADAPTERS, RANK, 512),
            bf16(ADAPTERS, RANK, 256),
            bf16(2, 2 * RANK, D),
            bf16(2, 2 * RANK, 2 * GROUP),
            bf16(2, TOKENS, 2 * RANK),
            bf16(2, TOKENS, 2 * GROUP),
            bf16(2, TOKENS, 2 * GROUP),
            bf16(2, TOKENS, 512),
            pltpu.VMEM((2, 8, 128), jnp.int32),
            f32(2, HALF, HD),
            f32(2, HALF, HD),
            bf16(4, TOKENS, COLS),
            bf16(4, TOKENS, COLS),
            bf16(3, TOKENS, COLS),
            bf16(TOKENS, COLS),
            bf16(2, TOKENS, COLS),
            f32(TOKENS, COLS),
            f32(2, 2 * RANK, TOKENS),
            f32(2, 2 * RANK, TOKENS),
            bf16(2, 2 * RANK, TOKENS),
            bf16(3, 2, 2 * RANK, TOKENS),
            bf16(2, 2 * RANK, TOKENS),
            bf16(2, SIDE, SIDE, RANK, UP),
            bf16(2, SIDE, SIDE, RANK, TAGGED),
            f32(TOKENS, 2 * RANK),
            f32(TOKENS, GROUP),
            pltpu.SemaphoreType.DMA((178,)),
            pltpu.SemaphoreType.DMA((178,)),
            pltpu.SemaphoreType.DMA((16,)),
        ],
        compiler_params=pltpu.CompilerParams(
            collective_id=0, has_side_effects=True, vmem_limit_bytes=VMEM_BYTES
        ),
    )(lengths, ids, *arrays)


def table_kernel(
    grad_ref, owner_ref, up_ref, down_ref,
    grad_out, qa_out, qb_out, va_out, vb_out,
    grad, owners, up, down, qa, qb, va, vb, in_sems, out_sems,
):
    width = 384
    rows = 16 * RANK
    pairs = [(owner_ref.at[s], owners.at[:, s * rows : (s + 1) * rows]) for s in range(2)]
    pairs.append((up_ref, up))
    for n in range(2 * COLS // width):
        cols = slice(n * width, (n + 1) * width)
        pairs.append((down_ref.at[:, :, cols], down.at[:, :, cols]))
    pairs.append((grad_ref, grad))
    loads = [
        pltpu.make_async_copy(src, dst, in_sems.at[n]) for n, (src, dst) in enumerate(pairs)
    ]
    for load in loads:
        load.start()
    stores = []

    def store(src, dst):
        copy = pltpu.make_async_copy(src, dst, out_sems.at[len(stores)])
        copy.start()
        stores.append(copy)

    def total(first, second):
        one = dot(owners[:, :rows], first, ((1,), (0,)))
        return one + dot(owners[:, rows:], second, ((1,), (0,)))

    for load in loads[:3]:
        load.wait()
    for out, to_ref, start, size in ((qb, qb_out, 0, 256), (vb, vb_out, 512, 128)):
        for d in range(2):
            for g in range(2):
                at, first = (2 * d + g) * size, g * HEAD + start
                out[:, at : at + size] = total(
                    up[d, :, first : first + size], up[d, :, first + size : first + 2 * size]
                )
        store(out, to_ref)
    for n in range(2 * COLS // width):
        loads[3 + n].wait()
        out, to_ref, c = (qa, qa_out, 0) if n < COLS // width else (va, va_out, COLS)
        cols = slice(n * width, (n + 1) * width)
        here = slice(n * width - c, (n + 1) * width - c)
        terms = down[:, :, cols].reshape(2 * rows, width)
        out[:, here] = dot(owners[...], terms, ((1,), (0,)))
        store(out.at[:, here], to_ref.at[:, here])
    loads[-1].wait()
    store(grad, grad_out)
    for copy in stores:
        copy.wait()


def table_call(grad, owners, *terms):
    hbm = pl.BlockSpec(memory_space=pl.ANY)
    rows = 16 * RANK
    widths = (COLS, 1024, COLS, 512)
    return pl.pallas_call(
        table_kernel,
        name="tables",
        out_shape=(jax.ShapeDtypeStruct((TOKENS, COLS), BF16),)
        + tuple(jax.ShapeDtypeStruct((rows, width), F32) for width in widths),
        in_specs=[hbm] * 4,
        out_specs=(hbm,) * 5,
        scratch_shapes=[
            pltpu.VMEM((TOKENS, COLS), BF16),
            pltpu.VMEM((rows, 2 * rows), BF16),
            pltpu.VMEM((2, rows, UP), BF16),
            pltpu.VMEM((2, rows, DOWN), BF16),
        ]
        + [pltpu.VMEM((rows, width), F32) for width in widths]
        + [pltpu.SemaphoreType.DMA((10,)), pltpu.SemaphoreType.DMA((9,))],
        compiler_params=pltpu.CompilerParams(vmem_limit_bytes=VMEM_BYTES),
    )(grad, owners, *(block.reshape(2, rows, -1) for block in terms))


def shards(
    x_in, lengths, adapter_ids, attn_grad, w_query, w_key, w_value,
    query_down, query_up, value_down, value_up,
):
    grad, owners, *terms = block_call(
        lengths, adapter_ids, x_in[0], attn_grad[0], w_query, w_key, w_value,
        query_down, value_down, query_up, value_up,
    )
    grad, qa, qb, va, vb = table_call(grad, owners, *terms)
    tables = (table.reshape(ADAPTERS, RANK, -1) for table in (qa, qb, va, vb))
    return (grad[None], *tables)


def solution(mesh):
    placed = (
        P(("dp", "fsdp"), None, "tensor"),
        P(("dp", "fsdp")),
        P(("dp", "fsdp")),
        P(("dp", "fsdp"), None, "tensor"),
        P("fsdp", "tensor"),
        P("fsdp", "tensor"),
        P("fsdp", "tensor"),
        P(),
        P(None, None, "tensor"),
        P(),
        P(None, None, "tensor"),
    )
    return jax.shard_map(
        shards,
        mesh=mesh,
        in_specs=placed,
        out_specs=(
            P(("dp", "fsdp"), None, "tensor"),
            P(None, None, "tensor"),
            P(None, None, "tensor"),
            P(None, None, "tensor"),
            P(None, None, "tensor"),
        ),
        check_vma=False,
    )
```
